32 devices in a mesh: dp: 16 (over z, x, core), tensor: 2 (over y).
Axes of the slice: x: 2, y: 2, z: 4, core: 2. Of those that a mesh axis runs over, the one named last changes fastest.
Arguments:
- inputs: bfloat16 [2048, 4096], P('dp'), may hold values from -6 to 6
- w_key: bfloat16 [4096, 1024], P(None, 'tensor'), may hold values from -0.09375 to 0.09375
- values: bfloat16 [2048, 1024], P('dp', 'tensor'), may hold values from -6 to 6
- queries: bfloat16 [2048, 4096], P('dp', 'tensor'), may hold values from -200 to 200
- d_out: bfloat16 [2048, 4096], P('dp', 'tensor'), may hold values from -6 to 6
- doc_lens: int32 [4], replicated, may hold values from 1 to 1024, 2048 in all
- block_pos: int32 [32], P('dp'), may hold values from 0 to 31, as said below
Outputs:
- d_query: bfloat16 [2048, 4096], P('dp', 'tensor')
- d_value: bfloat16 [2048, 1024], P('dp', 'tensor')
- d_input: bfloat16 [2048, 4096], P('dp', 'tensor')
- d_wkey: float32 [4096, 1024], P('dp', 'tensor')
The draws below stay inside these ranges and needn't reach their ends.
Inputs may be any that keep to these rules, and one draw needn't show every extreme that they name: `block_pos`: each stored block holds one block of 64 rows of the pack; every pack block is held once. `doc_lens`: lengths of the 4 documents in pack order; they sum to 2048.
All inputs are finite; a program needn't handle non-finite values.
Results may differ from the reference program's by a relative error of at most 0.023.
The reference program's roundings to bfloat16 on the way (of `key_rows` and `key_grad`) count: a program that leaves them out, or rounds other values in their place, can miss the bound.
Values may be sent and summed in bfloat16 or wider, within the bound.
No kernel may reach another device: no remote copies, remote signals or barrier semaphores. Data moves between devices by JAX's collectives and lax.ppermute only.
A program may use at most 64 MiB of HBM per device.

```python
import math
import jax
import jax.numpy as jnp
import numpy as np
from jax import lax

D = 4096
HEADS = 32
KVH = 8
HD = 128
BLK = 64
NDOC = 4
TOKENS = 2048
BPD = 2
NB = 32


def draw_queries(key, part):
    key = jax.random.fold_in(key, 7)
    noise_key = jax.random.fold_in(key, 0)
    base = jnp.clip(jax.random.normal(noise_key, (TOKENS, HEADS * HD), jnp.float32), -6.0, 6.0)
    return base.astype(jnp.bfloat16)


def draw_block_pos(key, part):
    key = jax.random.fold_in(key, 11)
    pair_order = jax.random.permutation(key, NB // 2).astype(jnp.int32)
    pairs = pair_order.reshape(NB // BPD, BPD // 2)
    mirrored = NB - 1 - pairs
    return jnp.concatenate([pairs, mirrored], axis=1).reshape(NB).astype(jnp.int32)


def steps_of(own_key, extent, cuts, low, largest):
    gain = 1.0
    for dim, parts in cuts:
        draws = jax.random.uniform(jax.random.fold_in(jax.random.fold_in(own_key, 6), dim), (parts,), jnp.float32, low / len(cuts), largest / len(cuts))
        gain = gain * jnp.repeat(jnp.exp(draws), extent[dim] // parts).reshape((-1,) + (1,) * (len(extent) - 1 - dim))
    return gain


def length_profile(amount, total, bound, lean):
    weights = [(1 << 20) // math.isqrt(standing ** lean) + 1 for standing in range(2, amount + 1)]
    rest, counts = total - bound - (amount - 1), [1] * (amount - 1)
    while rest > 0:
        free = [i for i in range(amount - 1) if counts[i] < bound]
        mass, budget = sum([weights[i] for i in free]), rest
        for i in free:
            extra = min(bound - counts[i], max(1, budget * weights[i] // mass), rest)
            counts[i] = counts[i] + extra
            rest = rest - extra
    return np.array([bound] + counts)


def ragged(key, count, total, most, skew):
    if count == 2:
        one = jax.random.randint(key, (), max(1, total - most), min(most, total - 1) + 1)
        return jnp.stack([one, total - one])
    tallies = jnp.asarray(length_profile(count, total, most, skew), jnp.int32)
    twos = (count - 1) // 2
    donor, receiver = tallies[1:1 + 2 * twos:2], tallies[2:2 + 2 * twos:2]
    margin = jnp.minimum(donor - 1, most - receiver)
    moved = jax.random.randint(jax.random.fold_in(key, 1), (twos,), 0, 1 << 20) % (margin + 1)
    tallies = tallies.at[1:1 + 2 * twos:2].set(donor - moved).at[2:2 + 2 * twos:2].set(receiver + moved)
    return tallies[jax.random.permutation(jax.random.fold_in(key, 2), count)]


def bell_draw(own_key, extent, spread, bound, shards=(), held_as=jnp.bfloat16):
    array = jax.random.normal(own_key, extent, jnp.float32) * spread
    if len(shards) > 0:
        array = steps_of(own_key, extent, shards, -0.22, 0.18) * array
    return jnp.clip(array, min=-bound, max=bound).astype(held_as)


def setup_inputs(seed: int = 0) -> dict:
    seeds = jax.random.split(jax.random.key(seed), 8)
    return {
        "inputs": bell_draw(seeds[0], (TOKENS, D), 1.0, 6.0, ((0, 16),)),
        "w_key": bell_draw(seeds[1], (D, KVH * HD), D ** -0.5, 0.09375, ((1, 2),)),
        "values": bell_draw(seeds[2], (TOKENS, KVH * HD), 1.0, 6.0, ((0, 16), (1, 2))),
        "queries": draw_queries(jax.random.fold_in(seeds[7], 71), 0),
        "d_out": bell_draw(seeds[4], (TOKENS, HEADS * HD), 1.0, 6.0, ((0, 16), (1, 2))),
        "doc_lens": ragged(seeds[5], NDOC, TOKENS, TOKENS // 2, 2).astype(jnp.int32),
        "block_pos": draw_block_pos(jax.random.fold_in(seeds[7], 71), 0),
    }


def row_positions(block_pos):
    within = jnp.tile(jnp.arange(BLK, dtype=jnp.int32), block_pos.shape[0])
    return jnp.repeat(block_pos, BLK) * BLK + within

def documents(positions, doc_lens):
    starts = jnp.cumsum(doc_lens) - doc_lens
    return lax.optimization_barrier(jnp.sum((positions[:, None] >= starts[None, :]).astype(jnp.int32), axis=1)) - 1

def reference(inputs, w_key, values, queries, d_out, doc_lens, block_pos):
    score_scale = 1.0 / math.sqrt(HD)
    group_size = HEADS // KVH
    positions = row_positions(block_pos)
    doc_ids = documents(positions, doc_lens)
    key_rows = jnp.dot(inputs, w_key, preferred_element_type=jnp.float32).astype(jnp.bfloat16)
    query_block = math.gcd(512, TOKENS)
    block_count = TOKENS // query_block
    query_split = queries.reshape(block_count, query_block, KVH, group_size, HD)
    grad_split = d_out.reshape(block_count, query_block, KVH, group_size, HD)
    pos_split = positions.reshape(block_count, query_block)
    doc_split = doc_ids.reshape(block_count, query_block)
    key_all = key_rows.reshape(TOKENS, KVH, HD).astype(jnp.float32)
    value_all = values.reshape(TOKENS, KVH, HD).astype(jnp.float32)
    key_parts = []
    value_parts = []
    query_parts = []
    for head_index in range(KVH):
        key_head = key_all[:, head_index]
        value_head = value_all[:, head_index]

        def one_block(running, items):
            key_sum, value_sum = running
            query_here, grad_here, pos_here, doc_here = items
            query_float = query_here.astype(jnp.float32)
            grad_float = grad_here.astype(jnp.float32)
            scores = jnp.einsum('qgd,kd->gqk', query_float, key_head) * score_scale
            allowed = (doc_here[:, None] == doc_ids[None, :]) & (positions[None, :] <= pos_here[:, None])
            allowed = allowed[None]
            masked = jnp.where(allowed, scores, -1e+30)
            row_max = lax.optimization_barrier(jnp.max(masked, axis=2, keepdims=True))
            exp_terms = jnp.where(allowed, jnp.exp(scores - row_max), 0.0)
            probabilities = exp_terms / lax.optimization_barrier(jnp.sum(exp_terms, axis=2, keepdims=True))
            d_prob = jnp.einsum('qgd,kd->gqk', grad_float, value_head)
            delta = lax.optimization_barrier(jnp.sum(probabilities * d_prob, axis=2, keepdims=True))
            d_score = probabilities * (d_prob - delta)
            prob_bf = lax.optimization_barrier(probabilities.astype(jnp.bfloat16)).astype(jnp.float32)
            score_bf = lax.optimization_barrier(d_score.astype(jnp.bfloat16)).astype(jnp.float32)
            query_grad = (score_scale * jnp.einsum('gqk,kd->qgd', score_bf, key_head)).astype(jnp.bfloat16)
            key_sum = key_sum + score_scale * jnp.einsum('gqk,qgd->kd', score_bf, query_float)
            value_sum = value_sum + jnp.einsum('gqk,qgd->kd', prob_bf, grad_float)
            return ((key_sum, value_sum), query_grad)
        empty_sum = jnp.zeros((TOKENS, HD), jnp.float32)
        (key_sum, value_sum), query_grad = lax.scan(one_block, (empty_sum, empty_sum), (query_split[:, :, head_index], grad_split[:, :, head_index], pos_split, doc_split))
        key_parts.append(key_sum)
        value_parts.append(value_sum)
        query_parts.append(query_grad.reshape(TOKENS, group_size, HD))
    key_grad = jnp.stack(key_parts, axis=1).reshape(TOKENS, KVH * HD).astype(jnp.bfloat16)
    d_value = jnp.stack(value_parts, axis=1).reshape(TOKENS, KVH * HD).astype(jnp.bfloat16)
    d_query = jnp.stack(query_parts, axis=1).reshape(TOKENS, HEADS * HD)
    d_wkey = jnp.dot(inputs.T, key_grad, preferred_element_type=jnp.float32)
    d_input = jnp.dot(key_grad, w_key.T, preferred_element_type=jnp.float32).astype(jnp.bfloat16)
    return (d_query, d_value, d_input, d_wkey)
```

```python
import math

import jax
import jax.numpy as jnp
from jax import lax
from jax.experimental import pallas as pl
from jax.experimental.pallas import tpu as pltpu
from jax.sharding import PartitionSpec as P

HD = 128
BLK = 64


masked_fill = -1e30


def row_positions(block_pos):
    within = jnp.tile(jnp.arange(BLK, dtype=jnp.int32), block_pos.shape[0])
    return jnp.repeat(block_pos, BLK) * BLK + within


def documents(positions, doc_lens):
    starts = jnp.cumsum(doc_lens) - doc_lens
    return jnp.sum((positions[:, None] >= starts[None, :]).astype(jnp.int32), axis=1) - 1


def split_heads(block_rows, kv_heads):
    return block_rows.reshape(block_rows.shape[0], kv_heads, HD)


def scored(query_heads, key_block, score_scale):
    key_split = split_heads(key_block, query_heads.shape[1])
    return (
        jnp.einsum("qcgd,kcd->cgqk", query_heads, key_split, preferred_element_type=jnp.float32)
        * score_scale
    )


def contributions(
    query_heads, grad_heads, key_block, value_block, allowed, row_max, row_sum, delta, score_scale
):
    kv_heads = query_heads.shape[1]
    key_split = split_heads(key_block, kv_heads)
    value_split = split_heads(value_block, kv_heads)
    scores = scored(query_heads, key_block, score_scale)
    mask_full = allowed[None, None]
    probabilities = (
        jnp.where(mask_full, jnp.exp(scores - row_max[..., None]), 0.0) / row_sum[..., None]
    )
    d_prob = jnp.einsum(
        "qcgd,kcd->cgqk", grad_heads, value_split, preferred_element_type=jnp.float32
    )
    d_score = probabilities * (d_prob - delta[..., None])
    prob_bf = probabilities.astype(jnp.bfloat16)
    score_bf = d_score.astype(jnp.bfloat16)
    query_part = score_scale * jnp.einsum(
        "cgqk,kcd->qcgd", score_bf, key_split, preferred_element_type=jnp.float32
    )
    key_part = score_scale * jnp.einsum(
        "cgqk,qcgd->kcd", score_bf, query_heads, preferred_element_type=jnp.float32
    )
    value_part = jnp.einsum(
        "cgqk,qcgd->kcd", prob_bf, grad_heads, preferred_element_type=jnp.float32
    )
    width_rows = key_block.shape[0]
    partial_value = jnp.concatenate(
        [key_part.reshape(width_rows, -1), value_part.reshape(width_rows, -1)], axis=1
    )
    return (query_part, partial_value)


def on_device(inputs, w_key, values, queries, d_out, doc_lens, block_pos):
    local_rows = inputs.shape[0]
    kv_heads = values.shape[1] // HD
    group_size = queries.shape[1] // (kv_heads * HD)
    kv_columns = kv_heads * HD
    score_scale = 1.0 / math.sqrt(HD)
    key_rows = jnp.dot(inputs, w_key, preferred_element_type=jnp.float32).astype(jnp.bfloat16)
    all_keys, all_values, all_blocks = (
        lax.all_gather(key_rows, "dp", axis=0, tiled=True),
        lax.all_gather(values, "dp", axis=0, tiled=True),
        lax.all_gather(block_pos, "dp", axis=0, tiled=True),
    )
    key_pos = row_positions(all_blocks)
    key_doc = documents(key_pos, doc_lens)
    query_pos = row_positions(block_pos)
    query_doc = documents(query_pos, doc_lens)
    query_heads = queries.reshape(local_rows, kv_heads, group_size, HD)
    grad_heads = d_out.reshape(local_rows, kv_heads, group_size, HD)
    total_rows = all_keys.shape[0]
    key_width = math.gcd(512, total_rows)
    stat_shape = (kv_heads, group_size, local_rows)

    def mask_for(first_row, width_rows):
        pos_here = lax.dynamic_slice_in_dim(key_pos, first_row, width_rows, 0)
        doc_here = lax.dynamic_slice_in_dim(key_doc, first_row, width_rows, 0)
        return (query_doc[:, None] == doc_here[None, :]) & (pos_here[None, :] <= query_pos[:, None])

    def visit_stats(block_index, running):
        first_row = block_index * key_width
        key_block = lax.dynamic_slice_in_dim(all_keys, first_row, key_width, 0)
        value_block = lax.dynamic_slice_in_dim(all_values, first_row, key_width, 0)
        allowed = mask_for(first_row, key_width)

        def visit_compute_live(state_now):
            row_max, row_sum, weighted = state_now
            scores = scored(query_heads, key_block, score_scale)
            mask_full = allowed[None, None]
            new_max = jnp.maximum(
                row_max, jnp.max(jnp.where(mask_full, scores, masked_fill), axis=3)
            )
            exp_terms = jnp.where(mask_full, jnp.exp(scores - new_max[..., None]), 0.0)
            d_prob = jnp.einsum(
                "qcgd,kcd->cgqk",
                grad_heads,
                split_heads(value_block, kv_heads),
                preferred_element_type=jnp.float32,
            )
            shrink = jnp.exp(row_max - new_max)
            return (
                new_max,
                row_sum * shrink + jnp.sum(exp_terms, axis=3),
                weighted * shrink + jnp.sum(exp_terms * d_prob, axis=3),
            )

        return lax.cond(jnp.any(allowed), visit_compute_live, lambda state_now: state_now, running)

    start_state = (
        jnp.full(stat_shape, masked_fill, jnp.float32),
        jnp.zeros(stat_shape, jnp.float32),
        jnp.zeros(stat_shape, jnp.float32),
    )
    row_max, row_sum, weighted = lax.fori_loop(0, total_rows // key_width, visit_stats, start_state)
    delta = weighted / row_sum

    def block_work(key_block, value_block, allowed):
        width_rows = key_block.shape[0]

        def block_compute_live(operands):
            return contributions(
                query_heads,
                grad_heads,
                operands[0],
                operands[1],
                operands[2],
                row_max,
                row_sum,
                delta,
                score_scale,
            )

        def dead_block(operands):
            return (
                jnp.zeros((local_rows, kv_heads, group_size, HD), jnp.float32),
                jnp.zeros((width_rows, 2 * kv_columns), jnp.float32),
            )

        return lax.cond(
            jnp.any(allowed), block_compute_live, dead_block, (key_block, value_block, allowed)
        )

    query_start = jnp.zeros((local_rows, kv_heads, group_size, HD), jnp.float32)

    def visit_block(block_index, running):
        query_sum, buffer_rows = running
        first_row = block_index * key_width
        key_block = lax.dynamic_slice_in_dim(all_keys, first_row, key_width, 0)
        value_block = lax.dynamic_slice_in_dim(all_values, first_row, key_width, 0)
        query_part, partial_value = block_work(
            key_block, value_block, mask_for(first_row, key_width)
        )
        return (
            query_sum + query_part,
            lax.dynamic_update_slice_in_dim(buffer_rows, partial_value, first_row, 0),
        )

    empty_buffer = jnp.zeros((total_rows, 2 * kv_columns), jnp.float32)
    query_sum, buffer_rows = lax.fori_loop(
        0, total_rows // key_width, visit_block, (query_start, empty_buffer)
    )
    arrived = lax.all_to_all(
        buffer_rows.astype(jnp.bfloat16), "dp", split_axis=0, concat_axis=0, tiled=True
    ).astype(buffer_rows.dtype)
    own_sums = jnp.sum(arrived.reshape(-1, local_rows, 2 * kv_columns), axis=0)
    d_query = query_sum.astype(jnp.bfloat16).reshape(local_rows, kv_columns * group_size)
    key_grad = own_sums[:, :kv_columns].astype(jnp.bfloat16)
    d_value = own_sums[:, kv_columns:].astype(jnp.bfloat16)
    d_wkey = lax.psum_scatter(
        lax.dot_general(
            inputs, key_grad, (((0,), (0,)), ((), ())), preferred_element_type=jnp.float32
        ),
        "dp",
        scatter_dimension=0,
        tiled=True,
    )
    partial_input = lax.dot_general(
        key_grad, w_key, (((1,), (1,)), ((), ())), preferred_element_type=jnp.float32
    )
    d_input = lax.psum_scatter(
        partial_input.astype(jnp.bfloat16), "tensor", scatter_dimension=1, tiled=True
    )
    return (d_query, d_value, d_input, d_wkey)


CORE, Z_HI = 1, 8
GROUP = 4
ROWS = 128
TILE = 256
Q_BLOCKS = GROUP * ROWS // BLK
SMEM = pltpu.SMEM
VMEM = pltpu.VMEM


def swap(array, mask):
    return lax.ppermute(array, "dp", [(i, i ^ mask) for i in range(16)])


def swap_tensor(array):
    return lax.ppermute(array, "tensor", [(0, 1), (1, 0)])


def own_head():
    return (lax.axis_index("dp") >> 1) & 3


def columns(index, width):
    return pl.ds(pl.multiple_of(index * width, width), width)


def whole_spec(space=VMEM):
    return pl.BlockSpec(memory_space=space)


def pack_rows(queries_ref, grads_ref, *out_refs):
    head = own_head()
    for m, out_ref in enumerate(out_refs):
        span = columns(head ^ m, GROUP * HD)
        out_ref[:, : GROUP * HD] = queries_ref[:, span]
        out_ref[:, GROUP * HD :] = grads_ref[:, span]


def project_keys(inputs_ref, values_ref, w_ref, *refs):
    pair_refs, feature_refs, total = refs[:GROUP], refs[GROUP : 2 * GROUP], refs[-1]
    step = pl.program_id(0)
    head = own_head()

    @pl.when(step == 0)
    def _():
        total[...] = jnp.zeros_like(total)
        chip = lax.axis_index("dp") >> 1
        side = lax.axis_index("tensor")
        for m in range(GROUP):
            pair_refs[m][:, HD:] = values_ref[:, columns(head ^ m, HD)]
            for far in range(2):
                target = chip ^ (m + GROUP * far)
                feature_refs[m][far] = inputs_ref[:, columns(2 * target + side, 256)]

    total[...] += jnp.dot(
        inputs_ref[:, columns(step, 512)], w_ref[...], preferred_element_type=jnp.float32
    )

    @pl.when(step == pl.num_programs(0) - 1)
    def _():
        for m in range(GROUP):
            pair_refs[m][:, :HD] = total[:, columns(head ^ m, HD)].astype(jnp.bfloat16)


def dot_nt(left, right):
    return lax.dot_general(
        left, right, (((1,), (1,)), ((), ())), preferred_element_type=jnp.float32
    )


def folded(array, reduce):
    return reduce(array.reshape(-1, 8, array.shape[-1]), axis=0)


def attend(pos_ref, lens_ref, *refs):
    row_refs, pair_refs, refs = refs[:GROUP], refs[GROUP : 2 * GROUP], refs[2 * GROUP :]
    dq_ref, dk_keep, dk_send, dv_keep, dv_send = refs[:5]
    q_rows, g_rows, keys, keys_t, values, dk, dv, scores, d_prob = refs[5:]
    score_scale = 1.0 / math.sqrt(HD)
    base_two = score_scale * math.log2(math.e)

    for block in range(Q_BLOCKS):
        here = pl.ds(block % 2 * BLK, BLK)
        for h in range(GROUP):
            there = pl.ds(h * BLK, BLK)
            q_rows[block, there] = row_refs[block // 2][here, h * HD : (h + 1) * HD]
            g_rows[block, there] = row_refs[block // 2][
                here, (GROUP + h) * HD : (GROUP + h + 1) * HD
            ]
    for block in range(4 * Q_BLOCKS):
        here = pl.ds(block % Q_BLOCKS * BLK, BLK)
        there = pl.ds(pl.multiple_of(pos_ref[block] * BLK, BLK), BLK)
        keys[there] = pair_refs[block // Q_BLOCKS][here, :HD]
        values[there] = pair_refs[block // Q_BLOCKS][here, HD:]
    for tile in range(keys.shape[0] // TILE):
        here = pl.ds(tile * TILE, TILE)
        keys_t[:, here] = keys[here].astype(jnp.float32).T.astype(jnp.bfloat16)
    dk[...] = jnp.zeros_like(dk)
    dv[...] = jnp.zeros_like(dv)
    starts = [lens_ref[0]]
    for k in (1, 2):
        starts.append(starts[-1] + lens_ref[k])

    def document_start(position):
        found = jnp.zeros_like(position)
        for start in starts:
            found = jnp.where(start <= position, start, found)
        return found

    @pl.loop(0, Q_BLOCKS)
    def _(block):
        first = pos_ref[block] * BLK
        lanes = lax.broadcasted_iota(jnp.int32, (1, GROUP * BLK), 1)
        position = first + (lanes & (BLK - 1))
        start = document_start(position)
        low = document_start(first) // TILE
        high = (first + BLK - 1) // TILE + 1
        query = q_rows[block]
        grad = g_rows[block]
        folded_shape = (8, GROUP * BLK)

        def visit_scores(tile, row_max):
            here = columns(tile, TILE)
            raw = dot_nt(keys[here], query)
            key_position = tile * TILE + lax.broadcasted_iota(jnp.int32, raw.shape, 0)
            allowed = (key_position <= position) & (key_position >= start)
            raw = jnp.where(allowed, raw, masked_fill)
            scores[here] = raw
            d_prob[here] = dot_nt(values[here], grad)
            return jnp.maximum(row_max, folded(raw, jnp.max))

        row_max = lax.fori_loop(
            low, high, visit_scores, jnp.full(folded_shape, masked_fill, jnp.float32)
        )
        row_max = jnp.max(row_max, axis=0, keepdims=True)

        def visit_sums(tile, running):
            here = columns(tile, TILE)
            terms = jnp.exp2((scores[here] - row_max) * base_two)
            scores[here] = terms
            return (
                running[0] + folded(terms, jnp.sum),
                running[1] + folded(terms * d_prob[here], jnp.sum),
            )

        zeros = jnp.zeros(folded_shape, jnp.float32)
        row_sum, weighted = lax.fori_loop(low, high, visit_sums, (zeros, zeros))
        inverse = 1.0 / jnp.sum(row_sum, axis=0, keepdims=True)
        delta = jnp.sum(weighted, axis=0, keepdims=True) * inverse

        def visit_grads(tile, dq):
            here = columns(tile, TILE)
            prob = scores[here] * inverse
            score_bf = (prob * (d_prob[here] - delta)).astype(jnp.bfloat16)
            dk[here] += jnp.dot(score_bf, query, preferred_element_type=jnp.float32)
            dv[here] += jnp.dot(
                prob.astype(jnp.bfloat16), grad, preferred_element_type=jnp.float32
            )
            return dq + jnp.dot(keys_t[:, here], score_bf, preferred_element_type=jnp.float32)

        dq = lax.fori_loop(
            low, high, visit_grads, jnp.zeros((HD, GROUP * BLK), jnp.float32)
        )
        dq = (dq * score_scale).T.astype(jnp.bfloat16)
        for h in range(GROUP):
            dq_ref[block, :, h * HD : (h + 1) * HD] = dq[h * BLK : (h + 1) * BLK]

    for block in range(4 * Q_BLOCKS):
        quarter = block // Q_BLOCKS
        here = pl.ds(quarter // 2 * Q_BLOCKS * BLK + block % Q_BLOCKS * BLK, BLK)
        there = pl.ds(pl.multiple_of(pos_ref[block] * BLK, BLK), BLK)
        (dk_send if quarter % 2 else dk_keep)[here] = dk[there] * score_scale
        (dv_send if quarter % 2 else dv_keep)[here] = dv[there]


def weight_grad(own_ref, other_ref, *refs):
    grad_refs, out_ref, grads = refs[:GROUP], refs[GROUP], refs[GROUP + 1]
    head = own_head()
    for k, grad_ref in enumerate(grad_refs):
        for far in range(2):
            for m in range(GROUP):
                here = pl.ds((far * GROUP + m) * ROWS, ROWS)
                there = pl.ds((far * GROUP + (m ^ k)) * ROWS, ROWS)
                grads[here, columns(head ^ k, HD)] = grad_ref[there]
    slot = (lax.axis_index("dp") & 1) ^ lax.axis_index("tensor")
    out_ref[slot] = jnp.dot(own_ref[...], grads[...], preferred_element_type=jnp.float32)
    out_ref[1 - slot] = jnp.dot(other_ref[...], grads[...], preferred_element_type=jnp.float32)


def input_grad(ids_ref, own_ref, other_ref, w_own, w_near, w_far, out_ref, own_all, other_all):
    step = pl.program_id(0)
    head = ids_ref[0]

    @pl.when(step == 0)
    def _():
        for k in range(GROUP):
            own_all[:, columns(head ^ k, HD)] = own_ref[k]
            other_all[:, columns(head ^ k, HD)] = other_ref[k]

    part = dot_nt(own_all[...], w_own[...])

    @pl.when(step < 2)
    def _():
        out_ref[...] = (part + dot_nt(other_all[...], w_near[...])).astype(jnp.bfloat16)

    @pl.when(step >= 2)
    def _():
        out_ref[...] = (part + dot_nt(other_all[...], w_far[...])).astype(jnp.bfloat16)


def place_rows(*refs):
    dq_refs, dv_refs = refs[:GROUP], refs[GROUP : 2 * GROUP]
    dq_out, dv_out = refs[2 * GROUP :]
    head = own_head()
    for m in range(GROUP):
        dq_out[:, columns(head ^ m, GROUP * HD)] = dq_refs[m][...]
        dv_out[:, columns(head ^ m, HD)] = dv_refs[m][...]


def shaped(shape, dtype=jnp.bfloat16):
    return jax.ShapeDtypeStruct(shape, dtype)


def limits(mebibytes):
    return pltpu.CompilerParams(vmem_limit_bytes=mebibytes << 20)


def on_device_by_heads(inputs, w_key, values, queries, d_out, doc_lens, block_pos):
    features = inputs.shape[1]
    kv_columns = values.shape[1]
    total_rows = 16 * ROWS
    index = lax.axis_index("dp")
    side = lax.axis_index("tensor")
    core = index & 1
    vmem, smem = whole_spec(), whole_spec(SMEM)

    packed_rows = pl.pallas_call(
        pack_rows,
        out_shape=[shaped((ROWS, 2 * GROUP * HD))] * GROUP,
        in_specs=[vmem] * 2,
        out_specs=[vmem] * GROUP,
        compiler_params=limits(16),
        name="pack_rows",
    )(queries, d_out)
    rows = [packed_rows[0]] + [swap(packed_rows[m], 2 * m) for m in (1, 2, 3)]

    steps = features // 512
    projected = pl.pallas_call(
        project_keys,
        out_shape=[shaped((ROWS, 2 * HD))] * GROUP + [shaped((2, ROWS, 256))] * GROUP,
        grid=(steps,),
        in_specs=[
            pl.BlockSpec((ROWS, features), lambda k: (0, 0)),
            pl.BlockSpec((ROWS, kv_columns), lambda k: (0, 0)),
            pl.BlockSpec((512, kv_columns), lambda k: (k, 0)),
        ],
        out_specs=[pl.BlockSpec((ROWS, 2 * HD), lambda k: (0, 0))] * GROUP
        + [pl.BlockSpec((2, ROWS, 256), lambda k: (0, 0, 0))] * GROUP,
        scratch_shapes=[VMEM((ROWS, kv_columns), jnp.float32)],
        compiler_params=limits(24),
        cost_estimate=pl.CostEstimate(
            flops=2 * ROWS * features * kv_columns,
            bytes_accessed=features * kv_columns * 2,
            transcendentals=0,
        ),
        name="project_keys",
    )(inputs, values, w_key)
    pairs, feature_parts = projected[:GROUP], projected[GROUP:]

    own_pairs = jnp.concatenate([pairs[0]] + [swap(pairs[m], 2 * m) for m in (1, 2, 3)], axis=0)
    far_pairs = swap(own_pairs, Z_HI)
    core_pairs = swap(own_pairs, CORE)
    far_core_pairs = swap(far_pairs, CORE)

    own_pos = jnp.concatenate([block_pos] + [swap(block_pos, 2 * m) for m in (1, 2, 3)])
    far_pos = swap(own_pos, Z_HI)
    positions = jnp.concatenate([own_pos, swap(own_pos, CORE), far_pos, swap(far_pos, CORE)])

    half = total_rows // 2
    d_rows, dk_keep, dk_send, dv_keep, dv_send = pl.pallas_call(
        attend,
        out_shape=[shaped((Q_BLOCKS, BLK, GROUP * HD))] + [shaped((half, HD), jnp.float32)] * 4,
        in_specs=[smem] * 2 + [vmem] * (2 * GROUP),
        out_specs=[vmem] * 5,
        scratch_shapes=[
            VMEM((Q_BLOCKS, GROUP * BLK, HD), jnp.bfloat16),
            VMEM((Q_BLOCKS, GROUP * BLK, HD), jnp.bfloat16),
            VMEM((total_rows, HD), jnp.bfloat16),
            VMEM((HD, total_rows), jnp.bfloat16),
            VMEM((total_rows, HD), jnp.bfloat16),
            VMEM((total_rows, HD), jnp.float32),
            VMEM((total_rows, HD), jnp.float32),
            VMEM((total_rows, GROUP * BLK), jnp.float32),
            VMEM((total_rows, GROUP * BLK), jnp.float32),
        ],
        compiler_params=limits(40),
        cost_estimate=pl.CostEstimate(
            flops=4 * 10 * 512 * 512 * HD,
            bytes_accessed=6 << 20,
            transcendentals=512 * 2048,
        ),
        name="attend",
    )(positions, doc_lens, *rows, own_pairs, core_pairs, far_pairs, far_core_pairs)

    dk_sum = dk_keep + swap(dk_send, CORE)
    dk_far = swap(dk_sum.astype(jnp.bfloat16), Z_HI)
    quarter = half // 2
    dk_far = jnp.concatenate([dk_far[quarter:], dk_far[:quarter]], axis=0)
    key_grad = (dk_sum + dk_far.astype(jnp.float32)).astype(jnp.bfloat16)
    key_grads = [key_grad] + [swap(key_grad, 2 * m) for m in (1, 2, 3)]
    own_key_grad = jnp.stack([key_grads[m][m * ROWS : (m + 1) * ROWS] for m in range(GROUP)])
    other_key_grad = swap_tensor(own_key_grad)

    arrived = [feature_parts[0]] + [swap(feature_parts[m], 2 * m) for m in (1, 2, 3)]
    near = jnp.concatenate([part[0] for part in arrived], axis=0)
    beyond = swap(jnp.concatenate([part[1] for part in arrived], axis=0), Z_HI)
    own_features = jnp.concatenate([near, beyond], axis=0).T
    other_features = swap_tensor(own_features)

    partial = pl.pallas_call(
        weight_grad,
        out_shape=shaped((2, 256, kv_columns), jnp.float32),
        in_specs=[vmem] * (2 + GROUP),
        out_specs=vmem,
        scratch_shapes=[VMEM((half, kv_columns), jnp.bfloat16)],
        compiler_params=limits(24),
        cost_estimate=pl.CostEstimate(
            flops=4 * 256 * half * kv_columns, bytes_accessed=4 << 20, transcendentals=0
        ),
        name="weight_grad",
    )(own_features, other_features, *key_grads)
    d_wkey = partial[0] + swap(partial[1], CORE)

    leaving = lax.dynamic_slice_in_dim(w_key, (1 - side) * 2048 + core * 1024, 1024, 0)
    w_near = swap_tensor(leaving)
    w_far = swap(w_near, CORE)
    ids = jnp.stack([(index >> 1) & 3, core, side]).astype(jnp.int32)
    d_input = pl.pallas_call(
        input_grad,
        out_shape=shaped((ROWS, features // 2)),
        grid_spec=pltpu.PrefetchScalarGridSpec(
            num_scalar_prefetch=1,
            grid=(4,),
            in_specs=[
                pl.BlockSpec((GROUP, ROWS, HD), lambda k, ids: (0, 0, 0)),
                pl.BlockSpec((GROUP, ROWS, HD), lambda k, ids: (0, 0, 0)),
                pl.BlockSpec((512, kv_columns), lambda k, ids: (ids[2] * 4 + (k ^ (2 * ids[1])), 0)),
                pl.BlockSpec((512, kv_columns), lambda k, ids: (jnp.minimum(k, 1), 0)),
                pl.BlockSpec((512, kv_columns), lambda k, ids: (jnp.maximum(k - 2, 0), 0)),
            ],
            out_specs=pl.BlockSpec((ROWS, 512), lambda k, ids: (0, k ^ (2 * ids[1]))),
            scratch_shapes=[VMEM((ROWS, kv_columns), jnp.bfloat16)] * 2,
        ),
        compiler_params=limits(24),
        cost_estimate=pl.CostEstimate(
            flops=4 * ROWS * 2048 * kv_columns, bytes_accessed=5 << 20, transcendentals=0
        ),
        name="input_grad",
    )(ids, own_key_grad, other_key_grad, w_key, w_near, w_far)

    dv_sum = dv_keep + swap(dv_send, CORE)
    dv_far = swap(dv_sum[quarter:].astype(jnp.bfloat16), Z_HI)
    value_grad = (dv_sum[:quarter] + dv_far.astype(jnp.float32)).astype(jnp.bfloat16)
    value_grads = [value_grad[m * ROWS : (m + 1) * ROWS] for m in range(GROUP)]
    value_grads = [value_grads[0]] + [swap(value_grads[m], 2 * m) for m in (1, 2, 3)]
    row_grads = d_rows.reshape(GROUP, ROWS, GROUP * HD)
    row_grads = [row_grads[0]] + [swap(row_grads[m], 2 * m) for m in (1, 2, 3)]
    d_query, d_value = pl.pallas_call(
        place_rows,
        out_shape=[shaped(queries.shape), shaped(values.shape)],
        in_specs=[vmem] * (2 * GROUP),
        out_specs=[vmem] * 2,
        compiler_params=limits(16),
        name="place_rows",
    )(*row_grads, *value_grads)
    return (d_query, d_value, d_input, d_wkey)


def solution(mesh):
    by_heads = mesh.shape["dp"] == 16 and mesh.shape["tensor"] == 2
    return jax.shard_map(
        on_device_by_heads if by_heads else on_device,
        mesh=mesh,
        in_specs=(
            P("dp", None),
            P(None, "tensor"),
            P("dp", "tensor"),
            P("dp", "tensor"),
            P("dp", "tensor"),
            P(),
            P("dp"),
        ),
        out_specs=(P("dp", "tensor"), P("dp", "tensor"), P("dp", "tensor"), P("dp", "tensor")),
        check_vma=False,
    )
```

```python
import math

import jax
import jax.numpy as jnp
from jax import lax
from jax.experimental import pallas as pl
from jax.experimental.pallas import tpu as pltpu
from jax.sharding import PartitionSpec as P

HD = 128
BLK = 64


masked_fill = -1e30


def row_positions(block_pos):
    within = jnp.tile(jnp.arange(BLK, dtype=jnp.int32), block_pos.shape[0])
    return jnp.repeat(block_pos, BLK) * BLK + within


def documents(positions, doc_lens):
    starts = jnp.cumsum(doc_lens) - doc_lens
    return jnp.sum((positions[:, None] >= starts[None, :]).astype(jnp.int32), axis=1) - 1


def split_heads(block_rows, kv_heads):
    return block_rows.reshape(block_rows.shape[0], kv_heads, HD)


def scored(query_heads, key_block, score_scale):
    key_split = split_heads(key_block, query_heads.shape[1])
    return (
        jnp.einsum("qcgd,kcd->cgqk", query_heads, key_split, preferred_element_type=jnp.float32)
        * score_scale
    )


def contributions(
    query_heads, grad_heads, key_block, value_block, allowed, row_max, row_sum, delta, score_scale
):
    kv_heads = query_heads.shape[1]
    key_split = split_heads(key_block, kv_heads)
    value_split = split_heads(value_block, kv_heads)
    scores = scored(query_heads, key_block, score_scale)
    mask_full = allowed[None, None]
    probabilities = (
        jnp.where(mask_full, jnp.exp(scores - row_max[..., None]), 0.0) / row_sum[..., None]
    )
    d_prob = jnp.einsum(
        "qcgd,kcd->cgqk", grad_heads, value_split, preferred_element_type=jnp.float32
    )
    d_score = probabilities * (d_prob - delta[..., None])
    prob_bf = probabilities.astype(jnp.bfloat16)
    score_bf = d_score.astype(jnp.bfloat16)
    query_part = score_scale * jnp.einsum(
        "cgqk,kcd->qcgd", score_bf, key_split, preferred_element_type=jnp.float32
    )
    key_part = score_scale * jnp.einsum(
        "cgqk,qcgd->kcd", score_bf, query_heads, preferred_element_type=jnp.float32
    )
    value_part = jnp.einsum(
        "cgqk,qcgd->kcd", prob_bf, grad_heads, preferred_element_type=jnp.float32
    )
    width_rows = key_block.shape[0]
    partial_value = jnp.concatenate(
        [key_part.reshape(width_rows, -1), value_part.reshape(width_rows, -1)], axis=1
    )
    return (query_part, partial_value)


def on_device(inputs, w_key, values, queries, d_out, doc_lens, block_pos):
    local_rows = inputs.shape[0]
    kv_heads = values.shape[1] // HD
    group_size = queries.shape[1] // (kv_heads * HD)
    kv_columns = kv_heads * HD
    score_scale = 1.0 / math.sqrt(HD)
    key_rows = jnp.dot(inputs, w_key, preferred_element_type=jnp.float32).astype(jnp.bfloat16)
    all_keys, all_values, all_blocks = (
        lax.all_gather(key_rows, "dp", axis=0, tiled=True),
        lax.all_gather(values, "dp", axis=0, tiled=True),
        lax.all_gather(block_pos, "dp", axis=0, tiled=True),
    )
    key_pos = row_positions(all_blocks)
    key_doc = documents(key_pos, doc_lens)
    query_pos = row_positions(block_pos)
    query_doc = documents(query_pos, doc_lens)
    query_heads = queries.reshape(local_rows, kv_heads, group_size, HD)
    grad_heads = d_out.reshape(local_rows, kv_heads, group_size, HD)
    total_rows = all_keys.shape[0]
    key_width = math.gcd(512, total_rows)
    stat_shape = (kv_heads, group_size, local_rows)

    def mask_for(first_row, width_rows):
        pos_here = lax.dynamic_slice_in_dim(key_pos, first_row, width_rows, 0)
        doc_here = lax.dynamic_slice_in_dim(key_doc, first_row, width_rows, 0)
        return (query_doc[:, None] == doc_here[None, :]) & (pos_here[None, :] <= query_pos[:, None])

    def visit_stats(block_index, running):
        first_row = block_index * key_width
        key_block = lax.dynamic_slice_in_dim(all_keys, first_row, key_width, 0)
        value_block = lax.dynamic_slice_in_dim(all_values, first_row, key_width, 0)
        allowed = mask_for(first_row, key_width)

        def visit_compute_live(state_now):
            row_max, row_sum, weighted = state_now
            scores = scored(query_heads, key_block, score_scale)
            mask_full = allowed[None, None]
            new_max = jnp.maximum(
                row_max, jnp.max(jnp.where(mask_full, scores, masked_fill), axis=3)
            )
            exp_terms = jnp.where(mask_full, jnp.exp(scores - new_max[..., None]), 0.0)
            d_prob = jnp.einsum(
                "qcgd,kcd->cgqk",
                grad_heads,
                split_heads(value_block, kv_heads),
                preferred_element_type=jnp.float32,
            )
            shrink = jnp.exp(row_max - new_max)
            return (
                new_max,
                row_sum * shrink + jnp.sum(exp_terms, axis=3),
                weighted * shrink + jnp.sum(exp_terms * d_prob, axis=3),
            )

        return lax.cond(jnp.any(allowed), visit_compute_live, lambda state_now: state_now, running)

    start_state = (
        jnp.full(stat_shape, masked_fill, jnp.float32),
        jnp.zeros(stat_shape, jnp.float32),
        jnp.zeros(stat_shape, jnp.float32),
    )
    row_max, row_sum, weighted = lax.fori_loop(0, total_rows // key_width, visit_stats, start_state)
    delta = weighted / row_sum

    def block_work(key_block, value_block, allowed):
        width_rows = key_block.shape[0]

        def block_compute_live(operands):
            return contributions(
                query_heads,
                grad_heads,
                operands[0],
                operands[1],
                operands[2],
                row_max,
                row_sum,
                delta,
                score_scale,
            )

        def dead_block(operands):
            return (
                jnp.zeros((local_rows, kv_heads, group_size, HD), jnp.float32),
                jnp.zeros((width_rows, 2 * kv_columns), jnp.float32),
            )

        return lax.cond(
            jnp.any(allowed), block_compute_live, dead_block, (key_block, value_block, allowed)
        )

    query_start = jnp.zeros((local_rows, kv_heads, group_size, HD), jnp.float32)

    def visit_block(block_index, running):
        query_sum, buffer_rows = running
        first_row = block_index * key_width
        key_block = lax.dynamic_slice_in_dim(all_keys, first_row, key_width, 0)
        value_block = lax.dynamic_slice_in_dim(all_values, first_row, key_width, 0)
        query_part, partial_value = block_work(
            key_block, value_block, mask_for(first_row, key_width)
        )
        return (
            query_sum + query_part,
            lax.dynamic_update_slice_in_dim(buffer_rows, partial_value, first_row, 0),
        )

    empty_buffer = jnp.zeros((total_rows, 2 * kv_columns), jnp.float32)
    query_sum, buffer_rows = lax.fori_loop(
        0, total_rows // key_width, visit_block, (query_start, empty_buffer)
    )
    arrived = lax.all_to_all(
        buffer_rows.astype(jnp.bfloat16), "dp", split_axis=0, concat_axis=0, tiled=True
    ).astype(buffer_rows.dtype)
    own_sums = jnp.sum(arrived.reshape(-1, local_rows, 2 * kv_columns), axis=0)
    d_query = query_sum.astype(jnp.bfloat16).reshape(local_rows, kv_columns * group_size)
    key_grad = own_sums[:, :kv_columns].astype(jnp.bfloat16)
    d_value = own_sums[:, kv_columns:].astype(jnp.bfloat16)
    d_wkey = lax.psum_scatter(
        lax.dot_general(
            inputs, key_grad, (((0,), (0,)), ((), ())), preferred_element_type=jnp.float32
        ),
        "dp",
        scatter_dimension=0,
        tiled=True,
    )
    partial_input = lax.dot_general(
        key_grad, w_key, (((1,), (1,)), ((), ())), preferred_element_type=jnp.float32
    )
    d_input = lax.psum_scatter(
        partial_input.astype(jnp.bfloat16), "tensor", scatter_dimension=1, tiled=True
    )
    return (d_query, d_value, d_input, d_wkey)


CORE, Z_HI = 1, 8
GROUP = 4
ROWS = 128
TILE = 256
STACK_BYTES = 8 << 20
PART = 512
MARKED = ROWS + 16
Q_BLOCKS = GROUP * ROWS // BLK
SMEM = pltpu.SMEM
VMEM = pltpu.VMEM
HBM = pltpu.HBM
DMA = pltpu.SemaphoreType.DMA


def swap(array, mask):
    return lax.ppermute(array, "dp", [(i, i ^ mask) for i in range(16)])


def swap_tensor(array):
    return lax.ppermute(array, "tensor", [(0, 1), (1, 0)])


def own_head():
    return (lax.axis_index("dp") >> 1) & 3


def columns(index, width):
    return pl.ds(pl.multiple_of(index * width, width), width)


def whole_spec(space=VMEM):
    return pl.BlockSpec(memory_space=space)


def after(array, *earlier):
    return lax.optimization_barrier((array,) + earlier)[0]


def copy_all(pairs, semaphores):
    copies = [
        pltpu.make_async_copy(source, target, semaphores.at[i])
        for i, (source, target) in enumerate(pairs)
    ]
    for copy in copies:
        copy.start()
    return copies


def project_keys(pos_ref, inputs_ref, values_ref, w_ref, *refs):
    pair_refs, leaving_ref = refs[:GROUP], refs[GROUP]
    inputs, weights, total, semaphores = refs[GROUP + 1 :]
    head = own_head()
    spans = [pl.ds(k * PART, PART) for k in range(weights.shape[0] // PART)]
    copies = copy_all(
        [(inputs_ref, inputs)] + [(w_ref.at[span], weights.at[span]) for span in spans],
        semaphores,
    )
    lanes = lax.broadcasted_iota(jnp.int32, (16, 2 * HD), 1)
    marks = jnp.where(lanes == 0, pos_ref[0], jnp.where(lanes == 1, pos_ref[1], 0))
    for m in range(GROUP):
        pair_refs[m][:ROWS, HD:] = values_ref[:, columns(head ^ m, HD)]
        pair_refs[m][ROWS:] = marks.astype(jnp.float32).astype(jnp.bfloat16)
    copies[0].wait()
    for k, span in enumerate(spans):
        copies[1 + k].wait()
        part = jnp.dot(inputs[:, span], weights[span], preferred_element_type=jnp.float32)
        total[...] = part if k == 0 else total[...] + part
    first = (1 - lax.axis_index("tensor")) * 2 + (lax.axis_index("dp") & 1)
    leave = pltpu.make_async_copy(
        weights.at[columns(first, 1024)], leaving_ref, semaphores.at[0]
    )
    leave.start()
    for m in range(GROUP):
        pair_refs[m][:ROWS, :HD] = total[:, columns(head ^ m, HD)].astype(jnp.bfloat16)
    leave.wait()


def pack_rows(queries_ref, grads_ref, *refs):
    out_refs, semaphores = refs[:GROUP], refs[GROUP]
    head = own_head()
    pairs = []
    for m in range(GROUP):
        span = columns(head ^ m, GROUP * HD)
        pairs.append((queries_ref.at[:, span], out_refs[m].at[:, : GROUP * HD]))
        pairs.append((grads_ref.at[:, span], out_refs[m].at[:, GROUP * HD :]))
    for copy in copy_all(pairs, semaphores):
        copy.wait()


def pack_features(inputs_ref, near_ref, far_ref, semaphores):
    chip = lax.axis_index("dp") >> 1
    side = lax.axis_index("tensor")
    pairs = []
    for m in range(GROUP):
        span = columns(2 * (chip ^ m) + side, 256)
        pairs.append((inputs_ref.at[:, span], near_ref.at[m]))
        span = columns(2 * (chip ^ (m + GROUP)) + side, 256)
        pairs.append((inputs_ref.at[:, span], far_ref.at[m]))
    for copy in copy_all(pairs, semaphores):
        copy.wait()


def join_features(near_ref, far_ref, *refs):
    pairs = []
    for m, joined_ref in enumerate(refs[:GROUP]):
        pairs.append((near_ref.at[m], joined_ref.at[0]))
        pairs.append((far_ref.at[m], joined_ref.at[1]))
    for copy in copy_all(pairs, refs[GROUP]):
        copy.wait()


def turn_features(*refs):
    for j in range(2 * GROUP):
        turned = refs[j % GROUP][j // GROUP].astype(jnp.float32).T
        refs[-1][:, j * ROWS : (j + 1) * ROWS] = turned.astype(jnp.bfloat16)


def dot_nt(left, right):
    return lax.dot_general(
        left, right, (((1,), (1,)), ((), ())), preferred_element_type=jnp.float32
    )


def folded(array, reduce):
    return reduce(array.reshape(-1, 8, array.shape[-1]), axis=0)


def stack_rows(*refs):
    row_refs, (q_rows, g_rows) = refs[:GROUP], refs[GROUP:]
    for block in range(Q_BLOCKS):
        here = pl.ds(block % 2 * BLK, BLK)
        for h in range(GROUP):
            there = pl.ds(h * BLK, BLK)
            q_rows[block, there] = row_refs[block // 2][here, h * HD : (h + 1) * HD]
            g_rows[block, there] = row_refs[block // 2][
                here, (GROUP + h) * HD : (GROUP + h + 1) * HD
            ]


def attend(lens_ref, q_rows, g_rows, own_pairs, far_pairs, core_pairs, *refs):
    reach = GROUP * MARKED
    pair_refs = [own_pairs, core_pairs.at[:reach], far_pairs, core_pairs.at[reach:]]
    dq_refs, refs = refs[:GROUP], refs[GROUP:]
    dk_keep, dk_send, dv_keep, dv_send = refs[:4]
    keys, keys_t, values, dk, dv, dq_all, scores, d_prob = refs[4:12]
    marks, positions, semaphore = refs[12:]
    score_scale = 1.0 / math.sqrt(HD)
    base_two = score_scale * math.log2(math.e)

    for part in range(4 * GROUP):
        here = pl.ds(part % GROUP * MARKED + ROWS, 16)
        row = pair_refs[part // GROUP][here, :HD].astype(jnp.float32).astype(jnp.int32)
        marks[part : part + 1] = row[:1]
    to_scalars = pltpu.make_async_copy(marks, positions, semaphore)
    to_scalars.start()
    to_scalars.wait()

    def first_row(block):
        return pl.multiple_of(positions[block // 2, block % 2] * BLK, BLK)

    for block in range(4 * Q_BLOCKS):
        part = block // 2 % GROUP
        here = pl.ds(part * MARKED + block % 2 * BLK, BLK)
        there = pl.ds(first_row(block), BLK)
        keys[there] = pair_refs[block // Q_BLOCKS][here, :HD]
        values[there] = pair_refs[block // Q_BLOCKS][here, HD:]
    for tile in range(keys.shape[0] // TILE):
        here = pl.ds(tile * TILE, TILE)
        keys_t[:, here] = keys[here].astype(jnp.float32).T.astype(jnp.bfloat16)
    dk[...] = jnp.zeros_like(dk)
    dv[...] = jnp.zeros_like(dv)
    starts = [lens_ref[0]]
    for k in (1, 2):
        starts.append(starts[-1] + lens_ref[k])

    def document_start(position):
        found = jnp.zeros_like(position)
        for start in starts:
            found = jnp.where(start <= position, start, found)
        return found

    @pl.loop(0, Q_BLOCKS)
    def _(block):
        first = first_row(block)
        lanes = lax.broadcasted_iota(jnp.int32, (1, GROUP * BLK), 1)
        position = first + (lanes & (BLK - 1))
        start = document_start(position)
        low = document_start(first) // TILE
        high = (first + BLK - 1) // TILE + 1
        query = q_rows[block]
        grad = g_rows[block]
        folded_shape = (8, GROUP * BLK)

        def visit_scores(tile, row_max):
            here = columns(tile, TILE)
            raw = dot_nt(keys[here], query)
            key_position = tile * TILE + lax.broadcasted_iota(jnp.int32, raw.shape, 0)
            allowed = (key_position <= position) & (key_position >= start)
            raw = jnp.where(allowed, raw, masked_fill)
            scores[here] = raw
            d_prob[here] = dot_nt(values[here], grad)
            return jnp.maximum(row_max, folded(raw, jnp.max))

        row_max = lax.fori_loop(
            low, high, visit_scores, jnp.full(folded_shape, masked_fill, jnp.float32)
        )
        row_max = jnp.max(row_max, axis=0, keepdims=True)

        def visit_sums(tile, running):
            here = columns(tile, TILE)
            terms = jnp.exp2((scores[here] - row_max) * base_two)
            scores[here] = terms
            return (
                running[0] + folded(terms, jnp.sum),
                running[1] + folded(terms * d_prob[here], jnp.sum),
            )

        zeros = jnp.zeros(folded_shape, jnp.float32)
        row_sum, weighted = lax.fori_loop(low, high, visit_sums, (zeros, zeros))
        inverse = 1.0 / jnp.sum(row_sum, axis=0, keepdims=True)
        delta = jnp.sum(weighted, axis=0, keepdims=True) * inverse

        def visit_grads(tile, dq):
            here = columns(tile, TILE)
            prob = scores[here] * inverse
            score_bf = (prob * (d_prob[here] - delta)).astype(jnp.bfloat16)
            dk[here] += jnp.dot(score_bf, query, preferred_element_type=jnp.float32)
            dv[here] += jnp.dot(
                prob.astype(jnp.bfloat16), grad, preferred_element_type=jnp.float32
            )
            return dq + jnp.dot(keys_t[:, here], score_bf, preferred_element_type=jnp.float32)

        dq = lax.fori_loop(
            low, high, visit_grads, jnp.zeros((HD, GROUP * BLK), jnp.float32)
        )
        dq = (dq * score_scale).T.astype(jnp.bfloat16)
        for h in range(GROUP):
            dq_all[block, :, h * HD : (h + 1) * HD] = dq[h * BLK : (h + 1) * BLK]

    for block in range(Q_BLOCKS):
        dq_refs[block // 2][pl.ds(block % 2 * BLK, BLK)] = dq_all[block]
    for block in range(4 * Q_BLOCKS):
        quarter = block // Q_BLOCKS
        here = pl.ds(quarter // 2 * Q_BLOCKS * BLK + block % Q_BLOCKS * BLK, BLK)
        there = pl.ds(first_row(block), BLK)
        (dk_send if quarter % 2 else dk_keep)[here] = dk[there] * score_scale
        (dv_send if quarter % 2 else dv_keep)[here] = dv[there]


def weight_grad(own_ref, other_ref, *refs):
    grad_refs, (keep_ref, send_ref, grads) = refs[:GROUP], refs[GROUP:]
    head = own_head()
    for k, grad_ref in enumerate(grad_refs):
        for far in range(2):
            for m in range(GROUP):
                here = pl.ds((far * GROUP + m) * ROWS, ROWS)
                there = pl.ds((far * GROUP + (m ^ k)) * ROWS, ROWS)
                grads[here, columns(head ^ k, HD)] = grad_ref[there]
    own = jnp.dot(own_ref[...], grads[...], preferred_element_type=jnp.float32)
    other = jnp.dot(other_ref[...], grads[...], preferred_element_type=jnp.float32)
    crossed = (lax.axis_index("dp") & 1) ^ lax.axis_index("tensor")

    @pl.when(crossed == 0)
    def _():
        keep_ref[...] = own
        send_ref[...] = other

    @pl.when(crossed == 1)
    def _():
        keep_ref[...] = other
        send_ref[...] = own


def input_grad(own_ref, other_ref, w_own, w_near, w_far, out_ref, *refs):
    own_all, other_all, own_weights, other_weights, semaphores = refs
    head = own_head()
    core = lax.axis_index("dp") & 1
    side = lax.axis_index("tensor")
    halves = [core, 1 - core]
    pairs = []
    for k in range(4):
        half, span = halves[k // 2], pl.ds(k * PART, PART)
        pairs.append((w_own.at[columns(side * 4 + half * 2 + k % 2, PART)], own_weights.at[span]))
        source = (w_near, w_far)[k // 2].at[pl.ds(k % 2 * PART, PART)]
        pairs.append((source, other_weights.at[span]))
    copies = copy_all(pairs, semaphores)
    for k in range(GROUP):
        own_all[:, columns(head ^ k, HD)] = own_ref[k]
        other_all[:, columns(head ^ k, HD)] = other_ref[k]
    for k in range(4):
        span = pl.ds(k * PART, PART)
        copies[2 * k].wait()
        part = dot_nt(own_all[...], own_weights[span])
        copies[2 * k + 1].wait()
        part = part + dot_nt(other_all[...], other_weights[span])
        out_ref[:, columns(halves[k // 2] * 2 + k % 2, PART)] = part.astype(jnp.bfloat16)


def finish(keep_ref, arrived_ref, *refs):
    value_refs, (weight_out, value_out) = refs[:GROUP], refs[GROUP:]
    weight_out[...] = keep_ref[...] + arrived_ref[...]
    for m in range(GROUP):
        value_out[:, columns(own_head() ^ m, HD)] = value_refs[m][...]


def place_rows(*refs):
    for m, ref in enumerate(refs[:GROUP]):
        refs[GROUP][:, columns(own_head() ^ m, GROUP * HD)] = ref[...]


def shaped(shape, dtype=jnp.bfloat16):
    return jax.ShapeDtypeStruct(shape, dtype)


def limits(mebibytes):
    return pltpu.CompilerParams(vmem_limit_bytes=mebibytes << 20)


def with_partners(arrays):
    return [arrays[0]] + [swap(arrays[m], 2 * m) for m in (1, 2, 3)]


def on_device_by_heads(inputs, w_key, values, queries, d_out, doc_lens, block_pos):
    features = inputs.shape[1]
    kv_columns = values.shape[1]
    total_rows = 16 * ROWS
    half, quarter = total_rows // 2, total_rows // 4
    vmem, smem, hbm = whole_spec(), whole_spec(SMEM), whole_spec(HBM)

    near_features, far_features = pl.pallas_call(
        pack_features,
        out_shape=[shaped((GROUP, ROWS, 256))] * 2,
        in_specs=[hbm],
        out_specs=[hbm] * 2,
        scratch_shapes=[DMA((2 * GROUP,))],
        compiler_params=limits(60),
        name="pack_features",
    )(inputs)
    far_features = swap(far_features, Z_HI)
    *pairs, leaving = pl.pallas_call(
        project_keys,
        out_shape=[shaped((MARKED, 2 * HD))] * GROUP + [shaped((1024, kv_columns))],
        in_specs=[smem, hbm, vmem, hbm],
        out_specs=[vmem] * GROUP + [hbm],
        scratch_shapes=[
            VMEM((ROWS, features), jnp.bfloat16),
            VMEM((features, kv_columns), jnp.bfloat16),
            VMEM((ROWS, kv_columns), jnp.float32),
            DMA((1 + features // PART,)),
        ],
        compiler_params=limits(60),
        cost_estimate=pl.CostEstimate(
            flops=2 * ROWS * features * kv_columns,
            bytes_accessed=features * kv_columns * 2,
            transcendentals=0,
        ),
        name="project_keys",
    )(block_pos, after(inputs, near_features), values, w_key)
    packed_rows = pl.pallas_call(
        pack_rows,
        out_shape=[shaped((ROWS, 2 * GROUP * HD))] * GROUP,
        in_specs=[hbm] * 2,
        out_specs=[hbm] * GROUP,
        scratch_shapes=[DMA((2 * GROUP,))],
        compiler_params=limits(60),
        name="pack_rows",
    )(after(queries, pairs[0]), d_out)
    w_near = swap_tensor(leaving)
    own_pairs = jnp.concatenate(with_partners([after(pairs[0], packed_rows[0], far_features)] + pairs[1:]), axis=0)
    far_pairs = swap(own_pairs, Z_HI)

    rows = with_partners(packed_rows)
    near_pairs = jnp.concatenate([own_pairs, far_pairs], axis=0)
    core_pairs = swap(after(near_pairs, *rows), CORE)

    feature_parts = pl.pallas_call(
        join_features,
        out_shape=[shaped((2, ROWS, 256))] * GROUP,
        in_specs=[hbm] * 2,
        out_specs=[hbm] * GROUP,
        scratch_shapes=[DMA((2 * GROUP,))],
        compiler_params=limits(60),
        name="join_features",
    )(after(near_features, own_pairs), far_features)
    feature_parts = with_partners(feature_parts)

    stacked = shaped((Q_BLOCKS, GROUP * BLK, HD))
    q_rows, g_rows = pl.pallas_call(
        stack_rows,
        out_shape=[stacked] * 2,
        in_specs=[vmem] * GROUP,
        out_specs=[vmem] * 2,
        compiler_params=limits(16),
        cost_estimate=pl.CostEstimate(
            flops=0, bytes_accessed=STACK_BYTES, transcendentals=0
        ),
        name="stack_rows",
    )(*rows)
    q_rows = after(q_rows, w_near)
    attended = pl.pallas_call(
        attend,
        out_shape=[shaped((ROWS, GROUP * HD))] * GROUP + [shaped((half, HD), jnp.float32)] * 4,
        in_specs=[smem] + [vmem] * 5,
        out_specs=[vmem] * (GROUP + 4),
        scratch_shapes=[
            VMEM((total_rows, HD), jnp.bfloat16),
            VMEM((HD, total_rows), jnp.bfloat16),
            VMEM((total_rows, HD), jnp.bfloat16),
            VMEM((total_rows, HD), jnp.float32),
            VMEM((total_rows, HD), jnp.float32),
            VMEM((Q_BLOCKS, BLK, GROUP * HD), jnp.bfloat16),
            VMEM((total_rows, GROUP * BLK), jnp.float32),
            VMEM((total_rows, GROUP * BLK), jnp.float32),
            VMEM((4 * GROUP, HD), jnp.int32),
            SMEM((4 * GROUP, HD), jnp.int32),
            DMA,
        ],
        compiler_params=limits(32),
        cost_estimate=pl.CostEstimate(
            flops=14_000_000_000,
            bytes_accessed=6 << 20,
            transcendentals=512 * 2048,
        ),
        name="attend",
    )(doc_lens, q_rows, g_rows, own_pairs, far_pairs, core_pairs)
    row_grads, (dk_keep, dk_send, dv_keep, dv_send) = attended[:GROUP], attended[GROUP:]
    dk_send = after(dk_send, *feature_parts)

    own_features = pl.pallas_call(
        turn_features,
        out_shape=shaped((256, half)),
        in_specs=[vmem] * GROUP,
        out_specs=vmem,
        compiler_params=limits(16),
        name="turn_features",
    )(after(feature_parts[0], dk_keep), *feature_parts[1:])
    other_features = swap_tensor(own_features)
    w_far = swap(after(w_near, dk_keep), CORE)

    d_query = pl.pallas_call(
        place_rows,
        out_shape=shaped(queries.shape),
        in_specs=[vmem] * GROUP,
        out_specs=vmem,
        compiler_params=limits(16),
        name="place_rows",
    )(*with_partners(row_grads))

    dk_sum = after(dk_keep, own_features) + swap(dk_send, CORE)
    dk_far = swap(dk_sum.astype(jnp.bfloat16), Z_HI)
    dk_far = jnp.concatenate([dk_far[quarter:], dk_far[:quarter]], axis=0)
    key_grad = (dk_sum + dk_far.astype(jnp.float32)).astype(jnp.bfloat16)
    key_grad = after(key_grad, d_query)
    key_grads = with_partners([key_grad] * GROUP)
    own_key_grad = jnp.stack([key_grads[m][m * ROWS : (m + 1) * ROWS] for m in range(GROUP)])
    other_key_grad = swap_tensor(own_key_grad)

    keep, send = pl.pallas_call(
        weight_grad,
        out_shape=[shaped((256, kv_columns), jnp.float32)] * 2,
        in_specs=[vmem] * (2 + GROUP),
        out_specs=[vmem] * 2,
        scratch_shapes=[VMEM((half, kv_columns), jnp.bfloat16)],
        compiler_params=limits(24),
        cost_estimate=pl.CostEstimate(
            flops=4 * 256 * half * kv_columns, bytes_accessed=4 << 20, transcendentals=0
        ),
        name="weight_grad",
    )(own_features, other_features, *key_grads)
    arrived = swap(send, CORE)

    dv_sum = dv_keep + swap(after(dv_send, dk_sum), CORE)
    dv_far = swap(after(dv_sum[quarter:].astype(jnp.bfloat16), key_grad), Z_HI)
    value_grad = (dv_sum[:quarter] + dv_far.astype(jnp.float32)).astype(jnp.bfloat16)
    value_grads = with_partners([value_grad[m * ROWS : (m + 1) * ROWS] for m in range(GROUP)])

    d_input = pl.pallas_call(
        input_grad,
        out_shape=shaped((ROWS, features // 2)),
        in_specs=[vmem] * 2 + [hbm] * 3,
        out_specs=vmem,
        scratch_shapes=[VMEM((ROWS, kv_columns), jnp.bfloat16)] * 2
        + [VMEM((2048, kv_columns), jnp.bfloat16)] * 2
        + [DMA((8,))],
        compiler_params=limits(60),
        cost_estimate=pl.CostEstimate(
            flops=4 * ROWS * 2048 * kv_columns, bytes_accessed=5 << 20, transcendentals=0
        ),
        name="input_grad",
    )(after(own_key_grad, send), other_key_grad, w_key, w_near, w_far)

    d_wkey, d_value = pl.pallas_call(
        finish,
        out_shape=[shaped((256, kv_columns), jnp.float32), shaped(values.shape)],
        in_specs=[vmem] * (2 + GROUP),
        out_specs=[vmem] * 2,
        compiler_params=limits(16),
        name="finish",
    )(keep, arrived, *value_grads)
    return (d_query, d_value, d_input, d_wkey)


def solution(mesh):
    by_heads = mesh.shape["dp"] == 16 and mesh.shape["tensor"] == 2
    return jax.shard_map(
        on_device_by_heads if by_heads else on_device,
        mesh=mesh,
        in_specs=(
            P("dp", None),
            P(None, "tensor"),
            P("dp", "tensor"),
            P("dp", "tensor"),
            P("dp", "tensor"),
            P(),
            P("dp"),
        ),
        out_specs=(P("dp", "tensor"), P("dp", "tensor"), P("dp", "tensor"), P("dp", "tensor")),
        check_vma=False,
    )
```

```python
import math

import jax
import jax.numpy as jnp
from jax import lax
from jax.experimental import pallas as pl
from jax.experimental.pallas import tpu as pltpu
from jax.sharding import PartitionSpec as P

HD = 128
BLK = 64


masked_fill = -1e30


def row_positions(block_pos):
    within = jnp.tile(jnp.arange(BLK, dtype=jnp.int32), block_pos.shape[0])
    return jnp.repeat(block_pos, BLK) * BLK + within


def documents(positions, doc_lens):
    starts = jnp.cumsum(doc_lens) - doc_lens
    return jnp.sum((positions[:, None] >= starts[None, :]).astype(jnp.int32), axis=1) - 1


def split_heads(block_rows, kv_heads):
    return block_rows.reshape(block_rows.shape[0], kv_heads, HD)


def scored(query_heads, key_block, score_scale):
    key_split = split_heads(key_block, query_heads.shape[1])
    return (
        jnp.einsum("qcgd,kcd->cgqk", query_heads, key_split, preferred_element_type=jnp.float32)
        * score_scale
    )


def contributions(
    query_heads, grad_heads, key_block, value_block, allowed, row_max, row_sum, delta, score_scale
):
    kv_heads = query_heads.shape[1]
    key_split = split_heads(key_block, kv_heads)
    value_split = split_heads(value_block, kv_heads)
    scores = scored(query_heads, key_block, score_scale)
    mask_full = allowed[None, None]
    probabilities = (
        jnp.where(mask_full, jnp.exp(scores - row_max[..., None]), 0.0) / row_sum[..., None]
    )
    d_prob = jnp.einsum(
        "qcgd,kcd->cgqk", grad_heads, value_split, preferred_element_type=jnp.float32
    )
    d_score = probabilities * (d_prob - delta[..., None])
    prob_bf = probabilities.astype(jnp.bfloat16)
    score_bf = d_score.astype(jnp.bfloat16)
    query_part = score_scale * jnp.einsum(
        "cgqk,kcd->qcgd", score_bf, key_split, preferred_element_type=jnp.float32
    )
    key_part = score_scale * jnp.einsum(
        "cgqk,qcgd->kcd", score_bf, query_heads, preferred_element_type=jnp.float32
    )
    value_part = jnp.einsum(
        "cgqk,qcgd->kcd", prob_bf, grad_heads, preferred_element_type=jnp.float32
    )
    width_rows = key_block.shape[0]
    partial_value = jnp.concatenate(
        [key_part.reshape(width_rows, -1), value_part.reshape(width_rows, -1)], axis=1
    )
    return (query_part, partial_value)


def on_device(inputs, w_key, values, queries, d_out, doc_lens, block_pos):
    local_rows = inputs.shape[0]
    kv_heads = values.shape[1] // HD
    group_size = queries.shape[1] // (kv_heads * HD)
    kv_columns = kv_heads * HD
    score_scale = 1.0 / math.sqrt(HD)
    key_rows = jnp.dot(inputs, w_key, preferred_element_type=jnp.float32).astype(jnp.bfloat16)
    all_keys, all_values, all_blocks = (
        lax.all_gather(key_rows, "dp", axis=0, tiled=True),
        lax.all_gather(values, "dp", axis=0, tiled=True),
        lax.all_gather(block_pos, "dp", axis=0, tiled=True),
    )
    key_pos = row_positions(all_blocks)
    key_doc = documents(key_pos, doc_lens)
    query_pos = row_positions(block_pos)
    query_doc = documents(query_pos, doc_lens)
    query_heads = queries.reshape(local_rows, kv_heads, group_size, HD)
    grad_heads = d_out.reshape(local_rows, kv_heads, group_size, HD)
    total_rows = all_keys.shape[0]
    key_width = math.gcd(512, total_rows)
    stat_shape = (kv_heads, group_size, local_rows)

    def mask_for(first_row, width_rows):
        pos_here = lax.dynamic_slice_in_dim(key_pos, first_row, width_rows, 0)
        doc_here = lax.dynamic_slice_in_dim(key_doc, first_row, width_rows, 0)
        return (query_doc[:, None] == doc_here[None, :]) & (pos_here[None, :] <= query_pos[:, None])

    def visit_stats(block_index, running):
        first_row = block_index * key_width
        key_block = lax.dynamic_slice_in_dim(all_keys, first_row, key_width, 0)
        value_block = lax.dynamic_slice_in_dim(all_values, first_row, key_width, 0)
        allowed = mask_for(first_row, key_width)

        def visit_compute_live(state_now):
            row_max, row_sum, weighted = state_now
            scores = scored(query_heads, key_block, score_scale)
            mask_full = allowed[None, None]
            new_max = jnp.maximum(
                row_max, jnp.max(jnp.where(mask_full, scores, masked_fill), axis=3)
            )
            exp_terms = jnp.where(mask_full, jnp.exp(scores - new_max[..., None]), 0.0)
            d_prob = jnp.einsum(
                "qcgd,kcd->cgqk",
                grad_heads,
                split_heads(value_block, kv_heads),
                preferred_element_type=jnp.float32,
            )
            shrink = jnp.exp(row_max - new_max)
            return (
                new_max,
                row_sum * shrink + jnp.sum(exp_terms, axis=3),
                weighted * shrink + jnp.sum(exp_terms * d_prob, axis=3),
            )

        return lax.cond(jnp.any(allowed), visit_compute_live, lambda state_now: state_now, running)

    start_state = (
        jnp.full(stat_shape, masked_fill, jnp.float32),
        jnp.zeros(stat_shape, jnp.float32),
        jnp.zeros(stat_shape, jnp.float32),
    )
    row_max, row_sum, weighted = lax.fori_loop(0, total_rows // key_width, visit_stats, start_state)
    delta = weighted / row_sum

    def block_work(key_block, value_block, allowed):
        width_rows = key_block.shape[0]

        def block_compute_live(operands):
            return contributions(
                query_heads,
                grad_heads,
                operands[0],
                operands[1],
                operands[2],
                row_max,
                row_sum,
                delta,
                score_scale,
            )

        def dead_block(operands):
            return (
                jnp.zeros((local_rows, kv_heads, group_size, HD), jnp.float32),
                jnp.zeros((width_rows, 2 * kv_columns), jnp.float32),
            )

        return lax.cond(
            jnp.any(allowed), block_compute_live, dead_block, (key_block, value_block, allowed)
        )

    query_start = jnp.zeros((local_rows, kv_heads, group_size, HD), jnp.float32)

    def visit_block(block_index, running):
        query_sum, buffer_rows = running
        first_row = block_index * key_width
        key_block = lax.dynamic_slice_in_dim(all_keys, first_row, key_width, 0)
        value_block = lax.dynamic_slice_in_dim(all_values, first_row, key_width, 0)
        query_part, partial_value = block_work(
            key_block, value_block, mask_for(first_row, key_width)
        )
        return (
            query_sum + query_part,
            lax.dynamic_update_slice_in_dim(buffer_rows, partial_value, first_row, 0),
        )

    empty_buffer = jnp.zeros((total_rows, 2 * kv_columns), jnp.float32)
    query_sum, buffer_rows = lax.fori_loop(
        0, total_rows // key_width, visit_block, (query_start, empty_buffer)
    )
    arrived = lax.all_to_all(
        buffer_rows.astype(jnp.bfloat16), "dp", split_axis=0, concat_axis=0, tiled=True
    ).astype(buffer_rows.dtype)
    own_sums = jnp.sum(arrived.reshape(-1, local_rows, 2 * kv_columns), axis=0)
    d_query = query_sum.astype(jnp.bfloat16).reshape(local_rows, kv_columns * group_size)
    key_grad = own_sums[:, :kv_columns].astype(jnp.bfloat16)
    d_value = own_sums[:, kv_columns:].astype(jnp.bfloat16)
    d_wkey = lax.psum_scatter(
        lax.dot_general(
            inputs, key_grad, (((0,), (0,)), ((), ())), preferred_element_type=jnp.float32
        ),
        "dp",
        scatter_dimension=0,
        tiled=True,
    )
    partial_input = lax.dot_general(
        key_grad, w_key, (((1,), (1,)), ((), ())), preferred_element_type=jnp.float32
    )
    d_input = lax.psum_scatter(
        partial_input.astype(jnp.bfloat16), "tensor", scatter_dimension=1, tiled=True
    )
    return (d_query, d_value, d_input, d_wkey)


CORE, Z_HI = 1, 8
GROUP = 4
ROWS = 128
TILE = 256
UNROLLED = 5
ATTEND_COST = 1 << 20
PART = 512
MARKED = ROWS + 16
Q_BLOCKS = GROUP * ROWS // BLK
SMEM = pltpu.SMEM
VMEM = pltpu.VMEM
HBM = pltpu.HBM
DMA = pltpu.SemaphoreType.DMA


def swap(array, mask):
    return lax.ppermute(array, "dp", [(i, i ^ mask) for i in range(16)])


def swap_tensor(array):
    return lax.ppermute(array, "tensor", [(0, 1), (1, 0)])


def own_head():
    return (lax.axis_index("dp") >> 1) & 3


def columns(index, width):
    return pl.ds(pl.multiple_of(index * width, width), width)


def whole_spec(space=VMEM):
    return pl.BlockSpec(memory_space=space)


def after(array, *earlier):
    return lax.optimization_barrier((array,) + earlier)[0]


def copy_all(pairs, semaphores):
    copies = [
        pltpu.make_async_copy(source, target, semaphores.at[i])
        for i, (source, target) in enumerate(pairs)
    ]
    for copy in copies:
        copy.start()
    return copies


def project_keys(pos_ref, inputs_ref, values_ref, w_ref, *refs):
    pair_refs = refs[:GROUP]
    inputs, weights, total, semaphores = refs[GROUP:]
    head = own_head()
    spans = [pl.ds(k * PART, PART) for k in range(weights.shape[0] // PART)]
    copies = copy_all(
        [(inputs_ref, inputs)] + [(w_ref.at[span], weights.at[span]) for span in spans],
        semaphores,
    )
    lanes = lax.broadcasted_iota(jnp.int32, (16, 2 * HD), 1)
    marks = jnp.where(lanes == 0, pos_ref[0], jnp.where(lanes == 1, pos_ref[1], 0))
    for m in range(GROUP):
        pair_refs[m][:ROWS, HD:] = values_ref[:, columns(head ^ m, HD)]
        pair_refs[m][ROWS:] = marks.astype(jnp.float32).astype(jnp.bfloat16)
    copies[0].wait()
    for k, span in enumerate(spans):
        copies[1 + k].wait()
        part = jnp.dot(inputs[:, span], weights[span], preferred_element_type=jnp.float32)
        total[...] = part if k == 0 else total[...] + part
    for m in range(GROUP):
        pair_refs[m][:ROWS, :HD] = total[:, columns(head ^ m, HD)].astype(jnp.bfloat16)


def pack_rows(queries_ref, grads_ref, *out_refs):
    head = own_head()
    for m, out_ref in enumerate(out_refs):
        span = columns(head ^ m, GROUP * HD)
        out_ref[:, : GROUP * HD] = queries_ref[:, span]
        out_ref[:, GROUP * HD :] = grads_ref[:, span]


def pack_weights(w_ref, leaving_ref, semaphore):
    first = (1 - lax.axis_index("tensor")) * 2 + (lax.axis_index("dp") & 1)
    copy = pltpu.make_async_copy(w_ref.at[columns(first, 2 * PART)], leaving_ref, semaphore)
    copy.start()
    copy.wait()


def pack_features(inputs_ref, near_ref, far_ref):
    chip = lax.axis_index("dp") >> 1
    side = lax.axis_index("tensor")
    for m in range(GROUP):
        near_ref[m] = inputs_ref[:, columns(2 * (chip ^ m) + side, 256)]
        far_ref[m] = inputs_ref[:, columns(2 * (chip ^ (m + GROUP)) + side, 256)]


def join_features(near_ref, far_ref, *joined_refs):
    for m, joined_ref in enumerate(joined_refs):
        joined_ref[0] = near_ref[m]
        joined_ref[1] = far_ref[m]


def turn_features(*refs):
    for j in range(2 * GROUP):
        turned = refs[j % GROUP][j // GROUP].astype(jnp.float32).T
        refs[-1][:, j * ROWS : (j + 1) * ROWS] = turned.astype(jnp.bfloat16)


def dot_nt(left, right):
    return lax.dot_general(
        left, right, (((1,), (1,)), ((), ())), preferred_element_type=jnp.float32
    )


def folded(array, reduce):
    return reduce(array.reshape(-1, 8, array.shape[-1]), axis=0)


def first_row_of(positions):
    def first_row(block):
        return pl.multiple_of(positions[block // 2, block % 2] * BLK, BLK)

    return first_row


def attend_rows(
    first_part, first_row, lens_ref, row_refs, dq_refs, keys, keys_t, values, dk, dv, scratch
):
    q_rows, g_rows, dq_all, scores, d_prob = scratch
    score_scale = 1.0 / math.sqrt(HD)
    base_two = score_scale * math.log2(math.e)
    parts = len(row_refs)
    for block in range(2 * parts):
        here = pl.ds(block % 2 * BLK, BLK)
        for h in range(GROUP):
            there = pl.ds(h * BLK, BLK)
            q_rows[block, there] = row_refs[block // 2][here, h * HD : (h + 1) * HD]
            g_rows[block, there] = row_refs[block // 2][
                here, (GROUP + h) * HD : (GROUP + h + 1) * HD
            ]
    starts = [lens_ref[0]]
    for k in (1, 2):
        starts.append(starts[-1] + lens_ref[k])

    def document_start(position):
        found = jnp.zeros_like(position)
        for start in starts:
            found = jnp.where(start <= position, start, found)
        return found

    @pl.loop(0, 2 * parts)
    def _(block):
        first = first_row(2 * first_part + block)
        lanes = lax.broadcasted_iota(jnp.int32, (1, GROUP * BLK), 1)
        position = first + (lanes & (BLK - 1))
        start = document_start(position)
        low = document_start(first) // TILE
        count = (first + BLK - 1) // TILE + 1 - low

        def run(over_tiles):
            query = q_rows[block]
            grad = g_rows[block]
            zeros = jnp.zeros((8, GROUP * BLK), jnp.float32)

            def visit_scores(k, row_max):
                here = columns(low + k, TILE)
                raw = dot_nt(keys[here], query)
                row = (low + k) * TILE + lax.broadcasted_iota(jnp.int32, raw.shape, 0)
                raw = jnp.where((row <= position) & (row >= start), raw, masked_fill)
                scores[k] = raw
                d_prob[k] = dot_nt(values[here], grad)
                return jnp.maximum(row_max, folded(raw, jnp.max))

            row_max = over_tiles(visit_scores, zeros + masked_fill)
            row_max = jnp.max(row_max, axis=0, keepdims=True)

            def visit_sums(k, running):
                terms = jnp.exp2((scores[k] - row_max) * base_two)
                scores[k] = terms
                return (
                    running[0] + folded(terms, jnp.sum),
                    running[1] + folded(terms * d_prob[k], jnp.sum),
                )

            row_sum, weighted = over_tiles(visit_sums, (zeros, zeros))
            inverse = 1.0 / jnp.sum(row_sum, axis=0, keepdims=True)
            delta = jnp.sum(weighted, axis=0, keepdims=True) * inverse

            def visit_grads(k, dq):
                here = columns(low + k, TILE)
                prob = scores[k] * inverse
                score_bf = (prob * (d_prob[k] - delta)).astype(jnp.bfloat16)
                dk[here] += jnp.dot(score_bf, query, preferred_element_type=jnp.float32)
                dv[here] += jnp.dot(
                    prob.astype(jnp.bfloat16), grad, preferred_element_type=jnp.float32
                )
                return dq + jnp.dot(
                    keys_t[:, here], score_bf, preferred_element_type=jnp.float32
                )

            dq = over_tiles(visit_grads, jnp.zeros((HD, GROUP * BLK), jnp.float32))
            dq = (dq * score_scale).T.astype(jnp.bfloat16)
            for h in range(GROUP):
                dq_all[block, :, h * HD : (h + 1) * HD] = dq[h * BLK : (h + 1) * BLK]

        for fixed in range(1, UNROLLED + 1):

            @pl.when(count == fixed)
            def _(fixed=fixed):
                def over_tiles(visit, running):
                    for k in range(fixed):
                        running = visit(k, running)
                    return running

                run(over_tiles)

        @pl.when(count > UNROLLED)
        def _():
            run(lambda visit, running: lax.fori_loop(0, count, visit, running))

    for block in range(2 * parts):
        dq_refs[block // 2][pl.ds(block % 2 * BLK, BLK)] = dq_all[block]


def attend_first(lens_ref, *refs):
    row_refs, refs = refs[: GROUP - 1], refs[GROUP - 1 :]
    own_a, own_b, far_a, far_b, core_pairs, refs = *refs[:5], refs[5:]
    dq_refs, refs = refs[: GROUP - 1], refs[GROUP - 1 :]
    keys, keys_t, values, dk, dv, marks, refs = *refs[:6], refs[6:]
    scratch, (positions, semaphore) = refs[:5], refs[5:]
    reach = 2 * MARKED
    pair_refs = [own_a, own_b]
    pair_refs += [core_pairs.at[pl.ds(k * reach, reach)] for k in range(2)]
    pair_refs += [far_a, far_b]
    pair_refs += [core_pairs.at[pl.ds(k * reach, reach)] for k in range(2, 4)]
    for part in range(4 * GROUP):
        here = pl.ds(part % 2 * MARKED + ROWS, 16)
        row = pair_refs[part // 2][here, :HD].astype(jnp.float32).astype(jnp.int32)
        marks[part : part + 1] = row[:1]
    to_scalars = pltpu.make_async_copy(marks, positions, semaphore)
    to_scalars.start()
    dk[...] = jnp.zeros_like(dk)
    dv[...] = jnp.zeros_like(dv)
    to_scalars.wait()
    first_row = first_row_of(positions)
    for block in range(4 * Q_BLOCKS):
        part = block // 2
        here = pl.ds(part % 2 * MARKED + block % 2 * BLK, BLK)
        there = pl.ds(first_row(block), BLK)
        keys[there] = pair_refs[part // 2][here, :HD]
        values[there] = pair_refs[part // 2][here, HD:]
    for tile in range(keys.shape[0] // TILE):
        here = pl.ds(tile * TILE, TILE)
        keys_t[:, here] = keys[here].astype(jnp.float32).T.astype(jnp.bfloat16)
    attend_rows(
        0, first_row, lens_ref, row_refs, dq_refs, keys, keys_t, values, dk, dv, scratch
    )


def attend_last(lens_ref, row_ref, keys, keys_t, values, dk_first, dv_first, marks, *refs):
    dq_ref, kept, sent, dk, dv, refs = *refs[:5], refs[5:]
    scratch, (positions, semaphore) = refs[:5], refs[5:]
    score_scale = 1.0 / math.sqrt(HD)
    to_scalars = pltpu.make_async_copy(marks, positions, semaphore)
    to_scalars.start()
    dk[...] = dk_first[...]
    dv[...] = dv_first[...]
    to_scalars.wait()
    first_row = first_row_of(positions)
    attend_rows(
        GROUP - 1, first_row, lens_ref, [row_ref], [dq_ref], keys, keys_t, values, dk, dv, scratch
    )
    for block in range(4 * Q_BLOCKS):
        quarter = block // Q_BLOCKS
        here = pl.ds(quarter // 2 * Q_BLOCKS * BLK + block % Q_BLOCKS * BLK, BLK)
        there = pl.ds(first_row(block), BLK)
        out_ref = sent if quarter % 2 else kept
        out_ref[here, :HD] = dk[there] * score_scale
        out_ref[here, HD:] = dv[there]


def weight_grad(own_ref, other_ref, *refs):
    grad_refs, (keep_ref, send_ref, grads) = refs[:GROUP], refs[GROUP:]
    head = own_head()
    for k, grad_ref in enumerate(grad_refs):
        for far in range(2):
            for m in range(GROUP):
                here = pl.ds((far * GROUP + m) * ROWS, ROWS)
                there = pl.ds((far * GROUP + (m ^ k)) * ROWS, ROWS)
                grads[here, columns(head ^ k, HD)] = grad_ref[there]
    own = jnp.dot(own_ref[...], grads[...], preferred_element_type=jnp.float32)
    other = jnp.dot(other_ref[...], grads[...], preferred_element_type=jnp.float32)
    crossed = (lax.axis_index("dp") & 1) ^ lax.axis_index("tensor")

    @pl.when(crossed == 0)
    def _():
        keep_ref[...] = own
        send_ref[...] = other

    @pl.when(crossed == 1)
    def _():
        keep_ref[...] = other
        send_ref[...] = own


def input_grad(own_ref, other_ref, w_own, w_near, w_far, out_ref, own_all, other_all):
    head = own_head()
    core = lax.axis_index("dp") & 1
    side = lax.axis_index("tensor")
    for k in range(GROUP):
        own_all[:, columns(head ^ k, HD)] = own_ref[k]
        other_all[:, columns(head ^ k, HD)] = other_ref[k]
    for k in range(4):
        chunk = 2 * (core ^ (k // 2)) + k % 2
        w_other = (w_near, w_far)[k // 2][pl.ds(k % 2 * PART, PART)]
        part = dot_nt(own_all[...], w_own[columns(side * 4 + chunk, PART)])
        part = part + dot_nt(other_all[...], w_other)
        out_ref[:, columns(chunk, PART)] = part.astype(jnp.bfloat16)


def pack_grads(value_ref, row_ref, *refs):
    for m, out_ref in enumerate(refs):
        out_ref[:, :HD] = value_ref[m * ROWS : (m + 1) * ROWS]
    refs[-1][:, HD:] = row_ref[...]


def finish(keep_ref, arrived_ref, *refs):
    row_refs, grad_refs, refs = refs[: GROUP - 1], refs[GROUP - 1 : 2 * GROUP - 1], refs[2 * GROUP - 1 :]
    weight_out, query_out, value_out = refs
    head = own_head()
    weight_out[...] = keep_ref[...] + arrived_ref[...]
    for m in range(GROUP):
        row = row_refs[m][...] if m < GROUP - 1 else grad_refs[m][:, HD:]
        query_out[:, columns(head ^ m, GROUP * HD)] = row
        value_out[:, columns(head ^ m, HD)] = grad_refs[m][:, :HD]


def shaped(shape, dtype=jnp.bfloat16):
    return jax.ShapeDtypeStruct(shape, dtype)


def limits(mebibytes):
    return pltpu.CompilerParams(vmem_limit_bytes=mebibytes << 20)


def with_partners(arrays):
    return [arrays[0]] + [swap(arrays[m], 2 * m) for m in range(1, len(arrays))]


def on_device_by_heads(inputs, w_key, values, queries, d_out, doc_lens, block_pos):
    features = inputs.shape[1]
    kv_columns = values.shape[1]
    total_rows = 16 * ROWS
    half, quarter = total_rows // 2, total_rows // 4
    vmem, smem, hbm = whole_spec(), whole_spec(SMEM), whole_spec(HBM)

    pairs = pl.pallas_call(
        project_keys,
        out_shape=[shaped((MARKED, 2 * HD))] * GROUP,
        in_specs=[smem, hbm, vmem, hbm],
        out_specs=[vmem] * GROUP,
        scratch_shapes=[
            VMEM((ROWS, features), jnp.bfloat16),
            VMEM((features, kv_columns), jnp.bfloat16),
            VMEM((ROWS, kv_columns), jnp.float32),
            DMA((1 + features // PART,)),
        ],
        compiler_params=limits(60),
        cost_estimate=pl.CostEstimate(
            flops=2 * ROWS * features * kv_columns,
            bytes_accessed=features * kv_columns * 2,
            transcendentals=0,
        ),
        name="project_keys",
    )(block_pos, inputs, values, w_key)

    packed_rows = pl.pallas_call(
        pack_rows,
        out_shape=[shaped((ROWS, 2 * GROUP * HD))] * GROUP,
        in_specs=[vmem] * 2,
        out_specs=[vmem] * GROUP,
        compiler_params=limits(8),
        name="pack_rows",
    )(after(queries, pairs[0]), d_out)

    leaving = pl.pallas_call(
        pack_weights,
        out_shape=shaped((2 * PART, kv_columns)),
        in_specs=[hbm],
        out_specs=vmem,
        scratch_shapes=[DMA],
        compiler_params=limits(56),
        name="pack_weights",
    )(after(w_key, packed_rows[0]))
    pairs = [after(pairs[0], leaving)] + list(pairs[1:])
    pairs = with_partners(pairs)
    own_a = jnp.concatenate(pairs[:2], axis=0)
    own_b = jnp.concatenate(pairs[2:], axis=0)
    far_a = swap(own_a, Z_HI)
    far_b = swap(own_b, Z_HI)
    rows = with_partners(packed_rows)

    near_features, far_features = pl.pallas_call(
        pack_features,
        out_shape=[shaped((GROUP, ROWS, 256))] * 2,
        in_specs=[vmem],
        out_specs=[vmem] * 2,
        compiler_params=limits(8),
        name="pack_features",
    )(after(inputs, own_a))
    w_near = swap_tensor(leaving)
    near_pairs = jnp.concatenate([own_a, own_b, far_a, far_b], axis=0)
    core_pairs = swap(after(near_pairs, near_features, leaving, rows[1], rows[2]), CORE)
    far_features = swap(far_features, Z_HI)

    row_grad = shaped((ROWS, GROUP * HD))
    sorted_rows = shaped((total_rows, HD))
    sums = shaped((total_rows, HD), jnp.float32)
    half_sums = shaped((half, 2 * HD), jnp.float32)

    def attend_scratch(blocks):
        stacked = VMEM((blocks, GROUP * BLK, HD), jnp.bfloat16)
        tiles = VMEM((total_rows // TILE, TILE, GROUP * BLK), jnp.float32)
        return [
            stacked,
            stacked,
            VMEM((blocks, BLK, GROUP * HD), jnp.bfloat16),
            tiles,
            tiles,
            SMEM((4 * GROUP, HD), jnp.int32),
            DMA,
        ]

    *row_grads, keys, keys_t, all_values, dk_first, dv_first, marks = pl.pallas_call(
        attend_first,
        out_shape=[row_grad] * (GROUP - 1)
        + [sorted_rows, shaped((HD, total_rows)), sorted_rows, sums, sums]
        + [shaped((4 * GROUP, HD), jnp.int32)],
        in_specs=[smem] + [vmem] * (GROUP + 4),
        out_specs=[vmem] * (GROUP + 5),
        scratch_shapes=attend_scratch(Q_BLOCKS - 2),
        compiler_params=limits(20),
        cost_estimate=pl.CostEstimate(flops=ATTEND_COST, bytes_accessed=0, transcendentals=0),
        name="attend_first",
    )(doc_lens, *rows[:-1], own_a, own_b, far_a, far_b, core_pairs)
    last_grad, kept, sent = pl.pallas_call(
        attend_last,
        out_shape=[row_grad, half_sums, half_sums],
        in_specs=[smem] + [vmem] * 7,
        out_specs=[vmem] * 3,
        scratch_shapes=[VMEM((total_rows, HD), jnp.float32)] * 2 + attend_scratch(2),
        compiler_params=limits(20),
        cost_estimate=pl.CostEstimate(flops=ATTEND_COST, bytes_accessed=0, transcendentals=0),
        name="attend_last",
    )(doc_lens, rows[-1], keys, keys_t, all_values, dk_first, dv_first, marks)

    sent = after(sent, far_features, w_near)
    row_grads = with_partners(row_grads)
    grads = after(kept, *row_grads) + swap(sent, CORE)
    dk_sum, dv_sum = grads[:, :HD], grads[:, HD:]
    dk_far = swap(dk_sum.astype(jnp.bfloat16), Z_HI)
    w_far = swap(after(w_near, dk_sum), CORE)

    feature_parts = pl.pallas_call(
        join_features,
        out_shape=[shaped((2, ROWS, 256))] * GROUP,
        in_specs=[vmem] * 2,
        out_specs=[vmem] * GROUP,
        compiler_params=limits(16),
        name="join_features",
    )(after(near_features, sent), far_features)
    own_features = pl.pallas_call(
        turn_features,
        out_shape=shaped((256, half)),
        in_specs=[vmem] * GROUP,
        out_specs=vmem,
        compiler_params=limits(16),
        name="turn_features",
    )(*with_partners(feature_parts))
    other_features = swap_tensor(own_features)

    dk_far = jnp.concatenate([dk_far[quarter:], dk_far[:quarter]], axis=0)
    key_grad = (dk_sum + dk_far.astype(jnp.float32)).astype(jnp.bfloat16)
    key_grad = after(key_grad, own_features, w_far)
    key_grads = with_partners([key_grad] * GROUP)
    own_key_grad = jnp.stack([key_grads[m][m * ROWS : (m + 1) * ROWS] for m in range(GROUP)])
    other_key_grad = swap_tensor(own_key_grad)

    dv_far = swap(after(dv_sum[quarter:].astype(jnp.bfloat16), key_grad), Z_HI)
    value_grad = (dv_sum[:quarter] + dv_far.astype(jnp.float32)).astype(jnp.bfloat16)
    packed_grads = pl.pallas_call(
        pack_grads,
        out_shape=[shaped((ROWS, HD))] * (GROUP - 1) + [shaped((ROWS, (GROUP + 1) * HD))],
        in_specs=[vmem] * 2,
        out_specs=[vmem] * GROUP,
        compiler_params=limits(16),
        name="pack_grads",
    )(value_grad, last_grad)
    packed_grads = [after(packed_grads[0], own_key_grad)] + [
        after(grad, own_key_grad) for grad in packed_grads[1:]
    ]

    keep, send = pl.pallas_call(
        weight_grad,
        out_shape=[shaped((256, kv_columns), jnp.float32)] * 2,
        in_specs=[vmem] * (2 + GROUP),
        out_specs=[vmem] * 2,
        scratch_shapes=[VMEM((half, kv_columns), jnp.bfloat16)],
        compiler_params=limits(24),
        cost_estimate=pl.CostEstimate(
            flops=4 * 256 * half * kv_columns, bytes_accessed=4 << 20, transcendentals=0
        ),
        name="weight_grad",
    )(own_features, other_features, *key_grads)
    arrived = swap(send, CORE)

    d_input = pl.pallas_call(
        input_grad,
        out_shape=shaped((ROWS, features // 2)),
        in_specs=[vmem] * 5,
        out_specs=vmem,
        scratch_shapes=[VMEM((ROWS, kv_columns), jnp.bfloat16)] * 2,
        compiler_params=limits(16),
        cost_estimate=pl.CostEstimate(
            flops=4 * ROWS * 2048 * kv_columns, bytes_accessed=5 << 20, transcendentals=0
        ),
        name="input_grad",
    )(after(own_key_grad, send), other_key_grad, w_key, w_near, w_far)

    d_wkey, d_query, d_value = pl.pallas_call(
        finish,
        out_shape=[
            shaped((256, kv_columns), jnp.float32),
            shaped(queries.shape),
            shaped(values.shape),
        ],
        in_specs=[vmem] * (1 + 2 * GROUP),
        out_specs=[vmem] * 3,
        compiler_params=limits(16),
        name="finish",
    )(keep, arrived, *row_grads, *with_partners(packed_grads))
    return (d_query, d_value, d_input, d_wkey)


def solution(mesh):
    by_heads = mesh.shape["dp"] == 16 and mesh.shape["tensor"] == 2
    return jax.shard_map(
        on_device_by_heads if by_heads else on_device,
        mesh=mesh,
        in_specs=(
            P("dp", None),
            P(None, "tensor"),
            P("dp", "tensor"),
            P("dp", "tensor"),
            P("dp", "tensor"),
            P(),
            P("dp"),
        ),
        out_specs=(P("dp", "tensor"), P("dp", "tensor"), P("dp", "tensor"), P("dp", "tensor")),
        check_vma=False,
    )
```

```python
import math

import jax
import jax.numpy as jnp
from jax import lax
from jax.experimental import pallas as pl
from jax.experimental.pallas import tpu as pltpu
from jax.sharding import PartitionSpec as P

HD = 128
BLK = 64


masked_fill = -1e30


def row_positions(block_pos):
    within = jnp.tile(jnp.arange(BLK, dtype=jnp.int32), block_pos.shape[0])
    return jnp.repeat(block_pos, BLK) * BLK + within


def documents(positions, doc_lens):
    starts = jnp.cumsum(doc_lens) - doc_lens
    return jnp.sum((positions[:, None] >= starts[None, :]).astype(jnp.int32), axis=1) - 1


def split_heads(block_rows, kv_heads):
    return block_rows.reshape(block_rows.shape[0], kv_heads, HD)


def scored(query_heads, key_block, score_scale):
    key_split = split_heads(key_block, query_heads.shape[1])
    return (
        jnp.einsum("qcgd,kcd->cgqk", query_heads, key_split, preferred_element_type=jnp.float32)
        * score_scale
    )


def contributions(
    query_heads, grad_heads, key_block, value_block, allowed, row_max, row_sum, delta, score_scale
):
    kv_heads = query_heads.shape[1]
    key_split = split_heads(key_block, kv_heads)
    value_split = split_heads(value_block, kv_heads)
    scores = scored(query_heads, key_block, score_scale)
    mask_full = allowed[None, None]
    probabilities = (
        jnp.where(mask_full, jnp.exp(scores - row_max[..., None]), 0.0) / row_sum[..., None]
    )
    d_prob = jnp.einsum(
        "qcgd,kcd->cgqk", grad_heads, value_split, preferred_element_type=jnp.float32
    )
    d_score = probabilities * (d_prob - delta[..., None])
    prob_bf = probabilities.astype(jnp.bfloat16)
    score_bf = d_score.astype(jnp.bfloat16)
    query_part = score_scale * jnp.einsum(
        "cgqk,kcd->qcgd", score_bf, key_split, preferred_element_type=jnp.float32
    )
    key_part = score_scale * jnp.einsum(
        "cgqk,qcgd->kcd", score_bf, query_heads, preferred_element_type=jnp.float32
    )
    value_part = jnp.einsum(
        "cgqk,qcgd->kcd", prob_bf, grad_heads, preferred_element_type=jnp.float32
    )
    width_rows = key_block.shape[0]
    partial_value = jnp.concatenate(
        [key_part.reshape(width_rows, -1), value_part.reshape(width_rows, -1)], axis=1
    )
    return (query_part, partial_value)


def on_device(inputs, w_key, values, queries, d_out, doc_lens, block_pos):
    local_rows = inputs.shape[0]
    kv_heads = values.shape[1] // HD
    group_size = queries.shape[1] // (kv_heads * HD)
    kv_columns = kv_heads * HD
    score_scale = 1.0 / math.sqrt(HD)
    key_rows = jnp.dot(inputs, w_key, preferred_element_type=jnp.float32).astype(jnp.bfloat16)
    all_keys, all_values, all_blocks = (
        lax.all_gather(key_rows, "dp", axis=0, tiled=True),
        lax.all_gather(values, "dp", axis=0, tiled=True),
        lax.all_gather(block_pos, "dp", axis=0, tiled=True),
    )
    key_pos = row_positions(all_blocks)
    key_doc = documents(key_pos, doc_lens)
    query_pos = row_positions(block_pos)
    query_doc = documents(query_pos, doc_lens)
    query_heads = queries.reshape(local_rows, kv_heads, group_size, HD)
    grad_heads = d_out.reshape(local_rows, kv_heads, group_size, HD)
    total_rows = all_keys.shape[0]
    key_width = math.gcd(512, total_rows)
    stat_shape = (kv_heads, group_size, local_rows)

    def mask_for(first_row, width_rows):
        pos_here = lax.dynamic_slice_in_dim(key_pos, first_row, width_rows, 0)
        doc_here = lax.dynamic_slice_in_dim(key_doc, first_row, width_rows, 0)
        return (query_doc[:, None] == doc_here[None, :]) & (pos_here[None, :] <= query_pos[:, None])

    def visit_stats(block_index, running):
        first_row = block_index * key_width
        key_block = lax.dynamic_slice_in_dim(all_keys, first_row, key_width, 0)
        value_block = lax.dynamic_slice_in_dim(all_values, first_row, key_width, 0)
        allowed = mask_for(first_row, key_width)

        def visit_compute_live(state_now):
            row_max, row_sum, weighted = state_now
            scores = scored(query_heads, key_block, score_scale)
            mask_full = allowed[None, None]
            new_max = jnp.maximum(
                row_max, jnp.max(jnp.where(mask_full, scores, masked_fill), axis=3)
            )
            exp_terms = jnp.where(mask_full, jnp.exp(scores - new_max[..., None]), 0.0)
            d_prob = jnp.einsum(
                "qcgd,kcd->cgqk",
                grad_heads,
                split_heads(value_block, kv_heads),
                preferred_element_type=jnp.float32,
            )
            shrink = jnp.exp(row_max - new_max)
            return (
                new_max,
                row_sum * shrink + jnp.sum(exp_terms, axis=3),
                weighted * shrink + jnp.sum(exp_terms * d_prob, axis=3),
            )

        return lax.cond(jnp.any(allowed), visit_compute_live, lambda state_now: state_now, running)

    start_state = (
        jnp.full(stat_shape, masked_fill, jnp.float32),
        jnp.zeros(stat_shape, jnp.float32),
        jnp.zeros(stat_shape, jnp.float32),
    )
    row_max, row_sum, weighted = lax.fori_loop(0, total_rows // key_width, visit_stats, start_state)
    delta = weighted / row_sum

    def block_work(key_block, value_block, allowed):
        width_rows = key_block.shape[0]

        def block_compute_live(operands):
            return contributions(
                query_heads,
                grad_heads,
                operands[0],
                operands[1],
                operands[2],
                row_max,
                row_sum,
                delta,
                score_scale,
            )

        def dead_block(operands):
            return (
                jnp.zeros((local_rows, kv_heads, group_size, HD), jnp.float32),
                jnp.zeros((width_rows, 2 * kv_columns), jnp.float32),
            )

        return lax.cond(
            jnp.any(allowed), block_compute_live, dead_block, (key_block, value_block, allowed)
        )

    query_start = jnp.zeros((local_rows, kv_heads, group_size, HD), jnp.float32)

    def visit_block(block_index, running):
        query_sum, buffer_rows = running
        first_row = block_index * key_width
        key_block = lax.dynamic_slice_in_dim(all_keys, first_row, key_width, 0)
        value_block = lax.dynamic_slice_in_dim(all_values, first_row, key_width, 0)
        query_part, partial_value = block_work(
            key_block, value_block, mask_for(first_row, key_width)
        )
        return (
            query_sum + query_part,
            lax.dynamic_update_slice_in_dim(buffer_rows, partial_value, first_row, 0),
        )

    empty_buffer = jnp.zeros((total_rows, 2 * kv_columns), jnp.float32)
    query_sum, buffer_rows = lax.fori_loop(
        0, total_rows // key_width, visit_block, (query_start, empty_buffer)
    )
    arrived = lax.all_to_all(
        buffer_rows.astype(jnp.bfloat16), "dp", split_axis=0, concat_axis=0, tiled=True
    ).astype(buffer_rows.dtype)
    own_sums = jnp.sum(arrived.reshape(-1, local_rows, 2 * kv_columns), axis=0)
    d_query = query_sum.astype(jnp.bfloat16).reshape(local_rows, kv_columns * group_size)
    key_grad = own_sums[:, :kv_columns].astype(jnp.bfloat16)
    d_value = own_sums[:, kv_columns:].astype(jnp.bfloat16)
    d_wkey = lax.psum_scatter(
        lax.dot_general(
            inputs, key_grad, (((0,), (0,)), ((), ())), preferred_element_type=jnp.float32
        ),
        "dp",
        scatter_dimension=0,
        tiled=True,
    )
    partial_input = lax.dot_general(
        key_grad, w_key, (((1,), (1,)), ((), ())), preferred_element_type=jnp.float32
    )
    d_input = lax.psum_scatter(
        partial_input.astype(jnp.bfloat16), "tensor", scatter_dimension=1, tiled=True
    )
    return (d_query, d_value, d_input, d_wkey)


CORE, Z_HI = 1, 8
GROUP = 4
ROWS = 128
TILE = 256
UNROLLED = 5
ATTEND_COST = 1 << 20
PART = 512
MARKED = ROWS + 16
Q_BLOCKS = GROUP * ROWS // BLK
SMEM = pltpu.SMEM
VMEM = pltpu.VMEM
HBM = pltpu.HBM
DMA = pltpu.SemaphoreType.DMA


def swap(array, mask):
    return lax.ppermute(array, "dp", [(i, i ^ mask) for i in range(16)])


def swap_tensor(array):
    return lax.ppermute(array, "tensor", [(0, 1), (1, 0)])


def own_head():
    return (lax.axis_index("dp") >> 1) & 3


def columns(index, width):
    return pl.ds(pl.multiple_of(index * width, width), width)


def whole_spec(space=VMEM):
    return pl.BlockSpec(memory_space=space)


def after(array, *earlier):
    return lax.optimization_barrier((array,) + earlier)[0]


def copy_all(pairs, semaphores):
    copies = [
        pltpu.make_async_copy(source, target, semaphores.at[i])
        for i, (source, target) in enumerate(pairs)
    ]
    for copy in copies:
        copy.start()
    return copies


def project_keys(pos_ref, inputs_ref, values_ref, w_ref, *refs):
    pair_refs = refs[:GROUP]
    inputs, weights, total, semaphores = refs[GROUP:]
    head = own_head()
    spans = [pl.ds(k * PART, PART) for k in range(weights.shape[0] // PART)]
    copies = copy_all(
        [(inputs_ref, inputs)] + [(w_ref.at[span], weights.at[span]) for span in spans],
        semaphores,
    )
    lanes = lax.broadcasted_iota(jnp.int32, (16, 2 * HD), 1)
    marks = jnp.where(lanes == 0, pos_ref[0], jnp.where(lanes == 1, pos_ref[1], 0))
    for m in range(GROUP):
        pair_refs[m][:ROWS, HD:] = values_ref[:, columns(head ^ m, HD)]
        pair_refs[m][ROWS:] = marks.astype(jnp.float32).astype(jnp.bfloat16)
    copies[0].wait()
    for k, span in enumerate(spans):
        copies[1 + k].wait()
        part = jnp.dot(inputs[:, span], weights[span], preferred_element_type=jnp.float32)
        total[...] = part if k == 0 else total[...] + part
    for m in range(GROUP):
        pair_refs[m][:ROWS, :HD] = total[:, columns(head ^ m, HD)].astype(jnp.bfloat16)


def pack_rows(queries_ref, grads_ref, *out_refs):
    head = own_head()
    for m, out_ref in enumerate(out_refs):
        span = columns(head ^ m, GROUP * HD)
        out_ref[:, : GROUP * HD] = queries_ref[:, span]
        out_ref[:, GROUP * HD :] = grads_ref[:, span]


def pack_weights(w_ref, leaving_ref, semaphore):
    first = (1 - lax.axis_index("tensor")) * 2 + (lax.axis_index("dp") & 1)
    copy = pltpu.make_async_copy(w_ref.at[columns(first, 2 * PART)], leaving_ref, semaphore)
    copy.start()
    copy.wait()


def pack_features(inputs_ref, near_ref, far_ref):
    chip = lax.axis_index("dp") >> 1
    side = lax.axis_index("tensor")
    for m in range(GROUP):
        near_ref[m] = inputs_ref[:, columns(2 * (chip ^ m) + side, 256)]
        far_ref[m] = inputs_ref[:, columns(2 * (chip ^ (m + GROUP)) + side, 256)]


def join_features(near_ref, far_ref, *joined_refs):
    for m, joined_ref in enumerate(joined_refs):
        joined_ref[0] = near_ref[m]
        joined_ref[1] = far_ref[m]


def turn_features(*refs):
    for j in range(2 * GROUP):
        turned = refs[j % GROUP][j // GROUP].astype(jnp.float32).T
        refs[-1][:, j * ROWS : (j + 1) * ROWS] = turned.astype(jnp.bfloat16)


def dot_nt(left, right):
    return lax.dot_general(
        left, right, (((1,), (1,)), ((), ())), preferred_element_type=jnp.float32
    )


def folded(array, reduce):
    return reduce(array.reshape(-1, 8, array.shape[-1]), axis=0)


def first_row_of(positions):
    def first_row(block):
        return pl.multiple_of(positions[block // 2, block % 2] * BLK, BLK)

    return first_row


def attend_rows(
    first_part, first_row, lens_ref, row_refs, dq_refs, keys, keys_t, values, dk, dv, scratch
):
    q_rows, g_rows, dq_all, scores, d_prob = scratch
    score_scale = 1.0 / math.sqrt(HD)
    base_two = score_scale * math.log2(math.e)
    parts = len(row_refs)
    for block in range(2 * parts):
        here = pl.ds(block % 2 * BLK, BLK)
        for h in range(GROUP):
            there = pl.ds(h * BLK, BLK)
            q_rows[block, there] = row_refs[block // 2][here, h * HD : (h + 1) * HD]
            g_rows[block, there] = row_refs[block // 2][
                here, (GROUP + h) * HD : (GROUP + h + 1) * HD
            ]
    starts = [lens_ref[0]]
    for k in (1, 2):
        starts.append(starts[-1] + lens_ref[k])

    def document_start(position):
        found = jnp.zeros_like(position)
        for start in starts:
            found = jnp.where(start <= position, start, found)
        return found

    @pl.loop(0, 2 * parts)
    def _(block):
        first = first_row(2 * first_part + block)
        lanes = lax.broadcasted_iota(jnp.int32, (1, GROUP * BLK), 1)
        position = first + (lanes & (BLK - 1))
        start = document_start(position)
        low = document_start(first) // TILE
        count = (first + BLK - 1) // TILE + 1 - low

        def run(over_tiles):
            query = q_rows[block]
            grad = g_rows[block]
            zeros = jnp.zeros((8, GROUP * BLK), jnp.float32)

            def visit_scores(k, row_max):
                here = columns(low + k, TILE)
                raw = dot_nt(keys[here], query)
                row = (low + k) * TILE + lax.broadcasted_iota(jnp.int32, raw.shape, 0)
                raw = jnp.where((row <= position) & (row >= start), raw, masked_fill)
                scores[k] = raw
                d_prob[k] = dot_nt(values[here], grad)
                return jnp.maximum(row_max, folded(raw, jnp.max))

            row_max = over_tiles(visit_scores, zeros + masked_fill)
            row_max = jnp.max(row_max, axis=0, keepdims=True)

            def visit_sums(k, running):
                terms = jnp.exp2((scores[k] - row_max) * base_two)
                scores[k] = terms
                return (
                    running[0] + folded(terms, jnp.sum),
                    running[1] + folded(terms * d_prob[k], jnp.sum),
                )

            row_sum, weighted = over_tiles(visit_sums, (zeros, zeros))
            inverse = 1.0 / jnp.sum(row_sum, axis=0, keepdims=True)
            delta = jnp.sum(weighted, axis=0, keepdims=True) * inverse

            def visit_grads(k, dq):
                here = columns(low + k, TILE)
                prob = scores[k] * inverse
                score_bf = (prob * (d_prob[k] - delta)).astype(jnp.bfloat16)
                dk[here] += jnp.dot(score_bf, query, preferred_element_type=jnp.float32)
                dv[here] += jnp.dot(
                    prob.astype(jnp.bfloat16), grad, preferred_element_type=jnp.float32
                )
                return dq + jnp.dot(
                    keys_t[:, here], score_bf, preferred_element_type=jnp.float32
                )

            dq = over_tiles(visit_grads, jnp.zeros((HD, GROUP * BLK), jnp.float32))
            dq = (dq * score_scale).T.astype(jnp.bfloat16)
            for h in range(GROUP):
                dq_all[block, :, h * HD : (h + 1) * HD] = dq[h * BLK : (h + 1) * BLK]

        for fixed in range(1, UNROLLED + 1):

            @pl.when(count == fixed)
            def _(fixed=fixed):
                def over_tiles(visit, running):
                    for k in range(fixed):
                        running = visit(k, running)
                    return running

                run(over_tiles)

        @pl.when(count > UNROLLED)
        def _():
            run(lambda visit, running: lax.fori_loop(0, count, visit, running))

    for block in range(2 * parts):
        dq_refs[block // 2][pl.ds(block % 2 * BLK, BLK)] = dq_all[block]


def attend_first(lens_ref, *refs):
    row_refs, refs = refs[: GROUP - 1], refs[GROUP - 1 :]
    own_a, own_b, far_a, far_b, core_pairs, refs = *refs[:5], refs[5:]
    dq_refs, refs = refs[: GROUP - 1], refs[GROUP - 1 :]
    keys, keys_t, values, dk, dv, marks, refs = *refs[:6], refs[6:]
    scratch, (positions, semaphore) = refs[:5], refs[5:]
    reach = 2 * MARKED
    pair_refs = [own_a, own_b]
    pair_refs += [core_pairs.at[pl.ds(k * reach, reach)] for k in range(2)]
    pair_refs += [far_a, far_b]
    pair_refs += [core_pairs.at[pl.ds(k * reach, reach)] for k in range(2, 4)]
    for part in range(4 * GROUP):
        here = pl.ds(part % 2 * MARKED + ROWS, 16)
        row = pair_refs[part // 2][here, :HD].astype(jnp.float32).astype(jnp.int32)
        marks[part : part + 1] = row[:1]
    to_scalars = pltpu.make_async_copy(marks, positions, semaphore)
    to_scalars.start()
    dk[...] = jnp.zeros_like(dk)
    dv[...] = jnp.zeros_like(dv)
    to_scalars.wait()
    first_row = first_row_of(positions)
    for block in range(4 * Q_BLOCKS):
        part = block // 2
        here = pl.ds(part % 2 * MARKED + block % 2 * BLK, BLK)
        there = pl.ds(first_row(block), BLK)
        keys[there] = pair_refs[part // 2][here, :HD]
        values[there] = pair_refs[part // 2][here, HD:]
    for tile in range(keys.shape[0] // TILE):
        here = pl.ds(tile * TILE, TILE)
        keys_t[:, here] = keys[here].astype(jnp.float32).T.astype(jnp.bfloat16)
    attend_rows(
        0, first_row, lens_ref, row_refs, dq_refs, keys, keys_t, values, dk, dv, scratch
    )


def attend_last(lens_ref, row_ref, keys, keys_t, values, dk_first, dv_first, marks, *refs):
    dq_ref, kept, sent, dk, dv, refs = *refs[:5], refs[5:]
    scratch, (positions, semaphore) = refs[:5], refs[5:]
    score_scale = 1.0 / math.sqrt(HD)
    to_scalars = pltpu.make_async_copy(marks, positions, semaphore)
    to_scalars.start()
    dk[...] = dk_first[...]
    dv[...] = dv_first[...]
    to_scalars.wait()
    first_row = first_row_of(positions)
    attend_rows(
        GROUP - 1, first_row, lens_ref, [row_ref], [dq_ref], keys, keys_t, values, dk, dv, scratch
    )
    for block in range(4 * Q_BLOCKS):
        quarter = block // Q_BLOCKS
        here = pl.ds(quarter // 2 * Q_BLOCKS * BLK + block % Q_BLOCKS * BLK, BLK)
        there = pl.ds(first_row(block), BLK)
        out_ref = sent if quarter % 2 else kept
        out_ref[here, :HD] = dk[there] * score_scale
        out_ref[here, HD:] = dv[there]


def weight_grad(own_ref, other_ref, *refs):
    grad_refs, (keep_ref, send_ref, grads) = refs[:GROUP], refs[GROUP:]
    head = own_head()
    for k, grad_ref in enumerate(grad_refs):
        for far in range(2):
            for m in range(GROUP):
                here = pl.ds((far * GROUP + m) * ROWS, ROWS)
                there = pl.ds((far * GROUP + (m ^ k)) * ROWS, ROWS)
                grads[here, columns(head ^ k, HD)] = grad_ref[there]
    own = jnp.dot(own_ref[...], grads[...], preferred_element_type=jnp.float32)
    other = jnp.dot(other_ref[...], grads[...], preferred_element_type=jnp.float32)
    crossed = (lax.axis_index("dp") & 1) ^ lax.axis_index("tensor")

    @pl.when(crossed == 0)
    def _():
        keep_ref[...] = own
        send_ref[...] = other

    @pl.when(crossed == 1)
    def _():
        keep_ref[...] = other
        send_ref[...] = own


def input_grad(own_ref, other_ref, w_own, w_near, w_far, out_ref, own_all, other_all):
    head = own_head()
    core = lax.axis_index("dp") & 1
    side = lax.axis_index("tensor")
    for k in range(GROUP):
        own_all[:, columns(head ^ k, HD)] = own_ref[k]
        other_all[:, columns(head ^ k, HD)] = other_ref[k]
    for k in range(4):
        chunk = 2 * (core ^ (k // 2)) + k % 2
        w_other = (w_near, w_far)[k // 2][pl.ds(k % 2 * PART, PART)]
        part = dot_nt(own_all[...], w_own[columns(side * 4 + chunk, PART)])
        part = part + dot_nt(other_all[...], w_other)
        out_ref[:, columns(chunk, PART)] = part.astype(jnp.bfloat16)


def pack_grads(value_ref, row_ref, *refs):
    for m, out_ref in enumerate(refs):
        out_ref[:, :HD] = value_ref[m * ROWS : (m + 1) * ROWS]
    refs[-1][:, HD:] = row_ref[...]


def finish(keep_ref, arrived_ref, *refs):
    row_refs, grad_refs, refs = refs[: GROUP - 1], refs[GROUP - 1 : 2 * GROUP - 1], refs[2 * GROUP - 1 :]
    weight_out, query_out, value_out = refs
    head = own_head()
    weight_out[...] = keep_ref[...] + arrived_ref[...]
    for m in range(GROUP):
        row = row_refs[m][...] if m < GROUP - 1 else grad_refs[m][:, HD:]
        query_out[:, columns(head ^ m, GROUP * HD)] = row
        value_out[:, columns(head ^ m, HD)] = grad_refs[m][:, :HD]


def shaped(shape, dtype=jnp.bfloat16):
    return jax.ShapeDtypeStruct(shape, dtype)


def limits(mebibytes):
    return pltpu.CompilerParams(vmem_limit_bytes=mebibytes << 20)


def with_partners(arrays):
    return [arrays[0]] + [swap(arrays[m], 2 * m) for m in range(1, len(arrays))]


def on_device_by_heads(inputs, w_key, values, queries, d_out, doc_lens, block_pos):
    features = inputs.shape[1]
    kv_columns = values.shape[1]
    total_rows = 16 * ROWS
    half, quarter = total_rows // 2, total_rows // 4
    vmem, smem, hbm = whole_spec(), whole_spec(SMEM), whole_spec(HBM)

    pairs = pl.pallas_call(
        project_keys,
        out_shape=[shaped((MARKED, 2 * HD))] * GROUP,
        in_specs=[smem, hbm, vmem, hbm],
        out_specs=[vmem] * GROUP,
        scratch_shapes=[
            VMEM((ROWS, features), jnp.bfloat16),
            VMEM((features, kv_columns), jnp.bfloat16),
            VMEM((ROWS, kv_columns), jnp.float32),
            DMA((1 + features // PART,)),
        ],
        compiler_params=limits(60),
        cost_estimate=pl.CostEstimate(
            flops=2 * ROWS * features * kv_columns,
            bytes_accessed=features * kv_columns * 2,
            transcendentals=0,
        ),
        name="project_keys",
    )(block_pos, inputs, values, w_key)

    packed_rows = pl.pallas_call(
        pack_rows,
        out_shape=[shaped((ROWS, 2 * GROUP * HD))] * GROUP,
        in_specs=[vmem] * 2,
        out_specs=[vmem] * GROUP,
        compiler_params=limits(8),
        name="pack_rows",
    )(after(queries, pairs[0]), d_out)

    pairs = [after(pairs[0], packed_rows[0])] + list(pairs[1:])
    pairs = with_partners(pairs)
    own_a = jnp.concatenate(pairs[:2], axis=0)
    own_b = jnp.concatenate(pairs[2:], axis=0)
    far_a = swap(own_a, Z_HI)
    far_b = swap(own_b, Z_HI)
    rows = with_partners(packed_rows)

    near_features, far_features = pl.pallas_call(
        pack_features,
        out_shape=[shaped((GROUP, ROWS, 256))] * 2,
        in_specs=[vmem],
        out_specs=[vmem] * 2,
        compiler_params=limits(8),
        name="pack_features",
    )(after(inputs, own_a))
    leaving = pl.pallas_call(
        pack_weights,
        out_shape=shaped((2 * PART, kv_columns)),
        in_specs=[hbm],
        out_specs=vmem,
        scratch_shapes=[DMA],
        compiler_params=limits(56),
        name="pack_weights",
    )(after(w_key, own_b))
    w_near = swap_tensor(leaving)
    near_pairs = jnp.concatenate([own_a, own_b, far_a, far_b], axis=0)
    core_pairs = swap(after(near_pairs, near_features, leaving, rows[1], rows[2]), CORE)
    far_features = swap(far_features, Z_HI)

    row_grad = shaped((ROWS, GROUP * HD))
    sorted_rows = shaped((total_rows, HD))
    sums = shaped((total_rows, HD), jnp.float32)
    half_sums = shaped((half, 2 * HD), jnp.float32)

    def attend_scratch(blocks):
        stacked = VMEM((blocks, GROUP * BLK, HD), jnp.bfloat16)
        tiles = VMEM((total_rows // TILE, TILE, GROUP * BLK), jnp.float32)
        return [
            stacked,
            stacked,
            VMEM((blocks, BLK, GROUP * HD), jnp.bfloat16),
            tiles,
            tiles,
            SMEM((4 * GROUP, HD), jnp.int32),
            DMA,
        ]

    *row_grads, keys, keys_t, all_values, dk_first, dv_first, marks = pl.pallas_call(
        attend_first,
        out_shape=[row_grad] * (GROUP - 1)
        + [sorted_rows, shaped((HD, total_rows)), sorted_rows, sums, sums]
        + [shaped((4 * GROUP, HD), jnp.int32)],
        in_specs=[smem] + [vmem] * (GROUP + 4),
        out_specs=[vmem] * (GROUP + 5),
        scratch_shapes=attend_scratch(Q_BLOCKS - 2),
        compiler_params=limits(20),
        cost_estimate=pl.CostEstimate(flops=ATTEND_COST, bytes_accessed=0, transcendentals=0),
        name="attend_first",
    )(doc_lens, *rows[:-1], own_a, own_b, far_a, far_b, core_pairs)
    last_grad, kept, sent = pl.pallas_call(
        attend_last,
        out_shape=[row_grad, half_sums, half_sums],
        in_specs=[smem] + [vmem] * 7,
        out_specs=[vmem] * 3,
        scratch_shapes=[VMEM((total_rows, HD), jnp.float32)] * 2 + attend_scratch(2),
        compiler_params=limits(20),
        cost_estimate=pl.CostEstimate(flops=ATTEND_COST, bytes_accessed=0, transcendentals=0),
        name="attend_last",
    )(doc_lens, after(rows[-1], w_near), keys, keys_t, all_values, dk_first, dv_first, marks)

    row_grads = with_partners(row_grads)
    sent = after(sent, far_features, *row_grads)
    grads = kept + swap(sent, CORE)
    dk_sum, dv_sum = grads[:, :HD], grads[:, HD:]
    dk_far = swap(dk_sum.astype(jnp.bfloat16), Z_HI)
    w_far = swap(after(w_near, dk_sum), CORE)

    feature_parts = pl.pallas_call(
        join_features,
        out_shape=[shaped((2, ROWS, 256))] * GROUP,
        in_specs=[vmem] * 2,
        out_specs=[vmem] * GROUP,
        compiler_params=limits(16),
        name="join_features",
    )(after(near_features, sent), far_features)
    own_features = pl.pallas_call(
        turn_features,
        out_shape=shaped((256, half)),
        in_specs=[vmem] * GROUP,
        out_specs=vmem,
        compiler_params=limits(16),
        cost_estimate=pl.CostEstimate(flops=4_000_000_000, bytes_accessed=0, transcendentals=0),
        name="turn_features",
    )(*with_partners(feature_parts))
    other_features = swap_tensor(own_features)

    dk_far = jnp.concatenate([dk_far[quarter:], dk_far[:quarter]], axis=0)
    key_grad = (dk_sum + dk_far.astype(jnp.float32)).astype(jnp.bfloat16)
    key_grad = after(key_grad, own_features, w_far)
    key_grads = with_partners([key_grad] * GROUP)
    own_key_grad = jnp.stack([key_grads[m][m * ROWS : (m + 1) * ROWS] for m in range(GROUP)])
    other_key_grad = swap_tensor(own_key_grad)

    dv_far = swap(after(dv_sum[quarter:].astype(jnp.bfloat16), key_grad), Z_HI)
    value_grad = (dv_sum[:quarter] + dv_far.astype(jnp.float32)).astype(jnp.bfloat16)
    packed_grads = pl.pallas_call(
        pack_grads,
        out_shape=[shaped((ROWS, HD))] * (GROUP - 1) + [shaped((ROWS, (GROUP + 1) * HD))],
        in_specs=[vmem] * 2,
        out_specs=[vmem] * GROUP,
        compiler_params=limits(16),
        name="pack_grads",
    )(value_grad, last_grad)
    packed_grads = [after(packed_grads[0], own_key_grad)] + [
        after(grad, own_key_grad) for grad in packed_grads[1:]
    ]

    keep, send = pl.pallas_call(
        weight_grad,
        out_shape=[shaped((256, kv_columns), jnp.float32)] * 2,
        in_specs=[vmem] * (2 + GROUP),
        out_specs=[vmem] * 2,
        scratch_shapes=[VMEM((half, kv_columns), jnp.bfloat16)],
        compiler_params=limits(24),
        cost_estimate=pl.CostEstimate(
            flops=4 * 256 * half * kv_columns, bytes_accessed=4 << 20, transcendentals=0
        ),
        name="weight_grad",
    )(own_features, other_features, *key_grads)
    arrived = swap(send, CORE)

    d_input = pl.pallas_call(
        input_grad,
        out_shape=shaped((ROWS, features // 2)),
        in_specs=[vmem] * 5,
        out_specs=vmem,
        scratch_shapes=[VMEM((ROWS, kv_columns), jnp.bfloat16)] * 2,
        compiler_params=limits(16),
        cost_estimate=pl.CostEstimate(
            flops=4 * ROWS * 2048 * kv_columns, bytes_accessed=5 << 20, transcendentals=0
        ),
        name="input_grad",
    )(after(own_key_grad, send), other_key_grad, w_key, w_near, w_far)

    d_wkey, d_query, d_value = pl.pallas_call(
        finish,
        out_shape=[
            shaped((256, kv_columns), jnp.float32),
            shaped(queries.shape),
            shaped(values.shape),
        ],
        in_specs=[vmem] * (1 + 2 * GROUP),
        out_specs=[vmem] * 3,
        compiler_params=limits(16),
        name="finish",
    )(keep, arrived, *row_grads, *with_partners(packed_grads))
    return (d_query, d_value, d_input, d_wkey)


def solution(mesh):
    by_heads = mesh.shape["dp"] == 16 and mesh.shape["tensor"] == 2
    return jax.shard_map(
        on_device_by_heads if by_heads else on_device,
        mesh=mesh,
        in_specs=(
            P("dp", None),
            P(None, "tensor"),
            P("dp", "tensor"),
            P("dp", "tensor"),
            P("dp", "tensor"),
            P(),
            P("dp"),
        ),
        out_specs=(P("dp", "tensor"), P("dp", "tensor"), P("dp", "tensor"), P("dp", "tensor")),
        check_vma=False,
    )
```

```python
import math

import jax
import jax.numpy as jnp
from jax import lax
from jax.experimental import pallas as pl
from jax.experimental.pallas import tpu as pltpu
from jax.sharding import PartitionSpec as P

HD = 128
BLK = 64


masked_fill = -1e30


def row_positions(block_pos):
    within = jnp.tile(jnp.arange(BLK, dtype=jnp.int32), block_pos.shape[0])
    return jnp.repeat(block_pos, BLK) * BLK + within


def documents(positions, doc_lens):
    starts = jnp.cumsum(doc_lens) - doc_lens
    return jnp.sum((positions[:, None] >= starts[None, :]).astype(jnp.int32), axis=1) - 1


def split_heads(block_rows, kv_heads):
    return block_rows.reshape(block_rows.shape[0], kv_heads, HD)


def scored(query_heads, key_block, score_scale):
    key_split = split_heads(key_block, query_heads.shape[1])
    return (
        jnp.einsum("qcgd,kcd->cgqk", query_heads, key_split, preferred_element_type=jnp.float32)
        * score_scale
    )


def contributions(
    query_heads, grad_heads, key_block, value_block, allowed, row_max, row_sum, delta, score_scale
):
    kv_heads = query_heads.shape[1]
    key_split = split_heads(key_block, kv_heads)
    value_split = split_heads(value_block, kv_heads)
    scores = scored(query_heads, key_block, score_scale)
    mask_full = allowed[None, None]
    probabilities = (
        jnp.where(mask_full, jnp.exp(scores - row_max[..., None]), 0.0) / row_sum[..., None]
    )
    d_prob = jnp.einsum(
        "qcgd,kcd->cgqk", grad_heads, value_split, preferred_element_type=jnp.float32
    )
    d_score = probabilities * (d_prob - delta[..., None])
    prob_bf = probabilities.astype(jnp.bfloat16)
    score_bf = d_score.astype(jnp.bfloat16)
    query_part = score_scale * jnp.einsum(
        "cgqk,kcd->qcgd", score_bf, key_split, preferred_element_type=jnp.float32
    )
    key_part = score_scale * jnp.einsum(
        "cgqk,qcgd->kcd", score_bf, query_heads, preferred_element_type=jnp.float32
    )
    value_part = jnp.einsum(
        "cgqk,qcgd->kcd", prob_bf, grad_heads, preferred_element_type=jnp.float32
    )
    width_rows = key_block.shape[0]
    partial_value = jnp.concatenate(
        [key_part.reshape(width_rows, -1), value_part.reshape(width_rows, -1)], axis=1
    )
    return (query_part, partial_value)


def on_device(inputs, w_key, values, queries, d_out, doc_lens, block_pos):
    local_rows = inputs.shape[0]
    kv_heads = values.shape[1] // HD
    group_size = queries.shape[1] // (kv_heads * HD)
    kv_columns = kv_heads * HD
    score_scale = 1.0 / math.sqrt(HD)
    key_rows = jnp.dot(inputs, w_key, preferred_element_type=jnp.float32).astype(jnp.bfloat16)
    all_keys, all_values, all_blocks = (
        lax.all_gather(key_rows, "dp", axis=0, tiled=True),
        lax.all_gather(values, "dp", axis=0, tiled=True),
        lax.all_gather(block_pos, "dp", axis=0, tiled=True),
    )
    key_pos = row_positions(all_blocks)
    key_doc = documents(key_pos, doc_lens)
    query_pos = row_positions(block_pos)
    query_doc = documents(query_pos, doc_lens)
    query_heads = queries.reshape(local_rows, kv_heads, group_size, HD)
    grad_heads = d_out.reshape(local_rows, kv_heads, group_size, HD)
    total_rows = all_keys.shape[0]
    key_width = math.gcd(512, total_rows)
    stat_shape = (kv_heads, group_size, local_rows)

    def mask_for(first_row, width_rows):
        pos_here = lax.dynamic_slice_in_dim(key_pos, first_row, width_rows, 0)
        doc_here = lax.dynamic_slice_in_dim(key_doc, first_row, width_rows, 0)
        return (query_doc[:, None] == doc_here[None, :]) & (pos_here[None, :] <= query_pos[:, None])

    def visit_stats(block_index, running):
        first_row = block_index * key_width
        key_block = lax.dynamic_slice_in_dim(all_keys, first_row, key_width, 0)
        value_block = lax.dynamic_slice_in_dim(all_values, first_row, key_width, 0)
        allowed = mask_for(first_row, key_width)

        def visit_compute_live(state_now):
            row_max, row_sum, weighted = state_now
            scores = scored(query_heads, key_block, score_scale)
            mask_full = allowed[None, None]
            new_max = jnp.maximum(
                row_max, jnp.max(jnp.where(mask_full, scores, masked_fill), axis=3)
            )
            exp_terms = jnp.where(mask_full, jnp.exp(scores - new_max[..., None]), 0.0)
            d_prob = jnp.einsum(
                "qcgd,kcd->cgqk",
                grad_heads,
                split_heads(value_block, kv_heads),
                preferred_element_type=jnp.float32,
            )
            shrink = jnp.exp(row_max - new_max)
            return (
                new_max,
                row_sum * shrink + jnp.sum(exp_terms, axis=3),
                weighted * shrink + jnp.sum(exp_terms * d_prob, axis=3),
            )

        return lax.cond(jnp.any(allowed), visit_compute_live, lambda state_now: state_now, running)

    start_state = (
        jnp.full(stat_shape, masked_fill, jnp.float32),
        jnp.zeros(stat_shape, jnp.float32),
        jnp.zeros(stat_shape, jnp.float32),
    )
    row_max, row_sum, weighted = lax.fori_loop(0, total_rows // key_width, visit_stats, start_state)
    delta = weighted / row_sum

    def block_work(key_block, value_block, allowed):
        width_rows = key_block.shape[0]

        def block_compute_live(operands):
            return contributions(
                query_heads,
                grad_heads,
                operands[0],
                operands[1],
                operands[2],
                row_max,
                row_sum,
                delta,
                score_scale,
            )

        def dead_block(operands):
            return (
                jnp.zeros((local_rows, kv_heads, group_size, HD), jnp.float32),
                jnp.zeros((width_rows, 2 * kv_columns), jnp.float32),
            )

        return lax.cond(
            jnp.any(allowed), block_compute_live, dead_block, (key_block, value_block, allowed)
        )

    query_start = jnp.zeros((local_rows, kv_heads, group_size, HD), jnp.float32)

    def visit_block(block_index, running):
        query_sum, buffer_rows = running
        first_row = block_index * key_width
        key_block = lax.dynamic_slice_in_dim(all_keys, first_row, key_width, 0)
        value_block = lax.dynamic_slice_in_dim(all_values, first_row, key_width, 0)
        query_part, partial_value = block_work(
            key_block, value_block, mask_for(first_row, key_width)
        )
        return (
            query_sum + query_part,
            lax.dynamic_update_slice_in_dim(buffer_rows, partial_value, first_row, 0),
        )

    empty_buffer = jnp.zeros((total_rows, 2 * kv_columns), jnp.float32)
    query_sum, buffer_rows = lax.fori_loop(
        0, total_rows // key_width, visit_block, (query_start, empty_buffer)
    )
    arrived = lax.all_to_all(
        buffer_rows.astype(jnp.bfloat16), "dp", split_axis=0, concat_axis=0, tiled=True
    ).astype(buffer_rows.dtype)
    own_sums = jnp.sum(arrived.reshape(-1, local_rows, 2 * kv_columns), axis=0)
    d_query = query_sum.astype(jnp.bfloat16).reshape(local_rows, kv_columns * group_size)
    key_grad = own_sums[:, :kv_columns].astype(jnp.bfloat16)
    d_value = own_sums[:, kv_columns:].astype(jnp.bfloat16)
    d_wkey = lax.psum_scatter(
        lax.dot_general(
            inputs, key_grad, (((0,), (0,)), ((), ())), preferred_element_type=jnp.float32
        ),
        "dp",
        scatter_dimension=0,
        tiled=True,
    )
    partial_input = lax.dot_general(
        key_grad, w_key, (((1,), (1,)), ((), ())), preferred_element_type=jnp.float32
    )
    d_input = lax.psum_scatter(
        partial_input.astype(jnp.bfloat16), "tensor", scatter_dimension=1, tiled=True
    )
    return (d_query, d_value, d_input, d_wkey)


CORE, Z_HI = 1, 8
GROUP = 4
ROWS = 128
TILE = 256
UNROLLED = 5
ATTEND_COST = 4_000_000_000
PART = 512
MARKED = ROWS + 16
Q_BLOCKS = GROUP * ROWS // BLK
SMEM = pltpu.SMEM
VMEM = pltpu.VMEM
HBM = pltpu.HBM
DMA = pltpu.SemaphoreType.DMA


def swap(array, mask):
    return lax.ppermute(array, "dp", [(i, i ^ mask) for i in range(16)])


def swap_tensor(array):
    return lax.ppermute(array, "tensor", [(0, 1), (1, 0)])


def own_head():
    return (lax.axis_index("dp") >> 1) & 3


def columns(index, width):
    return pl.ds(pl.multiple_of(index * width, width), width)


def whole_spec(space=VMEM):
    return pl.BlockSpec(memory_space=space)


def after(array, *earlier):
    return lax.optimization_barrier((array,) + earlier)[0]


def copy_all(pairs, semaphores):
    copies = [
        pltpu.make_async_copy(source, target, semaphores.at[i])
        for i, (source, target) in enumerate(pairs)
    ]
    for copy in copies:
        copy.start()
    return copies


def project_keys(pos_ref, inputs_ref, values_ref, w_ref, *refs):
    pair_refs = refs[:GROUP]
    inputs, weights, total, semaphores = refs[GROUP:]
    head = own_head()
    spans = [pl.ds(k * PART, PART) for k in range(weights.shape[0] // PART)]
    copies = copy_all(
        [(inputs_ref, inputs)] + [(w_ref.at[span], weights.at[span]) for span in spans],
        semaphores,
    )
    lanes = lax.broadcasted_iota(jnp.int32, (16, 2 * HD), 1)
    marks = jnp.where(lanes == 0, pos_ref[0], jnp.where(lanes == 1, pos_ref[1], 0))
    for m in range(GROUP):
        pair_refs[m][:ROWS, HD:] = values_ref[:, columns(head ^ m, HD)]
        pair_refs[m][ROWS:] = marks.astype(jnp.float32).astype(jnp.bfloat16)
    copies[0].wait()
    for k, span in enumerate(spans):
        copies[1 + k].wait()
        part = jnp.dot(inputs[:, span], weights[span], preferred_element_type=jnp.float32)
        total[...] = part if k == 0 else total[...] + part
    for m in range(GROUP):
        pair_refs[m][:ROWS, :HD] = total[:, columns(head ^ m, HD)].astype(jnp.bfloat16)


def pack_rows(queries_ref, grads_ref, *out_refs):
    head = own_head()
    for m, out_ref in enumerate(out_refs):
        span = columns(head ^ m, GROUP * HD)
        out_ref[:, : GROUP * HD] = queries_ref[:, span]
        out_ref[:, GROUP * HD :] = grads_ref[:, span]


def pack_weights(w_ref, leaving_ref, semaphore):
    first = (1 - lax.axis_index("tensor")) * 2 + (lax.axis_index("dp") & 1)
    copy = pltpu.make_async_copy(w_ref.at[columns(first, 2 * PART)], leaving_ref, semaphore)
    copy.start()
    copy.wait()


def pack_features(inputs_ref, near_ref, far_ref):
    chip = lax.axis_index("dp") >> 1
    side = lax.axis_index("tensor")
    for m in range(GROUP):
        near_ref[m] = inputs_ref[:, columns(2 * (chip ^ m) + side, 256)]
        far_ref[m] = inputs_ref[:, columns(2 * (chip ^ (m + GROUP)) + side, 256)]


def join_features(near_ref, far_ref, *joined_refs):
    for m, joined_ref in enumerate(joined_refs):
        joined_ref[0] = near_ref[m]
        joined_ref[1] = far_ref[m]


def turn_features(*refs):
    for j in range(2 * GROUP):
        turned = refs[j % GROUP][j // GROUP].astype(jnp.float32).T
        refs[-1][:, j * ROWS : (j + 1) * ROWS] = turned.astype(jnp.bfloat16)


def dot_nt(left, right):
    return lax.dot_general(
        left, right, (((1,), (1,)), ((), ())), preferred_element_type=jnp.float32
    )


def folded(array, reduce):
    return reduce(array.reshape(-1, 8, array.shape[-1]), axis=0)


def first_row_of(positions):
    def first_row(block):
        return pl.multiple_of(positions[block // 2, block % 2] * BLK, BLK)

    return first_row


def attend_rows(
    first_part, first_row, lens_ref, row_refs, dq_refs, keys, keys_t, values, dk, dv, scratch
):
    q_rows, g_rows, dq_all, scores, d_prob = scratch
    score_scale = 1.0 / math.sqrt(HD)
    base_two = score_scale * math.log2(math.e)
    parts = len(row_refs)
    for block in range(2 * parts):
        here = pl.ds(block % 2 * BLK, BLK)
        for h in range(GROUP):
            there = pl.ds(h * BLK, BLK)
            q_rows[block, there] = row_refs[block // 2][here, h * HD : (h + 1) * HD]
            g_rows[block, there] = row_refs[block // 2][
                here, (GROUP + h) * HD : (GROUP + h + 1) * HD
            ]
    starts = [lens_ref[0]]
    for k in (1, 2):
        starts.append(starts[-1] + lens_ref[k])

    def document_start(position):
        found = jnp.zeros_like(position)
        for start in starts:
            found = jnp.where(start <= position, start, found)
        return found

    @pl.loop(0, 2 * parts)
    def _(block):
        first = first_row(2 * first_part + block)
        lanes = lax.broadcasted_iota(jnp.int32, (1, GROUP * BLK), 1)
        position = first + (lanes & (BLK - 1))
        start = document_start(position)
        low = document_start(first) // TILE
        count = (first + BLK - 1) // TILE + 1 - low

        def run(over_tiles):
            query = q_rows[block]
            grad = g_rows[block]
            zeros = jnp.zeros((8, GROUP * BLK), jnp.float32)

            def visit_scores(k, row_max):
                here = columns(low + k, TILE)
                raw = dot_nt(keys[here], query)
                row = (low + k) * TILE + lax.broadcasted_iota(jnp.int32, raw.shape, 0)
                raw = jnp.where((row <= position) & (row >= start), raw, masked_fill)
                scores[k] = raw
                d_prob[k] = dot_nt(values[here], grad)
                return jnp.maximum(row_max, folded(raw, jnp.max))

            row_max = over_tiles(visit_scores, zeros + masked_fill)
            row_max = jnp.max(row_max, axis=0, keepdims=True)

            def visit_sums(k, running):
                terms = jnp.exp2((scores[k] - row_max) * base_two)
                scores[k] = terms
                return (
                    running[0] + folded(terms, jnp.sum),
                    running[1] + folded(terms * d_prob[k], jnp.sum),
                )

            row_sum, weighted = over_tiles(visit_sums, (zeros, zeros))
            inverse = 1.0 / jnp.sum(row_sum, axis=0, keepdims=True)
            delta = jnp.sum(weighted, axis=0, keepdims=True) * inverse

            def visit_grads(k, dq):
                here = columns(low + k, TILE)
                prob = scores[k] * inverse
                score_bf = (prob * (d_prob[k] - delta)).astype(jnp.bfloat16)
                dk[here] += jnp.dot(score_bf, query, preferred_element_type=jnp.float32)
                dv[here] += jnp.dot(
                    prob.astype(jnp.bfloat16), grad, preferred_element_type=jnp.float32
                )
                return dq + jnp.dot(
                    keys_t[:, here], score_bf, preferred_element_type=jnp.float32
                )

            dq = over_tiles(visit_grads, jnp.zeros((HD, GROUP * BLK), jnp.float32))
            dq = (dq * score_scale).T.astype(jnp.bfloat16)
            for h in range(GROUP):
                dq_all[block, :, h * HD : (h + 1) * HD] = dq[h * BLK : (h + 1) * BLK]

        for fixed in range(1, UNROLLED + 1):

            @pl.when(count == fixed)
            def _(fixed=fixed):
                def over_tiles(visit, running):
                    for k in range(fixed):
                        running = visit(k, running)
                    return running

                run(over_tiles)

        @pl.when(count > UNROLLED)
        def _():
            run(lambda visit, running: lax.fori_loop(0, count, visit, running))

    for block in range(2 * parts):
        dq_refs[block // 2][pl.ds(block % 2 * BLK, BLK)] = dq_all[block]


def attend_first(lens_ref, *refs):
    row_refs, refs = refs[: GROUP - 1], refs[GROUP - 1 :]
    own_a, own_b, far_a, far_b, core_pairs, refs = *refs[:5], refs[5:]
    dq_refs, refs = refs[: GROUP - 1], refs[GROUP - 1 :]
    keys, keys_t, values, dk, dv, marks, refs = *refs[:6], refs[6:]
    scratch, (positions, semaphore) = refs[:5], refs[5:]
    reach = 2 * MARKED
    pair_refs = [own_a, own_b]
    pair_refs += [core_pairs.at[pl.ds(k * reach, reach)] for k in range(2)]
    pair_refs += [far_a, far_b]
    pair_refs += [core_pairs.at[pl.ds(k * reach, reach)] for k in range(2, 4)]
    for part in range(4 * GROUP):
        here = pl.ds(part % 2 * MARKED + ROWS, 16)
        row = pair_refs[part // 2][here, :HD].astype(jnp.float32).astype(jnp.int32)
        marks[part : part + 1] = row[:1]
    to_scalars = pltpu.make_async_copy(marks, positions, semaphore)
    to_scalars.start()
    dk[...] = jnp.zeros_like(dk)
    dv[...] = jnp.zeros_like(dv)
    to_scalars.wait()
    first_row = first_row_of(positions)
    for block in range(4 * Q_BLOCKS):
        part = block // 2
        here = pl.ds(part % 2 * MARKED + block % 2 * BLK, BLK)
        there = pl.ds(first_row(block), BLK)
        keys[there] = pair_refs[part // 2][here, :HD]
        values[there] = pair_refs[part // 2][here, HD:]
    for tile in range(keys.shape[0] // TILE):
        here = pl.ds(tile * TILE, TILE)
        keys_t[:, here] = keys[here].astype(jnp.float32).T.astype(jnp.bfloat16)
    attend_rows(
        0, first_row, lens_ref, row_refs, dq_refs, keys, keys_t, values, dk, dv, scratch
    )


def attend_last(lens_ref, row_ref, keys, keys_t, values, dk_first, dv_first, marks, *refs):
    dq_ref, kept, sent, dk, dv, refs = *refs[:5], refs[5:]
    scratch, (positions, semaphore) = refs[:5], refs[5:]
    score_scale = 1.0 / math.sqrt(HD)
    to_scalars = pltpu.make_async_copy(marks, positions, semaphore)
    to_scalars.start()
    dk[...] = dk_first[...]
    dv[...] = dv_first[...]
    to_scalars.wait()
    first_row = first_row_of(positions)
    attend_rows(
        GROUP - 1, first_row, lens_ref, [row_ref], [dq_ref], keys, keys_t, values, dk, dv, scratch
    )
    for block in range(4 * Q_BLOCKS):
        quarter = block // Q_BLOCKS
        here = pl.ds(quarter // 2 * Q_BLOCKS * BLK + block % Q_BLOCKS * BLK, BLK)
        there = pl.ds(first_row(block), BLK)
        out_ref = sent if quarter % 2 else kept
        out_ref[here, :HD] = dk[there] * score_scale
        out_ref[here, HD:] = dv[there]


def weight_grad(own_ref, other_ref, *refs):
    near_refs, far_refs = refs[:GROUP], refs[GROUP : 2 * GROUP]
    keep_ref, send_ref, grads = refs[2 * GROUP :]
    head = own_head()
    for k in range(GROUP):
        for far, grad_ref in enumerate((near_refs[k], far_refs[k])):
            for m in range(GROUP):
                here = pl.ds((far * GROUP + m) * ROWS, ROWS)
                grads[here, columns(head ^ k, HD)] = grad_ref[pl.ds((m ^ k) * ROWS, ROWS)]
    own = jnp.dot(own_ref[...], grads[...], preferred_element_type=jnp.float32)
    other = jnp.dot(other_ref[...], grads[...], preferred_element_type=jnp.float32)
    crossed = (lax.axis_index("dp") & 1) ^ lax.axis_index("tensor")

    @pl.when(crossed == 0)
    def _():
        keep_ref[...] = own
        send_ref[...] = other

    @pl.when(crossed == 1)
    def _():
        keep_ref[...] = other
        send_ref[...] = own


def input_grad(own_ref, other_ref, w_own, w_near, w_far, out_ref, own_all, other_all):
    head = own_head()
    core = lax.axis_index("dp") & 1
    side = lax.axis_index("tensor")
    for k in range(GROUP):
        own_all[:, columns(head ^ k, HD)] = own_ref[k]
        other_all[:, columns(head ^ k, HD)] = other_ref[k]
    for k in range(4):
        chunk = 2 * (core ^ (k // 2)) + k % 2
        w_other = (w_near, w_far)[k // 2][pl.ds(k % 2 * PART, PART)]
        part = dot_nt(own_all[...], w_own[columns(side * 4 + chunk, PART)])
        part = part + dot_nt(other_all[...], w_other)
        out_ref[:, columns(chunk, PART)] = part.astype(jnp.bfloat16)


def place_rows(*refs):
    for m, ref in enumerate(refs[:GROUP]):
        refs[GROUP][:, columns(own_head() ^ m, GROUP * HD)] = ref[...]


def finish(keep_ref, arrived_ref, *refs):
    value_refs, (weight_out, value_out) = refs[:GROUP], refs[GROUP:]
    weight_out[...] = keep_ref[...] + arrived_ref[...]
    for m in range(GROUP):
        value_out[:, columns(own_head() ^ m, HD)] = value_refs[m][...]


def shaped(shape, dtype=jnp.bfloat16):
    return jax.ShapeDtypeStruct(shape, dtype)


def limits(mebibytes):
    return pltpu.CompilerParams(vmem_limit_bytes=mebibytes << 20)


def with_partners(arrays):
    return [arrays[0]] + [swap(arrays[m], 2 * m) for m in range(1, len(arrays))]


def on_device_by_heads(inputs, w_key, values, queries, d_out, doc_lens, block_pos):
    features = inputs.shape[1]
    kv_columns = values.shape[1]
    total_rows = 16 * ROWS
    half, quarter = total_rows // 2, total_rows // 4
    vmem, smem, hbm = whole_spec(), whole_spec(SMEM), whole_spec(HBM)

    pairs = pl.pallas_call(
        project_keys,
        out_shape=[shaped((MARKED, 2 * HD))] * GROUP,
        in_specs=[smem, hbm, vmem, hbm],
        out_specs=[vmem] * GROUP,
        scratch_shapes=[
            VMEM((ROWS, features), jnp.bfloat16),
            VMEM((features, kv_columns), jnp.bfloat16),
            VMEM((ROWS, kv_columns), jnp.float32),
            DMA((1 + features // PART,)),
        ],
        compiler_params=limits(60),
        cost_estimate=pl.CostEstimate(
            flops=2 * ROWS * features * kv_columns,
            bytes_accessed=features * kv_columns * 2,
            transcendentals=0,
        ),
        name="project_keys",
    )(block_pos, inputs, values, w_key)

    packed_rows = pl.pallas_call(
        pack_rows,
        out_shape=[shaped((ROWS, 2 * GROUP * HD))] * GROUP,
        in_specs=[vmem] * 2,
        out_specs=[vmem] * GROUP,
        compiler_params=limits(8),
        name="pack_rows",
    )(after(queries, pairs[0]), d_out)

    pairs = [after(pairs[0], packed_rows[0])] + list(pairs[1:])
    pairs = with_partners(pairs)
    own_a = jnp.concatenate(pairs[:2], axis=0)
    own_b = jnp.concatenate(pairs[2:], axis=0)
    far_a = swap(own_a, Z_HI)
    far_b = swap(own_b, Z_HI)
    rows = with_partners(packed_rows)

    near_features, far_features = pl.pallas_call(
        pack_features,
        out_shape=[shaped((GROUP, ROWS, 256))] * 2,
        in_specs=[vmem],
        out_specs=[vmem] * 2,
        compiler_params=limits(8),
        name="pack_features",
    )(after(inputs, own_a))
    leaving = pl.pallas_call(
        pack_weights,
        out_shape=shaped((2 * PART, kv_columns)),
        in_specs=[hbm],
        out_specs=vmem,
        scratch_shapes=[DMA],
        compiler_params=limits(56),
        name="pack_weights",
    )(after(w_key, own_b))
    w_near = swap_tensor(leaving)
    near_pairs = jnp.concatenate([own_a, own_b, far_a, far_b], axis=0)
    core_pairs = swap(after(near_pairs, near_features, leaving, rows[1], rows[2]), CORE)
    far_features = swap(far_features, Z_HI)

    row_grad = shaped((ROWS, GROUP * HD))
    sorted_rows = shaped((total_rows, HD))
    sums = shaped((total_rows, HD), jnp.float32)
    half_sums = shaped((half, 2 * HD), jnp.float32)

    def attend_scratch(blocks):
        stacked = VMEM((blocks, GROUP * BLK, HD), jnp.bfloat16)
        tiles = VMEM((total_rows // TILE, TILE, GROUP * BLK), jnp.float32)
        return [
            stacked,
            stacked,
            VMEM((blocks, BLK, GROUP * HD), jnp.bfloat16),
            tiles,
            tiles,
            SMEM((4 * GROUP, HD), jnp.int32),
            DMA,
        ]

    *row_grads, keys, keys_t, all_values, dk_first, dv_first, marks = pl.pallas_call(
        attend_first,
        out_shape=[row_grad] * (GROUP - 1)
        + [sorted_rows, shaped((HD, total_rows)), sorted_rows, sums, sums]
        + [shaped((4 * GROUP, HD), jnp.int32)],
        in_specs=[smem] + [vmem] * (GROUP + 4),
        out_specs=[vmem] * (GROUP + 5),
        scratch_shapes=attend_scratch(Q_BLOCKS - 2),
        compiler_params=limits(20),
        cost_estimate=pl.CostEstimate(flops=ATTEND_COST, bytes_accessed=0, transcendentals=0),
        name="attend_first",
    )(doc_lens, *rows[:-1], own_a, own_b, far_a, far_b, core_pairs)
    last_grad, kept, sent = pl.pallas_call(
        attend_last,
        out_shape=[row_grad, half_sums, half_sums],
        in_specs=[smem] + [vmem] * 7,
        out_specs=[vmem] * 3,
        scratch_shapes=[VMEM((total_rows, HD), jnp.float32)] * 2 + attend_scratch(2),
        compiler_params=limits(20),
        cost_estimate=pl.CostEstimate(flops=ATTEND_COST, bytes_accessed=0, transcendentals=0),
        name="attend_last",
    )(doc_lens, after(rows[-1], w_near), keys, keys_t, all_values, dk_first, dv_first, marks)

    row_grads = with_partners(row_grads)
    sent = after(sent, far_features, *row_grads)
    grads = kept + swap(sent, CORE)
    dk_sum, dv_sum = grads[:, :HD], grads[:, HD:]
    dk_far = swap(dk_sum.astype(jnp.bfloat16), Z_HI)

    feature_parts = pl.pallas_call(
        join_features,
        out_shape=[shaped((2, ROWS, 256))] * GROUP,
        in_specs=[vmem] * 2,
        out_specs=[vmem] * GROUP,
        compiler_params=limits(16),
        name="join_features",
    )(after(near_features, sent), far_features)
    feature_parts = with_partners(feature_parts)
    own_features = pl.pallas_call(
        turn_features,
        out_shape=shaped((256, half)),
        in_specs=[vmem] * GROUP,
        out_specs=vmem,
        compiler_params=limits(16),
        cost_estimate=pl.CostEstimate(flops=1_000_000, bytes_accessed=0, transcendentals=0),
        name="turn_features",
    )(after(feature_parts[0], dk_sum), *feature_parts[1:])
    other_features = swap_tensor(own_features)
    w_far = swap(after(w_near, dk_sum), CORE)

    dk_far = jnp.concatenate([dk_far[quarter:], dk_far[:quarter]], axis=0)
    key_grad = (dk_sum + dk_far.astype(jnp.float32)).astype(jnp.bfloat16)
    last_back = swap(after(last_grad, dk_sum), 6)
    key_grad = after(key_grad, own_features, w_far, last_back)
    from_x, from_z = swap(key_grad, 2), swap(key_grad, 4)
    dv_far = swap(after(dv_sum[quarter:].astype(jnp.bfloat16), key_grad), Z_HI)
    value_grad = (dv_sum[:quarter] + dv_far.astype(jnp.float32)).astype(jnp.bfloat16)
    from_x = after(from_x, value_grad)
    from_z = after(from_z, value_grad)
    near_grads = [part[:quarter] for part in (key_grad, from_x, from_z)]
    far_grads = [part[quarter:] for part in (key_grad, from_x, from_z)]
    value_grads = with_partners([
        after(value_grad[m * ROWS : (m + 1) * ROWS], from_x, from_z) for m in range(GROUP)
    ])
    near_grads.append(swap(near_grads[2], 2))
    far_grads.append(swap(far_grads[1], 4))
    own_key_grad = jnp.stack([near_grads[m][m * ROWS : (m + 1) * ROWS] for m in range(GROUP)])
    other_key_grad = swap_tensor(own_key_grad)

    d_query = pl.pallas_call(
        place_rows,
        out_shape=shaped(queries.shape),
        in_specs=[vmem] * GROUP,
        out_specs=vmem,
        compiler_params=limits(8),
        name="place_rows",
    )(*row_grads, last_back)
    keep, send = pl.pallas_call(
        weight_grad,
        out_shape=[shaped((256, kv_columns), jnp.float32)] * 2,
        in_specs=[vmem] * (2 + 2 * GROUP),
        out_specs=[vmem] * 2,
        scratch_shapes=[VMEM((half, kv_columns), jnp.bfloat16)],
        compiler_params=limits(24),
        cost_estimate=pl.CostEstimate(
            flops=4 * 256 * half * kv_columns, bytes_accessed=4 << 20, transcendentals=0
        ),
        name="weight_grad",
    )(after(own_features, d_query, *value_grads), other_features, *near_grads, *far_grads)
    arrived = swap(send, CORE)

    d_input = pl.pallas_call(
        input_grad,
        out_shape=shaped((ROWS, features // 2)),
        in_specs=[vmem] * 5,
        out_specs=vmem,
        scratch_shapes=[VMEM((ROWS, kv_columns), jnp.bfloat16)] * 2,
        compiler_params=limits(16),
        cost_estimate=pl.CostEstimate(
            flops=4 * ROWS * 2048 * kv_columns, bytes_accessed=5 << 20, transcendentals=0
        ),
        name="input_grad",
    )(after(own_key_grad, send), other_key_grad, w_key, w_near, w_far)

    d_wkey, d_value = pl.pallas_call(
        finish,
        out_shape=[shaped((256, kv_columns), jnp.float32), shaped(values.shape)],
        in_specs=[vmem] * (2 + GROUP),
        out_specs=[vmem] * 2,
        compiler_params=limits(16),
        name="finish",
    )(keep, arrived, *value_grads)
    return (d_query, d_value, d_input, d_wkey)


def solution(mesh):
    by_heads = mesh.shape["dp"] == 16 and mesh.shape["tensor"] == 2
    return jax.shard_map(
        on_device_by_heads if by_heads else on_device,
        mesh=mesh,
        in_specs=(
            P("dp", None),
            P(None, "tensor"),
            P("dp", "tensor"),
            P("dp", "tensor"),
            P("dp", "tensor"),
            P(),
            P("dp"),
        ),
        out_specs=(P("dp", "tensor"), P("dp", "tensor"), P("dp", "tensor"), P("dp", "tensor")),
        check_vma=False,
    )
```

```python
import math

import jax
import jax.numpy as jnp
from jax import lax
from jax.experimental import pallas as pl
from jax.experimental.pallas import tpu as pltpu
from jax.sharding import PartitionSpec as P

HD = 128
BLK = 64


masked_fill = -1e30


def row_positions(block_pos):
    within = jnp.tile(jnp.arange(BLK, dtype=jnp.int32), block_pos.shape[0])
    return jnp.repeat(block_pos, BLK) * BLK + within


def documents(positions, doc_lens):
    starts = jnp.cumsum(doc_lens) - doc_lens
    return jnp.sum((positions[:, None] >= starts[None, :]).astype(jnp.int32), axis=1) - 1


def split_heads(block_rows, kv_heads):
    return block_rows.reshape(block_rows.shape[0], kv_heads, HD)


def scored(query_heads, key_block, score_scale):
    key_split = split_heads(key_block, query_heads.shape[1])
    return (
        jnp.einsum("qcgd,kcd->cgqk", query_heads, key_split, preferred_element_type=jnp.float32)
        * score_scale
    )


def contributions(
    query_heads, grad_heads, key_block, value_block, allowed, row_max, row_sum, delta, score_scale
):
    kv_heads = query_heads.shape[1]
    key_split = split_heads(key_block, kv_heads)
    value_split = split_heads(value_block, kv_heads)
    scores = scored(query_heads, key_block, score_scale)
    mask_full = allowed[None, None]
    probabilities = (
        jnp.where(mask_full, jnp.exp(scores - row_max[..., None]), 0.0) / row_sum[..., None]
    )
    d_prob = jnp.einsum(
        "qcgd,kcd->cgqk", grad_heads, value_split, preferred_element_type=jnp.float32
    )
    d_score = probabilities * (d_prob - delta[..., None])
    prob_bf = probabilities.astype(jnp.bfloat16)
    score_bf = d_score.astype(jnp.bfloat16)
    query_part = score_scale * jnp.einsum(
        "cgqk,kcd->qcgd", score_bf, key_split, preferred_element_type=jnp.float32
    )
    key_part = score_scale * jnp.einsum(
        "cgqk,qcgd->kcd", score_bf, query_heads, preferred_element_type=jnp.float32
    )
    value_part = jnp.einsum(
        "cgqk,qcgd->kcd", prob_bf, grad_heads, preferred_element_type=jnp.float32
    )
    width_rows = key_block.shape[0]
    partial_value = jnp.concatenate(
        [key_part.reshape(width_rows, -1), value_part.reshape(width_rows, -1)], axis=1
    )
    return (query_part, partial_value)


def on_device(inputs, w_key, values, queries, d_out, doc_lens, block_pos):
    local_rows = inputs.shape[0]
    kv_heads = values.shape[1] // HD
    group_size = queries.shape[1] // (kv_heads * HD)
    kv_columns = kv_heads * HD
    score_scale = 1.0 / math.sqrt(HD)
    key_rows = jnp.dot(inputs, w_key, preferred_element_type=jnp.float32).astype(jnp.bfloat16)
    all_keys, all_values, all_blocks = (
        lax.all_gather(key_rows, "dp", axis=0, tiled=True),
        lax.all_gather(values, "dp", axis=0, tiled=True),
        lax.all_gather(block_pos, "dp", axis=0, tiled=True),
    )
    key_pos = row_positions(all_blocks)
    key_doc = documents(key_pos, doc_lens)
    query_pos = row_positions(block_pos)
    query_doc = documents(query_pos, doc_lens)
    query_heads = queries.reshape(local_rows, kv_heads, group_size, HD)
    grad_heads = d_out.reshape(local_rows, kv_heads, group_size, HD)
    total_rows = all_keys.shape[0]
    key_width = math.gcd(512, total_rows)
    stat_shape = (kv_heads, group_size, local_rows)

    def mask_for(first_row, width_rows):
        pos_here = lax.dynamic_slice_in_dim(key_pos, first_row, width_rows, 0)
        doc_here = lax.dynamic_slice_in_dim(key_doc, first_row, width_rows, 0)
        return (query_doc[:, None] == doc_here[None, :]) & (pos_here[None, :] <= query_pos[:, None])

    def visit_stats(block_index, running):
        first_row = block_index * key_width
        key_block = lax.dynamic_slice_in_dim(all_keys, first_row, key_width, 0)
        value_block = lax.dynamic_slice_in_dim(all_values, first_row, key_width, 0)
        allowed = mask_for(first_row, key_width)

        def visit_compute_live(state_now):
            row_max, row_sum, weighted = state_now
            scores = scored(query_heads, key_block, score_scale)
            mask_full = allowed[None, None]
            new_max = jnp.maximum(
                row_max, jnp.max(jnp.where(mask_full, scores, masked_fill), axis=3)
            )
            exp_terms = jnp.where(mask_full, jnp.exp(scores - new_max[..., None]), 0.0)
            d_prob = jnp.einsum(
                "qcgd,kcd->cgqk",
                grad_heads,
                split_heads(value_block, kv_heads),
                preferred_element_type=jnp.float32,
            )
            shrink = jnp.exp(row_max - new_max)
            return (
                new_max,
                row_sum * shrink + jnp.sum(exp_terms, axis=3),
                weighted * shrink + jnp.sum(exp_terms * d_prob, axis=3),
            )

        return lax.cond(jnp.any(allowed), visit_compute_live, lambda state_now: state_now, running)

    start_state = (
        jnp.full(stat_shape, masked_fill, jnp.float32),
        jnp.zeros(stat_shape, jnp.float32),
        jnp.zeros(stat_shape, jnp.float32),
    )
    row_max, row_sum, weighted = lax.fori_loop(0, total_rows // key_width, visit_stats, start_state)
    delta = weighted / row_sum

    def block_work(key_block, value_block, allowed):
        width_rows = key_block.shape[0]

        def block_compute_live(operands):
            return contributions(
                query_heads,
                grad_heads,
                operands[0],
                operands[1],
                operands[2],
                row_max,
                row_sum,
                delta,
                score_scale,
            )

        def dead_block(operands):
            return (
                jnp.zeros((local_rows, kv_heads, group_size, HD), jnp.float32),
                jnp.zeros((width_rows, 2 * kv_columns), jnp.float32),
            )

        return lax.cond(
            jnp.any(allowed), block_compute_live, dead_block, (key_block, value_block, allowed)
        )

    query_start = jnp.zeros((local_rows, kv_heads, group_size, HD), jnp.float32)

    def visit_block(block_index, running):
        query_sum, buffer_rows = running
        first_row = block_index * key_width
        key_block = lax.dynamic_slice_in_dim(all_keys, first_row, key_width, 0)
        value_block = lax.dynamic_slice_in_dim(all_values, first_row, key_width, 0)
        query_part, partial_value = block_work(
            key_block, value_block, mask_for(first_row, key_width)
        )
        return (
            query_sum + query_part,
            lax.dynamic_update_slice_in_dim(buffer_rows, partial_value, first_row, 0),
        )

    empty_buffer = jnp.zeros((total_rows, 2 * kv_columns), jnp.float32)
    query_sum, buffer_rows = lax.fori_loop(
        0, total_rows // key_width, visit_block, (query_start, empty_buffer)
    )
    arrived = lax.all_to_all(
        buffer_rows.astype(jnp.bfloat16), "dp", split_axis=0, concat_axis=0, tiled=True
    ).astype(buffer_rows.dtype)
    own_sums = jnp.sum(arrived.reshape(-1, local_rows, 2 * kv_columns), axis=0)
    d_query = query_sum.astype(jnp.bfloat16).reshape(local_rows, kv_columns * group_size)
    key_grad = own_sums[:, :kv_columns].astype(jnp.bfloat16)
    d_value = own_sums[:, kv_columns:].astype(jnp.bfloat16)
    d_wkey = lax.psum_scatter(
        lax.dot_general(
            inputs, key_grad, (((0,), (0,)), ((), ())), preferred_element_type=jnp.float32
        ),
        "dp",
        scatter_dimension=0,
        tiled=True,
    )
    partial_input = lax.dot_general(
        key_grad, w_key, (((1,), (1,)), ((), ())), preferred_element_type=jnp.float32
    )
    d_input = lax.psum_scatter(
        partial_input.astype(jnp.bfloat16), "tensor", scatter_dimension=1, tiled=True
    )
    return (d_query, d_value, d_input, d_wkey)


CORE, Z_HI = 1, 8
GROUP = 4
ROWS = 128
TILE = 256
UNROLLED = 5
ATTEND_COST = 4_000_000_000
PART = 512
MARKED = ROWS + 16
Q_BLOCKS = GROUP * ROWS // BLK
SMEM = pltpu.SMEM
VMEM = pltpu.VMEM
HBM = pltpu.HBM
DMA = pltpu.SemaphoreType.DMA


def swap(array, mask):
    return lax.ppermute(array, "dp", [(i, i ^ mask) for i in range(16)])


def swap_tensor(array):
    return lax.ppermute(array, "tensor", [(0, 1), (1, 0)])


def own_head():
    return (lax.axis_index("dp") >> 1) & 3


def columns(index, width):
    return pl.ds(pl.multiple_of(index * width, width), width)


def whole_spec(space=VMEM):
    return pl.BlockSpec(memory_space=space)


def after(array, *earlier):
    return lax.optimization_barrier((array,) + earlier)[0]


def copy_all(pairs, semaphores):
    copies = [
        pltpu.make_async_copy(source, target, semaphores.at[i])
        for i, (source, target) in enumerate(pairs)
    ]
    for copy in copies:
        copy.start()
    return copies


def project_keys(pos_ref, inputs_ref, values_ref, w_ref, *refs):
    pair_refs = refs[:GROUP]
    inputs, weights, total, semaphores = refs[GROUP:]
    head = own_head()
    spans = [pl.ds(k * PART, PART) for k in range(weights.shape[0] // PART)]
    copies = copy_all(
        [(inputs_ref, inputs)] + [(w_ref.at[span], weights.at[span]) for span in spans],
        semaphores,
    )
    lanes = lax.broadcasted_iota(jnp.int32, (16, 2 * HD), 1)
    marks = jnp.where(lanes == 0, pos_ref[0], jnp.where(lanes == 1, pos_ref[1], 0))
    for m in range(GROUP):
        pair_refs[m][:ROWS, HD:] = values_ref[:, columns(head ^ m, HD)]
        pair_refs[m][ROWS:] = marks.astype(jnp.float32).astype(jnp.bfloat16)
    copies[0].wait()
    for k, span in enumerate(spans):
        copies[1 + k].wait()
        part = jnp.dot(inputs[:, span], weights[span], preferred_element_type=jnp.float32)
        total[...] = part if k == 0 else total[...] + part
    for m in range(GROUP):
        pair_refs[m][:ROWS, :HD] = total[:, columns(head ^ m, HD)].astype(jnp.bfloat16)


def pack_rows(queries_ref, grads_ref, *out_refs):
    head = own_head()
    for m, out_ref in enumerate(out_refs):
        span = columns(head ^ m, GROUP * HD)
        out_ref[:, : GROUP * HD] = queries_ref[:, span]
        out_ref[:, GROUP * HD :] = grads_ref[:, span]


def pack_weights(w_ref, leaving_ref, semaphore):
    first = (1 - lax.axis_index("tensor")) * 2 + (lax.axis_index("dp") & 1)
    copy = pltpu.make_async_copy(w_ref.at[columns(first, 2 * PART)], leaving_ref, semaphore)
    copy.start()
    copy.wait()


def pack_features(inputs_ref, near_ref, far_ref):
    chip = lax.axis_index("dp") >> 1
    side = lax.axis_index("tensor")
    for m in range(GROUP):
        near_ref[m] = inputs_ref[:, columns(2 * (chip ^ m) + side, 256)]
        far_ref[m] = inputs_ref[:, columns(2 * (chip ^ (m + GROUP)) + side, 256)]


def join_features(near_ref, far_ref, *joined_refs):
    for m, joined_ref in enumerate(joined_refs):
        joined_ref[0] = near_ref[m]
        joined_ref[1] = far_ref[m]


def turn_features(*refs):
    for j in range(2 * GROUP):
        turned = refs[j % GROUP][j // GROUP].astype(jnp.float32).T
        refs[-1][:, j * ROWS : (j + 1) * ROWS] = turned.astype(jnp.bfloat16)


def dot_nt(left, right):
    return lax.dot_general(
        left, right, (((1,), (1,)), ((), ())), preferred_element_type=jnp.float32
    )


def folded(array, reduce):
    return reduce(array.reshape(-1, 8, array.shape[-1]), axis=0)


def first_row_of(positions):
    def first_row(block):
        return pl.multiple_of(positions[block // 2, block % 2] * BLK, BLK)

    return first_row


def attend_rows(
    first_part, first_row, lens_ref, row_refs, dq_refs, keys, keys_t, values, dk, dv, scratch
):
    q_rows, g_rows, dq_all, scores, d_prob = scratch
    score_scale = 1.0 / math.sqrt(HD)
    base_two = score_scale * math.log2(math.e)
    parts = len(row_refs)
    for block in range(2 * parts):
        here = pl.ds(block % 2 * BLK, BLK)
        for h in range(GROUP):
            there = pl.ds(h * BLK, BLK)
            q_rows[block, there] = row_refs[block // 2][here, h * HD : (h + 1) * HD]
            g_rows[block, there] = row_refs[block // 2][
                here, (GROUP + h) * HD : (GROUP + h + 1) * HD
            ]
    starts = [lens_ref[0]]
    for k in (1, 2):
        starts.append(starts[-1] + lens_ref[k])

    def document_start(position):
        found = jnp.zeros_like(position)
        for start in starts:
            found = jnp.where(start <= position, start, found)
        return found

    @pl.loop(0, 2 * parts)
    def _(block):
        first = first_row(2 * first_part + block)
        lanes = lax.broadcasted_iota(jnp.int32, (1, GROUP * BLK), 1)
        position = first + (lanes & (BLK - 1))
        start = document_start(position)
        low = document_start(first) // TILE
        count = (first + BLK - 1) // TILE + 1 - low

        def run(over_tiles):
            query = q_rows[block]
            grad = g_rows[block]
            zeros = jnp.zeros((8, GROUP * BLK), jnp.float32)

            def visit_scores(k, row_max):
                here = columns(low + k, TILE)
                raw = dot_nt(keys[here], query)
                row = (low + k) * TILE + lax.broadcasted_iota(jnp.int32, raw.shape, 0)
                raw = jnp.where((row <= position) & (row >= start), raw, masked_fill)
                scores[k] = raw
                d_prob[k] = dot_nt(values[here], grad)
                return jnp.maximum(row_max, folded(raw, jnp.max))

            row_max = over_tiles(visit_scores, zeros + masked_fill)
            row_max = jnp.max(row_max, axis=0, keepdims=True)

            def visit_sums(k, running):
                terms = jnp.exp2((scores[k] - row_max) * base_two)
                scores[k] = terms
                return (
                    running[0] + folded(terms, jnp.sum),
                    running[1] + folded(terms * d_prob[k], jnp.sum),
                )

            row_sum, weighted = over_tiles(visit_sums, (zeros, zeros))
            inverse = 1.0 / jnp.sum(row_sum, axis=0, keepdims=True)
            delta = jnp.sum(weighted, axis=0, keepdims=True) * inverse

            def visit_grads(k, dq):
                here = columns(low + k, TILE)
                prob = scores[k] * inverse
                score_bf = (prob * (d_prob[k] - delta)).astype(jnp.bfloat16)
                dk[here] += jnp.dot(score_bf, query, preferred_element_type=jnp.float32)
                dv[here] += jnp.dot(
                    prob.astype(jnp.bfloat16), grad, preferred_element_type=jnp.float32
                )
                return dq + jnp.dot(
                    keys_t[:, here], score_bf, preferred_element_type=jnp.float32
                )

            dq = over_tiles(visit_grads, jnp.zeros((HD, GROUP * BLK), jnp.float32))
            dq = (dq * score_scale).T.astype(jnp.bfloat16)
            for h in range(GROUP):
                dq_all[block, :, h * HD : (h + 1) * HD] = dq[h * BLK : (h + 1) * BLK]

        for fixed in range(1, UNROLLED + 1):

            @pl.when(count == fixed)
            def _(fixed=fixed):
                def over_tiles(visit, running):
                    for k in range(fixed):
                        running = visit(k, running)
                    return running

                run(over_tiles)

        @pl.when(count > UNROLLED)
        def _():
            run(lambda visit, running: lax.fori_loop(0, count, visit, running))

    for block in range(2 * parts):
        dq_refs[block // 2][pl.ds(block % 2 * BLK, BLK)] = dq_all[block]


def attend_first(lens_ref, *refs):
    row_refs, refs = refs[: GROUP - 1], refs[GROUP - 1 :]
    own_a, own_b, far_a, far_b, core_pairs, refs = *refs[:5], refs[5:]
    dq_refs, refs = refs[: GROUP - 1], refs[GROUP - 1 :]
    keys, keys_t, values, dk, dv, marks, refs = *refs[:6], refs[6:]
    scratch, (positions, semaphore) = refs[:5], refs[5:]
    reach = 2 * MARKED
    pair_refs = [own_a, own_b]
    pair_refs += [core_pairs.at[pl.ds(k * reach, reach)] for k in range(2)]
    pair_refs += [far_a, far_b]
    pair_refs += [core_pairs.at[pl.ds(k * reach, reach)] for k in range(2, 4)]
    for part in range(4 * GROUP):
        here = pl.ds(part % 2 * MARKED + ROWS, 16)
        row = pair_refs[part // 2][here, :HD].astype(jnp.float32).astype(jnp.int32)
        marks[part : part + 1] = row[:1]
    to_scalars = pltpu.make_async_copy(marks, positions, semaphore)
    to_scalars.start()
    dk[...] = jnp.zeros_like(dk)
    dv[...] = jnp.zeros_like(dv)
    to_scalars.wait()
    first_row = first_row_of(positions)
    for block in range(4 * Q_BLOCKS):
        part = block // 2
        here = pl.ds(part % 2 * MARKED + block % 2 * BLK, BLK)
        there = pl.ds(first_row(block), BLK)
        keys[there] = pair_refs[part // 2][here, :HD]
        values[there] = pair_refs[part // 2][here, HD:]
    for tile in range(keys.shape[0] // TILE):
        here = pl.ds(tile * TILE, TILE)
        keys_t[:, here] = keys[here].astype(jnp.float32).T.astype(jnp.bfloat16)
    attend_rows(
        0, first_row, lens_ref, row_refs, dq_refs, keys, keys_t, values, dk, dv, scratch
    )


def attend_last(lens_ref, row_ref, keys, keys_t, values, dk_first, dv_first, marks, *refs):
    dq_ref, kept, sent, dk, dv, refs = *refs[:5], refs[5:]
    scratch, (positions, semaphore) = refs[:5], refs[5:]
    score_scale = 1.0 / math.sqrt(HD)
    to_scalars = pltpu.make_async_copy(marks, positions, semaphore)
    to_scalars.start()
    dk[...] = dk_first[...]
    dv[...] = dv_first[...]
    to_scalars.wait()
    first_row = first_row_of(positions)
    attend_rows(
        GROUP - 1, first_row, lens_ref, [row_ref], [dq_ref], keys, keys_t, values, dk, dv, scratch
    )
    for block in range(4 * Q_BLOCKS):
        quarter = block // Q_BLOCKS
        here = pl.ds(quarter // 2 * Q_BLOCKS * BLK + block % Q_BLOCKS * BLK, BLK)
        there = pl.ds(first_row(block), BLK)
        out_ref = sent if quarter % 2 else kept
        out_ref[here, :HD] = dk[there] * score_scale
        out_ref[here, HD:] = dv[there]


def weight_grad(own_ref, other_ref, *refs):
    grad_refs, (keep_ref, send_ref, grads) = refs[:GROUP], refs[GROUP:]
    head = own_head()
    for k, grad_ref in enumerate(grad_refs):
        for far in range(2):
            for m in range(GROUP):
                here = pl.ds((far * GROUP + m) * ROWS, ROWS)
                there = pl.ds((far * GROUP + (m ^ k)) * ROWS, ROWS)
                grads[here, columns(head ^ k, HD)] = grad_ref[there]
    own = jnp.dot(own_ref[...], grads[...], preferred_element_type=jnp.float32)
    other = jnp.dot(other_ref[...], grads[...], preferred_element_type=jnp.float32)
    crossed = (lax.axis_index("dp") & 1) ^ lax.axis_index("tensor")

    @pl.when(crossed == 0)
    def _():
        keep_ref[...] = own
        send_ref[...] = other

    @pl.when(crossed == 1)
    def _():
        keep_ref[...] = other
        send_ref[...] = own


def input_grad(own_ref, other_ref, w_own, w_near, w_far, out_ref, own_all, other_all):
    head = own_head()
    core = lax.axis_index("dp") & 1
    side = lax.axis_index("tensor")
    for k in range(GROUP):
        own_all[:, columns(head ^ k, HD)] = own_ref[k]
        other_all[:, columns(head ^ k, HD)] = other_ref[k]
    for k in range(4):
        chunk = 2 * (core ^ (k // 2)) + k % 2
        w_other = (w_near, w_far)[k // 2][pl.ds(k % 2 * PART, PART)]
        part = dot_nt(own_all[...], w_own[columns(side * 4 + chunk, PART)])
        part = part + dot_nt(other_all[...], w_other)
        out_ref[:, columns(chunk, PART)] = part.astype(jnp.bfloat16)


def sum_cores(kept_ref, arrived_ref, dk_ref, dk_bf_ref, *dv_refs):
    dk = kept_ref[:, :HD] + arrived_ref[:, :HD]
    dk_ref[...] = dk
    dk_bf_ref[...] = dk.astype(jnp.bfloat16)
    for m, dv_ref in enumerate(dv_refs):
        for far in range(2):
            here = pl.ds((far * GROUP + m) * ROWS, ROWS)
            dv_ref[far] = (kept_ref[here, HD:] + arrived_ref[here, HD:]).astype(jnp.bfloat16)


def sum_halves(near_ref, far_ref, out_ref):
    quarter = GROUP * ROWS
    for k in range(2):
        here, there = pl.ds(k * quarter, quarter), pl.ds((1 - k) * quarter, quarter)
        total = near_ref[here] + far_ref[there].astype(jnp.float32)
        out_ref[here] = total.astype(jnp.bfloat16)


def finish(keep_ref, arrived_ref, far_ref, *refs):
    row_refs, value_refs, refs = refs[:GROUP], refs[GROUP : 2 * GROUP], refs[2 * GROUP :]
    weight_out, query_out, value_out = refs
    head = own_head()
    weight_out[...] = keep_ref[...] + arrived_ref[...]
    for m in range(GROUP):
        query_out[:, columns(head ^ m, GROUP * HD)] = row_refs[m][...]
        value = value_refs[m][0].astype(jnp.float32) + far_ref[m].astype(jnp.float32)
        value_out[:, columns(head ^ m, HD)] = value.astype(jnp.bfloat16)


def shaped(shape, dtype=jnp.bfloat16):
    return jax.ShapeDtypeStruct(shape, dtype)


def limits(mebibytes):
    return pltpu.CompilerParams(vmem_limit_bytes=mebibytes << 20)


def with_partners(arrays):
    return [arrays[0]] + [swap(arrays[m], 2 * m) for m in range(1, len(arrays))]


def on_device_by_heads(inputs, w_key, values, queries, d_out, doc_lens, block_pos):
    features = inputs.shape[1]
    kv_columns = values.shape[1]
    total_rows = 16 * ROWS
    half = total_rows // 2
    vmem, smem, hbm = whole_spec(), whole_spec(SMEM), whole_spec(HBM)

    pairs = pl.pallas_call(
        project_keys,
        out_shape=[shaped((MARKED, 2 * HD))] * GROUP,
        in_specs=[smem, hbm, vmem, hbm],
        out_specs=[vmem] * GROUP,
        scratch_shapes=[
            VMEM((ROWS, features), jnp.bfloat16),
            VMEM((features, kv_columns), jnp.bfloat16),
            VMEM((ROWS, kv_columns), jnp.float32),
            DMA((1 + features // PART,)),
        ],
        compiler_params=limits(60),
        cost_estimate=pl.CostEstimate(
            flops=2 * ROWS * features * kv_columns,
            bytes_accessed=features * kv_columns * 2,
            transcendentals=0,
        ),
        name="project_keys",
    )(block_pos, inputs, values, w_key)

    packed_rows = pl.pallas_call(
        pack_rows,
        out_shape=[shaped((ROWS, 2 * GROUP * HD))] * GROUP,
        in_specs=[vmem] * 2,
        out_specs=[vmem] * GROUP,
        compiler_params=limits(8),
        name="pack_rows",
    )(after(queries, pairs[0]), d_out)

    pairs = [after(pairs[0], packed_rows[0])] + list(pairs[1:])
    pairs = with_partners(pairs)
    own_a = jnp.concatenate(pairs[:2], axis=0)
    own_b = jnp.concatenate(pairs[2:], axis=0)
    far_a = swap(own_a, Z_HI)
    far_b = swap(own_b, Z_HI)
    rows = with_partners(packed_rows)

    near_features, far_features = pl.pallas_call(
        pack_features,
        out_shape=[shaped((GROUP, ROWS, 256))] * 2,
        in_specs=[vmem],
        out_specs=[vmem] * 2,
        compiler_params=limits(8),
        name="pack_features",
    )(after(inputs, own_a))
    leaving = pl.pallas_call(
        pack_weights,
        out_shape=shaped((2 * PART, kv_columns)),
        in_specs=[hbm],
        out_specs=vmem,
        scratch_shapes=[DMA],
        compiler_params=limits(56),
        name="pack_weights",
    )(after(w_key, own_b))
    w_near = swap_tensor(leaving)
    near_pairs = jnp.concatenate([own_a, own_b, far_a, far_b], axis=0)
    core_pairs = swap(after(near_pairs, near_features, leaving, rows[1], rows[2]), CORE)
    far_features = swap(far_features, Z_HI)

    row_grad = shaped((ROWS, GROUP * HD))
    sorted_rows = shaped((total_rows, HD))
    sums = shaped((total_rows, HD), jnp.float32)
    half_sums = shaped((half, 2 * HD), jnp.float32)

    def attend_scratch(blocks):
        stacked = VMEM((blocks, GROUP * BLK, HD), jnp.bfloat16)
        tiles = VMEM((total_rows // TILE, TILE, GROUP * BLK), jnp.float32)
        return [
            stacked,
            stacked,
            VMEM((blocks, BLK, GROUP * HD), jnp.bfloat16),
            tiles,
            tiles,
            SMEM((4 * GROUP, HD), jnp.int32),
            DMA,
        ]

    *row_grads, keys, keys_t, all_values, dk_first, dv_first, marks = pl.pallas_call(
        attend_first,
        out_shape=[row_grad] * (GROUP - 1)
        + [sorted_rows, shaped((HD, total_rows)), sorted_rows, sums, sums]
        + [shaped((4 * GROUP, HD), jnp.int32)],
        in_specs=[smem] + [vmem] * (GROUP + 4),
        out_specs=[vmem] * (GROUP + 5),
        scratch_shapes=attend_scratch(Q_BLOCKS - 2),
        compiler_params=limits(20),
        cost_estimate=pl.CostEstimate(flops=ATTEND_COST, bytes_accessed=0, transcendentals=0),
        name="attend_first",
    )(doc_lens, *rows[:-1], own_a, own_b, far_a, far_b, core_pairs)
    last_grad, kept, sent = pl.pallas_call(
        attend_last,
        out_shape=[row_grad, half_sums, half_sums],
        in_specs=[smem] + [vmem] * 7,
        out_specs=[vmem] * 3,
        scratch_shapes=[VMEM((total_rows, HD), jnp.float32)] * 2 + attend_scratch(2),
        compiler_params=limits(20),
        cost_estimate=pl.CostEstimate(flops=ATTEND_COST, bytes_accessed=0, transcendentals=0),
        name="attend_last",
    )(doc_lens, after(rows[-1], w_near), keys, keys_t, all_values, dk_first, dv_first, marks)

    row_grads = with_partners(row_grads)
    sent = after(sent, far_features, *row_grads)
    dk_sum, dk_near, *value_grads = pl.pallas_call(
        sum_cores,
        out_shape=[shaped((half, HD), jnp.float32), shaped((half, HD))]
        + [shaped((2, ROWS, HD))] * GROUP,
        in_specs=[vmem] * 2,
        out_specs=[vmem] * (2 + GROUP),
        compiler_params=limits(16),
        name="sum_cores",
    )(kept, swap(sent, CORE))
    dk_far = swap(dk_near, Z_HI)
    value_grads = with_partners(value_grads)
    value_far = jnp.stack([grad[1] for grad in value_grads])

    feature_parts = pl.pallas_call(
        join_features,
        out_shape=[shaped((2, ROWS, 256))] * GROUP,
        in_specs=[vmem] * 2,
        out_specs=[vmem] * GROUP,
        compiler_params=limits(16),
        name="join_features",
    )(after(near_features, sent), far_features)
    own_features = pl.pallas_call(
        turn_features,
        out_shape=shaped((256, half)),
        in_specs=[vmem] * GROUP,
        out_specs=vmem,
        compiler_params=limits(16),
        cost_estimate=pl.CostEstimate(flops=1_000_000_000, bytes_accessed=0, transcendentals=0),
        name="turn_features",
    )(*with_partners(feature_parts))
    other_features = swap_tensor(own_features)

    key_grad = pl.pallas_call(
        sum_halves,
        out_shape=shaped((half, HD)),
        in_specs=[vmem] * 2,
        out_specs=vmem,
        compiler_params=limits(8),
        cost_estimate=pl.CostEstimate(flops=1_000_000, bytes_accessed=0, transcendentals=0),
        name="sum_halves",
    )(dk_sum, dk_far)
    key_grad = after(key_grad, own_features, value_far)
    key_grads = with_partners([key_grad] * GROUP)
    w_far = swap(after(w_near, key_grad), CORE)
    own_key_grad = jnp.stack([key_grads[m][m * ROWS : (m + 1) * ROWS] for m in range(GROUP)])
    other_key_grad = swap_tensor(own_key_grad)

    value_far = swap(after(value_far, key_grad), Z_HI)
    last_grad = swap(after(last_grad, own_key_grad), 6)

    keep, send = pl.pallas_call(
        weight_grad,
        out_shape=[shaped((256, kv_columns), jnp.float32)] * 2,
        in_specs=[vmem] * (2 + GROUP),
        out_specs=[vmem] * 2,
        scratch_shapes=[VMEM((half, kv_columns), jnp.bfloat16)],
        compiler_params=limits(24),
        cost_estimate=pl.CostEstimate(
            flops=4 * 256 * half * kv_columns, bytes_accessed=4 << 20, transcendentals=0
        ),
        name="weight_grad",
    )(after(own_features, value_far), other_features, *key_grads)
    arrived = swap(send, CORE)

    d_input = pl.pallas_call(
        input_grad,
        out_shape=shaped((ROWS, features // 2)),
        in_specs=[vmem] * 5,
        out_specs=vmem,
        scratch_shapes=[VMEM((ROWS, kv_columns), jnp.bfloat16)] * 2,
        compiler_params=limits(16),
        cost_estimate=pl.CostEstimate(
            flops=4 * ROWS * 2048 * kv_columns, bytes_accessed=5 << 20, transcendentals=0
        ),
        name="input_grad",
    )(after(own_key_grad, send), other_key_grad, w_key, w_near, w_far)

    d_wkey, d_query, d_value = pl.pallas_call(
        finish,
        out_shape=[
            shaped((256, kv_columns), jnp.float32),
            shaped(queries.shape),
            shaped(values.shape),
        ],
        in_specs=[vmem] * (3 + 2 * GROUP),
        out_specs=[vmem] * 3,
        compiler_params=limits(16),
        name="finish",
    )(after(keep, d_input), arrived, value_far, *row_grads, last_grad, *value_grads)
    return (d_query, d_value, d_input, d_wkey)


def solution(mesh):
    by_heads = mesh.shape["dp"] == 16 and mesh.shape["tensor"] == 2
    return jax.shard_map(
        on_device_by_heads if by_heads else on_device,
        mesh=mesh,
        in_specs=(
            P("dp", None),
            P(None, "tensor"),
            P("dp", "tensor"),
            P("dp", "tensor"),
            P("dp", "tensor"),
            P(),
            P("dp"),
        ),
        out_specs=(P("dp", "tensor"), P("dp", "tensor"), P("dp", "tensor"), P("dp", "tensor")),
        check_vma=False,
    )
```

```python
import math

import jax
import jax.numpy as jnp
from jax import lax
from jax.experimental import pallas as pl
from jax.experimental.pallas import tpu as pltpu
from jax.sharding import PartitionSpec as P

HD = 128
BLK = 64


masked_fill = -1e30


def row_positions(block_pos):
    within = jnp.tile(jnp.arange(BLK, dtype=jnp.int32), block_pos.shape[0])
    return jnp.repeat(block_pos, BLK) * BLK + within


def documents(positions, doc_lens):
    starts = jnp.cumsum(doc_lens) - doc_lens
    return jnp.sum((positions[:, None] >= starts[None, :]).astype(jnp.int32), axis=1) - 1


def split_heads(block_rows, kv_heads):
    return block_rows.reshape(block_rows.shape[0], kv_heads, HD)


def scored(query_heads, key_block, score_scale):
    key_split = split_heads(key_block, query_heads.shape[1])
    return (
        jnp.einsum("qcgd,kcd->cgqk", query_heads, key_split, preferred_element_type=jnp.float32)
        * score_scale
    )


def contributions(
    query_heads, grad_heads, key_block, value_block, allowed, row_max, row_sum, delta, score_scale
):
    kv_heads = query_heads.shape[1]
    key_split = split_heads(key_block, kv_heads)
    value_split = split_heads(value_block, kv_heads)
    scores = scored(query_heads, key_block, score_scale)
    mask_full = allowed[None, None]
    probabilities = (
        jnp.where(mask_full, jnp.exp(scores - row_max[..., None]), 0.0) / row_sum[..., None]
    )
    d_prob = jnp.einsum(
        "qcgd,kcd->cgqk", grad_heads, value_split, preferred_element_type=jnp.float32
    )
    d_score = probabilities * (d_prob - delta[..., None])
    prob_bf = probabilities.astype(jnp.bfloat16)
    score_bf = d_score.astype(jnp.bfloat16)
    query_part = score_scale * jnp.einsum(
        "cgqk,kcd->qcgd", score_bf, key_split, preferred_element_type=jnp.float32
    )
    key_part = score_scale * jnp.einsum(
        "cgqk,qcgd->kcd", score_bf, query_heads, preferred_element_type=jnp.float32
    )
    value_part = jnp.einsum(
        "cgqk,qcgd->kcd", prob_bf, grad_heads, preferred_element_type=jnp.float32
    )
    width_rows = key_block.shape[0]
    partial_value = jnp.concatenate(
        [key_part.reshape(width_rows, -1), value_part.reshape(width_rows, -1)], axis=1
    )
    return (query_part, partial_value)


def on_device(inputs, w_key, values, queries, d_out, doc_lens, block_pos):
    local_rows = inputs.shape[0]
    kv_heads = values.shape[1] // HD
    group_size = queries.shape[1] // (kv_heads * HD)
    kv_columns = kv_heads * HD
    score_scale = 1.0 / math.sqrt(HD)
    key_rows = jnp.dot(inputs, w_key, preferred_element_type=jnp.float32).astype(jnp.bfloat16)
    all_keys, all_values, all_blocks = (
        lax.all_gather(key_rows, "dp", axis=0, tiled=True),
        lax.all_gather(values, "dp", axis=0, tiled=True),
        lax.all_gather(block_pos, "dp", axis=0, tiled=True),
    )
    key_pos = row_positions(all_blocks)
    key_doc = documents(key_pos, doc_lens)
    query_pos = row_positions(block_pos)
    query_doc = documents(query_pos, doc_lens)
    query_heads = queries.reshape(local_rows, kv_heads, group_size, HD)
    grad_heads = d_out.reshape(local_rows, kv_heads, group_size, HD)
    total_rows = all_keys.shape[0]
    key_width = math.gcd(512, total_rows)
    stat_shape = (kv_heads, group_size, local_rows)

    def mask_for(first_row, width_rows):
        pos_here = lax.dynamic_slice_in_dim(key_pos, first_row, width_rows, 0)
        doc_here = lax.dynamic_slice_in_dim(key_doc, first_row, width_rows, 0)
        return (query_doc[:, None] == doc_here[None, :]) & (pos_here[None, :] <= query_pos[:, None])

    def visit_stats(block_index, running):
        first_row = block_index * key_width
        key_block = lax.dynamic_slice_in_dim(all_keys, first_row, key_width, 0)
        value_block = lax.dynamic_slice_in_dim(all_values, first_row, key_width, 0)
        allowed = mask_for(first_row, key_width)

        def visit_compute_live(state_now):
            row_max, row_sum, weighted = state_now
            scores = scored(query_heads, key_block, score_scale)
            mask_full = allowed[None, None]
            new_max = jnp.maximum(
                row_max, jnp.max(jnp.where(mask_full, scores, masked_fill), axis=3)
            )
            exp_terms = jnp.where(mask_full, jnp.exp(scores - new_max[..., None]), 0.0)
            d_prob = jnp.einsum(
                "qcgd,kcd->cgqk",
                grad_heads,
                split_heads(value_block, kv_heads),
                preferred_element_type=jnp.float32,
            )
            shrink = jnp.exp(row_max - new_max)
            return (
                new_max,
                row_sum * shrink + jnp.sum(exp_terms, axis=3),
                weighted * shrink + jnp.sum(exp_terms * d_prob, axis=3),
            )

        return lax.cond(jnp.any(allowed), visit_compute_live, lambda state_now: state_now, running)

    start_state = (
        jnp.full(stat_shape, masked_fill, jnp.float32),
        jnp.zeros(stat_shape, jnp.float32),
        jnp.zeros(stat_shape, jnp.float32),
    )
    row_max, row_sum, weighted = lax.fori_loop(0, total_rows // key_width, visit_stats, start_state)
    delta = weighted / row_sum

    def block_work(key_block, value_block, allowed):
        width_rows = key_block.shape[0]

        def block_compute_live(operands):
            return contributions(
                query_heads,
                grad_heads,
                operands[0],
                operands[1],
                operands[2],
                row_max,
                row_sum,
                delta,
                score_scale,
            )

        def dead_block(operands):
            return (
                jnp.zeros((local_rows, kv_heads, group_size, HD), jnp.float32),
                jnp.zeros((width_rows, 2 * kv_columns), jnp.float32),
            )

        return lax.cond(
            jnp.any(allowed), block_compute_live, dead_block, (key_block, value_block, allowed)
        )

    query_start = jnp.zeros((local_rows, kv_heads, group_size, HD), jnp.float32)

    def visit_block(block_index, running):
        query_sum, buffer_rows = running
        first_row = block_index * key_width
        key_block = lax.dynamic_slice_in_dim(all_keys, first_row, key_width, 0)
        value_block = lax.dynamic_slice_in_dim(all_values, first_row, key_width, 0)
        query_part, partial_value = block_work(
            key_block, value_block, mask_for(first_row, key_width)
        )
        return (
            query_sum + query_part,
            lax.dynamic_update_slice_in_dim(buffer_rows, partial_value, first_row, 0),
        )

    empty_buffer = jnp.zeros((total_rows, 2 * kv_columns), jnp.float32)
    query_sum, buffer_rows = lax.fori_loop(
        0, total_rows // key_width, visit_block, (query_start, empty_buffer)
    )
    arrived = lax.all_to_all(
        buffer_rows.astype(jnp.bfloat16), "dp", split_axis=0, concat_axis=0, tiled=True
    ).astype(buffer_rows.dtype)
    own_sums = jnp.sum(arrived.reshape(-1, local_rows, 2 * kv_columns), axis=0)
    d_query = query_sum.astype(jnp.bfloat16).reshape(local_rows, kv_columns * group_size)
    key_grad = own_sums[:, :kv_columns].astype(jnp.bfloat16)
    d_value = own_sums[:, kv_columns:].astype(jnp.bfloat16)
    d_wkey = lax.psum_scatter(
        lax.dot_general(
            inputs, key_grad, (((0,), (0,)), ((), ())), preferred_element_type=jnp.float32
        ),
        "dp",
        scatter_dimension=0,
        tiled=True,
    )
    partial_input = lax.dot_general(
        key_grad, w_key, (((1,), (1,)), ((), ())), preferred_element_type=jnp.float32
    )
    d_input = lax.psum_scatter(
        partial_input.astype(jnp.bfloat16), "tensor", scatter_dimension=1, tiled=True
    )
    return (d_query, d_value, d_input, d_wkey)


CORE, Z_HI = 1, 8
GROUP = 4
ROWS = 128
TILE = 256
UNROLLED = 5
ATTEND_COST = 4_000_000_000
PART = 512
MARKED = ROWS + 16
Q_BLOCKS = GROUP * ROWS // BLK
SMEM = pltpu.SMEM
VMEM = pltpu.VMEM
HBM = pltpu.HBM
DMA = pltpu.SemaphoreType.DMA


def swap(array, mask):
    return lax.ppermute(array, "dp", [(i, i ^ mask) for i in range(16)])


def swap_tensor(array):
    return lax.ppermute(array, "tensor", [(0, 1), (1, 0)])


def own_head():
    return (lax.axis_index("dp") >> 1) & 3


def columns(index, width):
    return pl.ds(pl.multiple_of(index * width, width), width)


def whole_spec(space=VMEM):
    return pl.BlockSpec(memory_space=space)


def after(array, *earlier):
    return lax.optimization_barrier((array,) + earlier)[0]


def copy_all(pairs, semaphores):
    copies = [
        pltpu.make_async_copy(source, target, semaphores.at[i])
        for i, (source, target) in enumerate(pairs)
    ]
    for copy in copies:
        copy.start()
    return copies


def project_keys(pos_ref, inputs_ref, values_ref, w_ref, *refs):
    pair_refs = refs[:GROUP]
    inputs, weights, total, semaphores = refs[GROUP:]
    head = own_head()
    spans = [pl.ds(k * PART, PART) for k in range(weights.shape[0] // PART)]
    copies = copy_all(
        [(inputs_ref, inputs)] + [(w_ref.at[span], weights.at[span]) for span in spans],
        semaphores,
    )
    lanes = lax.broadcasted_iota(jnp.int32, (16, 2 * HD), 1)
    marks = jnp.where(lanes == 0, pos_ref[0], jnp.where(lanes == 1, pos_ref[1], 0))
    for m in range(GROUP):
        pair_refs[m][:ROWS, HD:] = values_ref[:, columns(head ^ m, HD)]
        pair_refs[m][ROWS:] = marks.astype(jnp.float32).astype(jnp.bfloat16)
    copies[0].wait()
    for k, span in enumerate(spans):
        copies[1 + k].wait()
        part = jnp.dot(inputs[:, span], weights[span], preferred_element_type=jnp.float32)
        total[...] = part if k == 0 else total[...] + part
    for m in range(GROUP):
        pair_refs[m][:ROWS, :HD] = total[:, columns(head ^ m, HD)].astype(jnp.bfloat16)


def pack_rows(queries_ref, grads_ref, *out_refs):
    head = own_head()
    for m, out_ref in enumerate(out_refs):
        span = columns(head ^ m, GROUP * HD)
        out_ref[:, : GROUP * HD] = queries_ref[:, span]
        out_ref[:, GROUP * HD :] = grads_ref[:, span]


def pack_weights(w_ref, leaving_ref, semaphore):
    first = (1 - lax.axis_index("tensor")) * 2 + (lax.axis_index("dp") & 1)
    copy = pltpu.make_async_copy(w_ref.at[columns(first, 2 * PART)], leaving_ref, semaphore)
    copy.start()
    copy.wait()


def pack_features(inputs_ref, near_ref, far_ref):
    chip = lax.axis_index("dp") >> 1
    side = lax.axis_index("tensor")
    for m in range(GROUP):
        near_ref[m] = inputs_ref[:, columns(2 * (chip ^ m) + side, 256)]
        far_ref[m] = inputs_ref[:, columns(2 * (chip ^ (m + GROUP)) + side, 256)]


def join_features(near_ref, far_ref, *joined_refs):
    for m, joined_ref in enumerate(joined_refs):
        joined_ref[0] = near_ref[m]
        joined_ref[1] = far_ref[m]


def turn_features(*refs):
    for j in range(2 * GROUP):
        turned = refs[j % GROUP][j // GROUP].astype(jnp.float32).T
        refs[-1][:, j * ROWS : (j + 1) * ROWS] = turned.astype(jnp.bfloat16)


def dot_nt(left, right):
    return lax.dot_general(
        left, right, (((1,), (1,)), ((), ())), preferred_element_type=jnp.float32
    )


def folded(array, reduce):
    return reduce(array.reshape(-1, 8, array.shape[-1]), axis=0)


def first_row_of(positions):
    def first_row(block):
        return pl.multiple_of(positions[block // 2, block % 2] * BLK, BLK)

    return first_row


def attend_rows(
    first_part, first_row, lens_ref, row_refs, dq_refs, keys, keys_t, values, dk, dv, scratch
):
    q_rows, g_rows, dq_all, scores, d_prob = scratch
    score_scale = 1.0 / math.sqrt(HD)
    base_two = score_scale * math.log2(math.e)
    parts = len(row_refs)
    for block in range(2 * parts):
        here = pl.ds(block % 2 * BLK, BLK)
        for h in range(GROUP):
            there = pl.ds(h * BLK, BLK)
            q_rows[block, there] = row_refs[block // 2][here, h * HD : (h + 1) * HD]
            g_rows[block, there] = row_refs[block // 2][
                here, (GROUP + h) * HD : (GROUP + h + 1) * HD
            ]
    starts = [lens_ref[0]]
    for k in (1, 2):
        starts.append(starts[-1] + lens_ref[k])

    def document_start(position):
        found = jnp.zeros_like(position)
        for start in starts:
            found = jnp.where(start <= position, start, found)
        return found

    @pl.loop(0, 2 * parts)
    def _(block):
        first = first_row(2 * first_part + block)
        lanes = lax.broadcasted_iota(jnp.int32, (1, GROUP * BLK), 1)
        position = first + (lanes & (BLK - 1))
        start = document_start(position)
        low = document_start(first) // HD * HD
        count = (first + BLK - low + TILE - 1) // TILE

        def rows_of(k):
            return pl.ds(pl.multiple_of(low + k * TILE, HD), TILE)

        def run(over_tiles):
            query = q_rows[block]
            grad = g_rows[block]
            zeros = jnp.zeros((8, GROUP * BLK), jnp.float32)

            def visit_scores(k, row_max):
                here = rows_of(k)
                raw = dot_nt(keys[here], query)
                row = low + k * TILE + lax.broadcasted_iota(jnp.int32, raw.shape, 0)
                raw = jnp.where((row <= position) & (row >= start), raw, masked_fill)
                scores[k] = raw
                d_prob[k] = dot_nt(values[here], grad)
                return jnp.maximum(row_max, folded(raw, jnp.max))

            row_max = over_tiles(visit_scores, zeros + masked_fill)
            row_max = jnp.max(row_max, axis=0, keepdims=True)

            def visit_sums(k, running):
                terms = jnp.exp2((scores[k] - row_max) * base_two)
                scores[k] = terms
                return (
                    running[0] + folded(terms, jnp.sum),
                    running[1] + folded(terms * d_prob[k], jnp.sum),
                )

            row_sum, weighted = over_tiles(visit_sums, (zeros, zeros))
            inverse = 1.0 / jnp.sum(row_sum, axis=0, keepdims=True)
            delta = jnp.sum(weighted, axis=0, keepdims=True) * inverse

            def visit_grads(k, dq):
                here = rows_of(k)
                prob = scores[k] * inverse
                score_bf = (prob * (d_prob[k] - delta)).astype(jnp.bfloat16)
                dk[here] += jnp.dot(score_bf, query, preferred_element_type=jnp.float32)
                dv[here] += jnp.dot(
                    prob.astype(jnp.bfloat16), grad, preferred_element_type=jnp.float32
                )
                return dq + jnp.dot(
                    keys_t[:, here], score_bf, preferred_element_type=jnp.float32
                )

            dq = over_tiles(visit_grads, jnp.zeros((HD, GROUP * BLK), jnp.float32))
            dq = (dq * score_scale).T.astype(jnp.bfloat16)
            for h in range(GROUP):
                dq_all[block, :, h * HD : (h + 1) * HD] = dq[h * BLK : (h + 1) * BLK]

        for fixed in range(1, UNROLLED + 1):

            @pl.when(count == fixed)
            def _(fixed=fixed):
                def over_tiles(visit, running):
                    for k in range(fixed):
                        running = visit(k, running)
                    return running

                run(over_tiles)

        @pl.when(count > UNROLLED)
        def _():
            run(lambda visit, running: lax.fori_loop(0, count, visit, running))

    for block in range(2 * parts):
        dq_refs[block // 2][pl.ds(block % 2 * BLK, BLK)] = dq_all[block]


def attend_first(lens_ref, *refs):
    row_refs, refs = refs[: GROUP - 1], refs[GROUP - 1 :]
    own_a, own_b, far_a, far_b, core_pairs, refs = *refs[:5], refs[5:]
    dq_refs, refs = refs[: GROUP - 1], refs[GROUP - 1 :]
    keys, keys_t, values, dk, dv, marks, refs = *refs[:6], refs[6:]
    scratch, (positions, semaphore) = refs[:5], refs[5:]
    reach = 2 * MARKED
    pair_refs = [own_a, own_b]
    pair_refs += [core_pairs.at[pl.ds(k * reach, reach)] for k in range(2)]
    pair_refs += [far_a, far_b]
    pair_refs += [core_pairs.at[pl.ds(k * reach, reach)] for k in range(2, 4)]
    for part in range(4 * GROUP):
        here = pl.ds(part % 2 * MARKED + ROWS, 16)
        row = pair_refs[part // 2][here, :HD].astype(jnp.float32).astype(jnp.int32)
        marks[part : part + 1] = row[:1]
    to_scalars = pltpu.make_async_copy(marks, positions, semaphore)
    to_scalars.start()
    dk[...] = jnp.zeros_like(dk)
    dv[...] = jnp.zeros_like(dv)
    to_scalars.wait()
    first_row = first_row_of(positions)
    for block in range(4 * Q_BLOCKS):
        part = block // 2
        here = pl.ds(part % 2 * MARKED + block % 2 * BLK, BLK)
        there = pl.ds(first_row(block), BLK)
        keys[there] = pair_refs[part // 2][here, :HD]
        values[there] = pair_refs[part // 2][here, HD:]
    beyond = pl.ds(4 * GROUP * ROWS, HD)
    keys[beyond] = jnp.zeros((HD, HD), jnp.bfloat16)
    keys_t[:, beyond] = jnp.zeros((HD, HD), jnp.bfloat16)
    values[beyond] = jnp.zeros((HD, HD), jnp.bfloat16)
    for tile in range(keys.shape[0] // TILE):
        here = pl.ds(tile * TILE, TILE)
        keys_t[:, here] = keys[here].astype(jnp.float32).T.astype(jnp.bfloat16)
    attend_rows(
        0, first_row, lens_ref, row_refs, dq_refs, keys, keys_t, values, dk, dv, scratch
    )


def attend_last(lens_ref, row_ref, keys, keys_t, values, dk_first, dv_first, marks, *refs):
    dq_ref, kept, sent, dk, dv, refs = *refs[:5], refs[5:]
    scratch, (positions, semaphore) = refs[:5], refs[5:]
    score_scale = 1.0 / math.sqrt(HD)
    to_scalars = pltpu.make_async_copy(marks, positions, semaphore)
    to_scalars.start()
    dk[...] = dk_first[...]
    dv[...] = dv_first[...]
    to_scalars.wait()
    first_row = first_row_of(positions)
    attend_rows(
        GROUP - 1, first_row, lens_ref, [row_ref], [dq_ref], keys, keys_t, values, dk, dv, scratch
    )
    for block in range(4 * Q_BLOCKS):
        quarter = block // Q_BLOCKS
        here = pl.ds(quarter // 2 * Q_BLOCKS * BLK + block % Q_BLOCKS * BLK, BLK)
        there = pl.ds(first_row(block), BLK)
        out_ref = sent if quarter % 2 else kept
        out_ref[here, :HD] = dk[there] * score_scale
        out_ref[here, HD:] = dv[there]


def weight_grad(own_ref, other_ref, *refs):
    grad_refs, (keep_ref, send_ref, grads) = refs[:GROUP], refs[GROUP:]
    head = own_head()
    for k, grad_ref in enumerate(grad_refs):
        for far in range(2):
            for m in range(GROUP):
                here = pl.ds((far * GROUP + m) * ROWS, ROWS)
                there = pl.ds((far * GROUP + (m ^ k)) * ROWS, ROWS)
                grads[here, columns(head ^ k, HD)] = grad_ref[there]
    own = jnp.dot(own_ref[...], grads[...], preferred_element_type=jnp.float32)
    other = jnp.dot(other_ref[...], grads[...], preferred_element_type=jnp.float32)
    crossed = (lax.axis_index("dp") & 1) ^ lax.axis_index("tensor")

    @pl.when(crossed == 0)
    def _():
        keep_ref[...] = own
        send_ref[...] = other

    @pl.when(crossed == 1)
    def _():
        keep_ref[...] = other
        send_ref[...] = own


def input_grad(own_ref, other_ref, w_own, w_near, w_far, out_ref, own_all, other_all):
    head = own_head()
    core = lax.axis_index("dp") & 1
    side = lax.axis_index("tensor")
    for k in range(GROUP):
        own_all[:, columns(head ^ k, HD)] = own_ref[k]
        other_all[:, columns(head ^ k, HD)] = other_ref[k]
    for k in range(4):
        chunk = 2 * (core ^ (k // 2)) + k % 2
        w_other = (w_near, w_far)[k // 2][pl.ds(k % 2 * PART, PART)]
        part = dot_nt(own_all[...], w_own[columns(side * 4 + chunk, PART)])
        part = part + dot_nt(other_all[...], w_other)
        out_ref[:, columns(chunk, PART)] = part.astype(jnp.bfloat16)


def sum_cores(kept_ref, arrived_ref, dk_ref, dk_bf_ref, *dv_refs):
    dk = kept_ref[:, :HD] + arrived_ref[:, :HD]
    dk_ref[...] = dk
    dk_bf_ref[...] = dk.astype(jnp.bfloat16)
    for m, dv_ref in enumerate(dv_refs):
        for far in range(2):
            here = pl.ds((far * GROUP + m) * ROWS, ROWS)
            dv_ref[far] = (kept_ref[here, HD:] + arrived_ref[here, HD:]).astype(jnp.bfloat16)


def sum_halves(near_ref, far_ref, out_ref):
    quarter = GROUP * ROWS
    for k in range(2):
        here, there = pl.ds(k * quarter, quarter), pl.ds((1 - k) * quarter, quarter)
        total = near_ref[here] + far_ref[there].astype(jnp.float32)
        out_ref[here] = total.astype(jnp.bfloat16)


def finish(keep_ref, arrived_ref, far_ref, *refs):
    row_refs, value_refs, refs = refs[:GROUP], refs[GROUP : 2 * GROUP], refs[2 * GROUP :]
    weight_out, query_out, value_out = refs
    head = own_head()
    weight_out[...] = keep_ref[...] + arrived_ref[...]
    for m in range(GROUP):
        query_out[:, columns(head ^ m, GROUP * HD)] = row_refs[m][...]
        value = value_refs[m][0].astype(jnp.float32) + far_ref[m].astype(jnp.float32)
        value_out[:, columns(head ^ m, HD)] = value.astype(jnp.bfloat16)


def shaped(shape, dtype=jnp.bfloat16):
    return jax.ShapeDtypeStruct(shape, dtype)


def limits(mebibytes):
    return pltpu.CompilerParams(vmem_limit_bytes=mebibytes << 20)


def with_partners(arrays):
    return [arrays[0]] + [swap(arrays[m], 2 * m) for m in range(1, len(arrays))]


def on_device_by_heads(inputs, w_key, values, queries, d_out, doc_lens, block_pos):
    features = inputs.shape[1]
    kv_columns = values.shape[1]
    total_rows = 16 * ROWS
    half = total_rows // 2
    vmem, smem, hbm = whole_spec(), whole_spec(SMEM), whole_spec(HBM)

    pairs = pl.pallas_call(
        project_keys,
        out_shape=[shaped((MARKED, 2 * HD))] * GROUP,
        in_specs=[smem, hbm, vmem, hbm],
        out_specs=[vmem] * GROUP,
        scratch_shapes=[
            VMEM((ROWS, features), jnp.bfloat16),
            VMEM((features, kv_columns), jnp.bfloat16),
            VMEM((ROWS, kv_columns), jnp.float32),
            DMA((1 + features // PART,)),
        ],
        compiler_params=limits(60),
        cost_estimate=pl.CostEstimate(
            flops=2 * ROWS * features * kv_columns,
            bytes_accessed=features * kv_columns * 2,
            transcendentals=0,
        ),
        name="project_keys",
    )(block_pos, inputs, values, w_key)

    packed_rows = pl.pallas_call(
        pack_rows,
        out_shape=[shaped((ROWS, 2 * GROUP * HD))] * GROUP,
        in_specs=[vmem] * 2,
        out_specs=[vmem] * GROUP,
        compiler_params=limits(8),
        name="pack_rows",
    )(after(queries, pairs[0]), d_out)

    pairs = [after(pairs[0], packed_rows[0])] + list(pairs[1:])
    pairs = with_partners(pairs)
    own_a = jnp.concatenate(pairs[:2], axis=0)
    own_b = jnp.concatenate(pairs[2:], axis=0)
    far_a = swap(own_a, Z_HI)
    far_b = swap(own_b, Z_HI)
    rows = with_partners(packed_rows)

    near_features, far_features = pl.pallas_call(
        pack_features,
        out_shape=[shaped((GROUP, ROWS, 256))] * 2,
        in_specs=[vmem],
        out_specs=[vmem] * 2,
        compiler_params=limits(8),
        name="pack_features",
    )(after(inputs, own_a))
    leaving = pl.pallas_call(
        pack_weights,
        out_shape=shaped((2 * PART, kv_columns)),
        in_specs=[hbm],
        out_specs=vmem,
        scratch_shapes=[DMA],
        compiler_params=limits(56),
        name="pack_weights",
    )(after(w_key, own_b))
    w_near = swap_tensor(leaving)
    near_pairs = jnp.concatenate([own_a, own_b, far_a, far_b], axis=0)
    core_pairs = swap(after(near_pairs, near_features, leaving, rows[1], rows[2]), CORE)
    far_features = swap(far_features, Z_HI)

    row_grad = shaped((ROWS, GROUP * HD))
    padded_rows = total_rows + HD
    sorted_rows = shaped((padded_rows, HD))
    sums = shaped((padded_rows, HD), jnp.float32)
    half_sums = shaped((half, 2 * HD), jnp.float32)

    def attend_scratch(blocks):
        stacked = VMEM((blocks, GROUP * BLK, HD), jnp.bfloat16)
        tiles = VMEM((total_rows // TILE, TILE, GROUP * BLK), jnp.float32)
        return [
            stacked,
            stacked,
            VMEM((blocks, BLK, GROUP * HD), jnp.bfloat16),
            tiles,
            tiles,
            SMEM((4 * GROUP, HD), jnp.int32),
            DMA,
        ]

    *row_grads, keys, keys_t, all_values, dk_first, dv_first, marks = pl.pallas_call(
        attend_first,
        out_shape=[row_grad] * (GROUP - 1)
        + [sorted_rows, shaped((HD, padded_rows)), sorted_rows, sums, sums]
        + [shaped((4 * GROUP, HD), jnp.int32)],
        in_specs=[smem] + [vmem] * (GROUP + 4),
        out_specs=[vmem] * (GROUP + 5),
        scratch_shapes=attend_scratch(Q_BLOCKS - 2),
        compiler_params=limits(20),
        cost_estimate=pl.CostEstimate(flops=ATTEND_COST, bytes_accessed=0, transcendentals=0),
        name="attend_first",
    )(doc_lens, *rows[:-1], own_a, own_b, far_a, far_b, core_pairs)
    last_grad, kept, sent = pl.pallas_call(
        attend_last,
        out_shape=[row_grad, half_sums, half_sums],
        in_specs=[smem] + [vmem] * 7,
        out_specs=[vmem] * 3,
        scratch_shapes=[VMEM((padded_rows, HD), jnp.float32)] * 2 + attend_scratch(2),
        compiler_params=limits(20),
        cost_estimate=pl.CostEstimate(flops=ATTEND_COST, bytes_accessed=0, transcendentals=0),
        name="attend_last",
    )(doc_lens, after(rows[-1], w_near), keys, keys_t, all_values, dk_first, dv_first, marks)

    row_grads = with_partners(row_grads)
    sent = after(sent, far_features, *row_grads)
    dk_sum, dk_near, *value_grads = pl.pallas_call(
        sum_cores,
        out_shape=[shaped((half, HD), jnp.float32), shaped((half, HD))]
        + [shaped((2, ROWS, HD))] * GROUP,
        in_specs=[vmem] * 2,
        out_specs=[vmem] * (2 + GROUP),
        compiler_params=limits(16),
        name="sum_cores",
    )(kept, swap(sent, CORE))
    dk_far = swap(dk_near, Z_HI)
    w_far = swap(after(w_near, sent), CORE)
    value_grads = with_partners(value_grads)
    value_far = jnp.stack([grad[1] for grad in value_grads])

    feature_parts = pl.pallas_call(
        join_features,
        out_shape=[shaped((2, ROWS, 256))] * GROUP,
        in_specs=[vmem] * 2,
        out_specs=[vmem] * GROUP,
        compiler_params=limits(16),
        name="join_features",
    )(after(near_features, sent), far_features)
    own_features = pl.pallas_call(
        turn_features,
        out_shape=shaped((256, half)),
        in_specs=[vmem] * GROUP,
        out_specs=vmem,
        compiler_params=limits(16),
        cost_estimate=pl.CostEstimate(flops=1_000_000_000, bytes_accessed=0, transcendentals=0),
        name="turn_features",
    )(*with_partners(feature_parts))
    other_features = swap_tensor(own_features)

    key_grad = pl.pallas_call(
        sum_halves,
        out_shape=shaped((half, HD)),
        in_specs=[vmem] * 2,
        out_specs=vmem,
        compiler_params=limits(8),
        cost_estimate=pl.CostEstimate(flops=1_000_000, bytes_accessed=0, transcendentals=0),
        name="sum_halves",
    )(dk_sum, dk_far)
    key_grad = after(key_grad, own_features, value_far, w_far)
    key_grads = with_partners([key_grad] * GROUP)
    own_key_grad = jnp.stack([key_grads[m][m * ROWS : (m + 1) * ROWS] for m in range(GROUP)])
    other_key_grad = swap_tensor(own_key_grad)

    value_far = swap(after(value_far, key_grad), Z_HI)
    last_grad = swap(after(last_grad, own_key_grad), 6)

    keep, send = pl.pallas_call(
        weight_grad,
        out_shape=[shaped((256, kv_columns), jnp.float32)] * 2,
        in_specs=[vmem] * (2 + GROUP),
        out_specs=[vmem] * 2,
        scratch_shapes=[VMEM((half, kv_columns), jnp.bfloat16)],
        compiler_params=limits(24),
        cost_estimate=pl.CostEstimate(
            flops=4 * 256 * half * kv_columns, bytes_accessed=4 << 20, transcendentals=0
        ),
        name="weight_grad",
    )(after(own_features, value_far), other_features, *key_grads)
    arrived = swap(send, CORE)

    d_input = pl.pallas_call(
        input_grad,
        out_shape=shaped((ROWS, features // 2)),
        in_specs=[vmem] * 5,
        out_specs=vmem,
        scratch_shapes=[VMEM((ROWS, kv_columns), jnp.bfloat16)] * 2,
        compiler_params=limits(16),
        cost_estimate=pl.CostEstimate(
            flops=8_000_000_000, bytes_accessed=5 << 20, transcendentals=0
        ),
        name="input_grad",
    )(after(own_key_grad, send), other_key_grad, w_key, w_near, w_far)

    d_wkey, d_query, d_value = pl.pallas_call(
        finish,
        out_shape=[
            shaped((256, kv_columns), jnp.float32),
            shaped(queries.shape),
            shaped(values.shape),
        ],
        in_specs=[vmem] * (3 + 2 * GROUP),
        out_specs=[vmem] * 3,
        compiler_params=limits(16),
        name="finish",
    )(after(keep, d_input), arrived, value_far, *row_grads, last_grad, *value_grads)
    return (d_query, d_value, d_input, d_wkey)


def solution(mesh):
    by_heads = mesh.shape["dp"] == 16 and mesh.shape["tensor"] == 2
    return jax.shard_map(
        on_device_by_heads if by_heads else on_device,
        mesh=mesh,
        in_specs=(
            P("dp", None),
            P(None, "tensor"),
            P("dp", "tensor"),
            P("dp", "tensor"),
            P("dp", "tensor"),
            P(),
            P("dp"),
        ),
        out_specs=(P("dp", "tensor"), P("dp", "tensor"), P("dp", "tensor"), P("dp", "tensor")),
        check_vma=False,
    )
```

```python
import math

import jax
import jax.numpy as jnp
from jax import lax
from jax.experimental import pallas as pl
from jax.experimental.pallas import tpu as pltpu
from jax.sharding import PartitionSpec as P

HD = 128
BLK = 64


masked_fill = -1e30


def row_positions(block_pos):
    within = jnp.tile(jnp.arange(BLK, dtype=jnp.int32), block_pos.shape[0])
    return jnp.repeat(block_pos, BLK) * BLK + within


def documents(positions, doc_lens):
    starts = jnp.cumsum(doc_lens) - doc_lens
    return jnp.sum((positions[:, None] >= starts[None, :]).astype(jnp.int32), axis=1) - 1


def split_heads(block_rows, kv_heads):
    return block_rows.reshape(block_rows.shape[0], kv_heads, HD)


def scored(query_heads, key_block, score_scale):
    key_split = split_heads(key_block, query_heads.shape[1])
    return (
        jnp.einsum("qcgd,kcd->cgqk", query_heads, key_split, preferred_element_type=jnp.float32)
        * score_scale
    )


def contributions(
    query_heads, grad_heads, key_block, value_block, allowed, row_max, row_sum, delta, score_scale
):
    kv_heads = query_heads.shape[1]
    key_split = split_heads(key_block, kv_heads)
    value_split = split_heads(value_block, kv_heads)
    scores = scored(query_heads, key_block, score_scale)
    mask_full = allowed[None, None]
    probabilities = (
        jnp.where(mask_full, jnp.exp(scores - row_max[..., None]), 0.0) / row_sum[..., None]
    )
    d_prob = jnp.einsum(
        "qcgd,kcd->cgqk", grad_heads, value_split, preferred_element_type=jnp.float32
    )
    d_score = probabilities * (d_prob - delta[..., None])
    prob_bf = probabilities.astype(jnp.bfloat16)
    score_bf = d_score.astype(jnp.bfloat16)
    query_part = score_scale * jnp.einsum(
        "cgqk,kcd->qcgd", score_bf, key_split, preferred_element_type=jnp.float32
    )
    key_part = score_scale * jnp.einsum(
        "cgqk,qcgd->kcd", score_bf, query_heads, preferred_element_type=jnp.float32
    )
    value_part = jnp.einsum(
        "cgqk,qcgd->kcd", prob_bf, grad_heads, preferred_element_type=jnp.float32
    )
    width_rows = key_block.shape[0]
    partial_value = jnp.concatenate(
        [key_part.reshape(width_rows, -1), value_part.reshape(width_rows, -1)], axis=1
    )
    return (query_part, partial_value)


def on_device(inputs, w_key, values, queries, d_out, doc_lens, block_pos):
    local_rows = inputs.shape[0]
    kv_heads = values.shape[1] // HD
    group_size = queries.shape[1] // (kv_heads * HD)
    kv_columns = kv_heads * HD
    score_scale = 1.0 / math.sqrt(HD)
    key_rows = jnp.dot(inputs, w_key, preferred_element_type=jnp.float32).astype(jnp.bfloat16)
    all_keys, all_values, all_blocks = (
        lax.all_gather(key_rows, "dp", axis=0, tiled=True),
        lax.all_gather(values, "dp", axis=0, tiled=True),
        lax.all_gather(block_pos, "dp", axis=0, tiled=True),
    )
    key_pos = row_positions(all_blocks)
    key_doc = documents(key_pos, doc_lens)
    query_pos = row_positions(block_pos)
    query_doc = documents(query_pos, doc_lens)
    query_heads = queries.reshape(local_rows, kv_heads, group_size, HD)
    grad_heads = d_out.reshape(local_rows, kv_heads, group_size, HD)
    total_rows = all_keys.shape[0]
    key_width = math.gcd(512, total_rows)
    stat_shape = (kv_heads, group_size, local_rows)

    def mask_for(first_row, width_rows):
        pos_here = lax.dynamic_slice_in_dim(key_pos, first_row, width_rows, 0)
        doc_here = lax.dynamic_slice_in_dim(key_doc, first_row, width_rows, 0)
        return (query_doc[:, None] == doc_here[None, :]) & (pos_here[None, :] <= query_pos[:, None])

    def visit_stats(block_index, running):
        first_row = block_index * key_width
        key_block = lax.dynamic_slice_in_dim(all_keys, first_row, key_width, 0)
        value_block = lax.dynamic_slice_in_dim(all_values, first_row, key_width, 0)
        allowed = mask_for(first_row, key_width)

        def visit_compute_live(state_now):
            row_max, row_sum, weighted = state_now
            scores = scored(query_heads, key_block, score_scale)
            mask_full = allowed[None, None]
            new_max = jnp.maximum(
                row_max, jnp.max(jnp.where(mask_full, scores, masked_fill), axis=3)
            )
            exp_terms = jnp.where(mask_full, jnp.exp(scores - new_max[..., None]), 0.0)
            d_prob = jnp.einsum(
                "qcgd,kcd->cgqk",
                grad_heads,
                split_heads(value_block, kv_heads),
                preferred_element_type=jnp.float32,
            )
            shrink = jnp.exp(row_max - new_max)
            return (
                new_max,
                row_sum * shrink + jnp.sum(exp_terms, axis=3),
                weighted * shrink + jnp.sum(exp_terms * d_prob, axis=3),
            )

        return lax.cond(jnp.any(allowed), visit_compute_live, lambda state_now: state_now, running)

    start_state = (
        jnp.full(stat_shape, masked_fill, jnp.float32),
        jnp.zeros(stat_shape, jnp.float32),
        jnp.zeros(stat_shape, jnp.float32),
    )
    row_max, row_sum, weighted = lax.fori_loop(0, total_rows // key_width, visit_stats, start_state)
    delta = weighted / row_sum

    def block_work(key_block, value_block, allowed):
        width_rows = key_block.shape[0]

        def block_compute_live(operands):
            return contributions(
                query_heads,
                grad_heads,
                operands[0],
                operands[1],
                operands[2],
                row_max,
                row_sum,
                delta,
                score_scale,
            )

        def dead_block(operands):
            return (
                jnp.zeros((local_rows, kv_heads, group_size, HD), jnp.float32),
                jnp.zeros((width_rows, 2 * kv_columns), jnp.float32),
            )

        return lax.cond(
            jnp.any(allowed), block_compute_live, dead_block, (key_block, value_block, allowed)
        )

    query_start = jnp.zeros((local_rows, kv_heads, group_size, HD), jnp.float32)

    def visit_block(block_index, running):
        query_sum, buffer_rows = running
        first_row = block_index * key_width
        key_block = lax.dynamic_slice_in_dim(all_keys, first_row, key_width, 0)
        value_block = lax.dynamic_slice_in_dim(all_values, first_row, key_width, 0)
        query_part, partial_value = block_work(
            key_block, value_block, mask_for(first_row, key_width)
        )
        return (
            query_sum + query_part,
            lax.dynamic_update_slice_in_dim(buffer_rows, partial_value, first_row, 0),
        )

    empty_buffer = jnp.zeros((total_rows, 2 * kv_columns), jnp.float32)
    query_sum, buffer_rows = lax.fori_loop(
        0, total_rows // key_width, visit_block, (query_start, empty_buffer)
    )
    arrived = lax.all_to_all(
        buffer_rows.astype(jnp.bfloat16), "dp", split_axis=0, concat_axis=0, tiled=True
    ).astype(buffer_rows.dtype)
    own_sums = jnp.sum(arrived.reshape(-1, local_rows, 2 * kv_columns), axis=0)
    d_query = query_sum.astype(jnp.bfloat16).reshape(local_rows, kv_columns * group_size)
    key_grad = own_sums[:, :kv_columns].astype(jnp.bfloat16)
    d_value = own_sums[:, kv_columns:].astype(jnp.bfloat16)
    d_wkey = lax.psum_scatter(
        lax.dot_general(
            inputs, key_grad, (((0,), (0,)), ((), ())), preferred_element_type=jnp.float32
        ),
        "dp",
        scatter_dimension=0,
        tiled=True,
    )
    partial_input = lax.dot_general(
        key_grad, w_key, (((1,), (1,)), ((), ())), preferred_element_type=jnp.float32
    )
    d_input = lax.psum_scatter(
        partial_input.astype(jnp.bfloat16), "tensor", scatter_dimension=1, tiled=True
    )
    return (d_query, d_value, d_input, d_wkey)


CORE, Z_HI = 1, 8
GROUP = 4
ROWS = 128
TILE = 256
UNROLLED = 5
ATTEND_COST = 4_000_000_000
PART = 512
MARKED = ROWS + 16
Q_BLOCKS = GROUP * ROWS // BLK
SMEM = pltpu.SMEM
VMEM = pltpu.VMEM
HBM = pltpu.HBM
DMA = pltpu.SemaphoreType.DMA


def swap(array, mask):
    return lax.ppermute(array, "dp", [(i, i ^ mask) for i in range(16)])


def swap_tensor(array):
    return lax.ppermute(array, "tensor", [(0, 1), (1, 0)])


def own_head():
    return (lax.axis_index("dp") >> 1) & 3


def columns(index, width):
    return pl.ds(pl.multiple_of(index * width, width), width)


def whole_spec(space=VMEM):
    return pl.BlockSpec(memory_space=space)


def after(array, *earlier):
    return lax.optimization_barrier((array,) + earlier)[0]


def copy_all(pairs, semaphores):
    copies = [
        pltpu.make_async_copy(source, target, semaphores.at[i])
        for i, (source, target) in enumerate(pairs)
    ]
    for copy in copies:
        copy.start()
    return copies


def project_keys(pos_ref, inputs_ref, values_ref, w_ref, *refs):
    pair_refs = refs[:GROUP]
    inputs, weights, total, semaphores = refs[GROUP:]
    head = own_head()
    spans = [pl.ds(k * PART, PART) for k in range(weights.shape[0] // PART)]
    copies = copy_all(
        [(inputs_ref, inputs)] + [(w_ref.at[span], weights.at[span]) for span in spans],
        semaphores,
    )
    lanes = lax.broadcasted_iota(jnp.int32, (16, 2 * HD), 1)
    marks = jnp.where(lanes == 0, pos_ref[0], jnp.where(lanes == 1, pos_ref[1], 0))
    for m in range(GROUP):
        pair_refs[m][:ROWS, HD:] = values_ref[:, columns(head ^ m, HD)]
        pair_refs[m][ROWS:] = marks.astype(jnp.float32).astype(jnp.bfloat16)
    copies[0].wait()
    for k, span in enumerate(spans):
        copies[1 + k].wait()
        part = jnp.dot(inputs[:, span], weights[span], preferred_element_type=jnp.float32)
        total[...] = part if k == 0 else total[...] + part
    for m in range(GROUP):
        pair_refs[m][:ROWS, :HD] = total[:, columns(head ^ m, HD)].astype(jnp.bfloat16)


def pack_rows(queries_ref, grads_ref, *out_refs):
    head = own_head()
    for m, out_ref in enumerate(out_refs):
        span = columns(head ^ m, GROUP * HD)
        out_ref[:, : GROUP * HD] = queries_ref[:, span]
        out_ref[:, GROUP * HD :] = grads_ref[:, span]


def pack_weights(w_ref, leaving_ref, semaphore):
    first = (1 - lax.axis_index("tensor")) * 2 + (lax.axis_index("dp") & 1)
    copy = pltpu.make_async_copy(w_ref.at[columns(first, 2 * PART)], leaving_ref, semaphore)
    copy.start()
    copy.wait()


def pack_features(inputs_ref, near_ref, far_ref):
    chip = lax.axis_index("dp") >> 1
    side = lax.axis_index("tensor")
    for m in range(GROUP):
        near_ref[m] = inputs_ref[:, columns(2 * (chip ^ m) + side, 256)]
        far_ref[m] = inputs_ref[:, columns(2 * (chip ^ (m + GROUP)) + side, 256)]


def join_features(near_ref, far_ref, *joined_refs):
    for m, joined_ref in enumerate(joined_refs):
        joined_ref[0] = near_ref[m]
        joined_ref[1] = far_ref[m]


def turn_features(*refs):
    for j in range(2 * GROUP):
        turned = refs[j % GROUP][j // GROUP].astype(jnp.float32).T
        refs[-1][:, j * ROWS : (j + 1) * ROWS] = turned.astype(jnp.bfloat16)


def dot_nt(left, right):
    return lax.dot_general(
        left, right, (((1,), (1,)), ((), ())), preferred_element_type=jnp.float32
    )


def folded(array, reduce):
    return reduce(array.reshape(-1, 8, array.shape[-1]), axis=0)


def first_row_of(positions):
    def first_row(block):
        return pl.multiple_of(positions[block // 2, block % 2] * BLK, BLK)

    return first_row


def attend_rows(
    first_part, first_row, lens_ref, row_refs, dq_refs, keys, keys_t, values, dk, dv, scratch
):
    q_rows, g_rows, dq_all, scores, d_prob = scratch
    score_scale = 1.0 / math.sqrt(HD)
    base_two = score_scale * math.log2(math.e)
    parts = len(row_refs)
    for block in range(2 * parts):
        here = pl.ds(block % 2 * BLK, BLK)
        for h in range(GROUP):
            there = pl.ds(h * BLK, BLK)
            q_rows[block, there] = row_refs[block // 2][here, h * HD : (h + 1) * HD]
            g_rows[block, there] = row_refs[block // 2][
                here, (GROUP + h) * HD : (GROUP + h + 1) * HD
            ]
    starts = [lens_ref[0]]
    for k in (1, 2):
        starts.append(starts[-1] + lens_ref[k])

    def document_start(position):
        found = jnp.zeros_like(position)
        for start in starts:
            found = jnp.where(start <= position, start, found)
        return found

    zeros = jnp.zeros((8, GROUP * BLK), jnp.float32)
    last_tile = keys.shape[0] - TILE

    @pl.loop(0, parts)
    def _(part):
        blocks = [2 * part, 2 * part + 1]
        firsts = [first_row(2 * first_part + block) for block in blocks]
        lanes = lax.broadcasted_iota(jnp.int32, (1, GROUP * BLK), 1)
        positions = [first + (lanes & (BLK - 1)) for first in firsts]
        row_starts = [document_start(position) for position in positions]
        lows = [document_start(first) // HD * HD for first in firsts]
        counts = [
            (first + BLK - low + TILE - 1) // TILE for first, low in zip(firsts, lows)
        ]
        count = jnp.maximum(*counts)

        def rows_of(j, k):
            offset = jnp.minimum(lows[j] + k * TILE, last_tile)
            return pl.ds(pl.multiple_of(offset, HD), TILE)

        def run(over_tiles):
            query = [q_rows[block] for block in blocks]
            grad = [g_rows[block] for block in blocks]

            def visit_scores(k, row_max):
                seen = []
                for j in range(2):
                    here = rows_of(j, k)
                    raw = dot_nt(keys[here], query[j])
                    row = lows[j] + k * TILE + lax.broadcasted_iota(jnp.int32, raw.shape, 0)
                    allowed = (row <= positions[j]) & (row >= row_starts[j])
                    raw = jnp.where(allowed, raw, masked_fill)
                    scores[j, k] = raw
                    d_prob[j, k] = dot_nt(values[here], grad[j])
                    seen.append(jnp.maximum(row_max[j], folded(raw, jnp.max)))
                return seen

            row_max = over_tiles(visit_scores, [zeros + masked_fill] * 2)
            row_max = [jnp.max(part_max, axis=0, keepdims=True) for part_max in row_max]

            def visit_sums(k, running):
                sums = []
                for j in range(2):
                    terms = jnp.exp2((scores[j, k] - row_max[j]) * base_two)
                    scores[j, k] = terms
                    sums.append(running[2 * j] + folded(terms, jnp.sum))
                    sums.append(running[2 * j + 1] + folded(terms * d_prob[j, k], jnp.sum))
                return sums

            sums = over_tiles(visit_sums, [zeros] * 4)
            sums = [jnp.sum(part_sum, axis=0, keepdims=True) for part_sum in sums]
            inverse = [1.0 / sums[2 * j] for j in range(2)]
            delta = [sums[2 * j + 1] * inverse[j] for j in range(2)]

            def visit_grads(k, dq):
                added = []
                for j in range(2):
                    here = rows_of(j, k)
                    prob = scores[j, k] * inverse[j]
                    score_bf = (prob * (d_prob[j, k] - delta[j])).astype(jnp.bfloat16)
                    dk[here] += jnp.dot(score_bf, query[j], preferred_element_type=jnp.float32)
                    dv[here] += jnp.dot(
                        prob.astype(jnp.bfloat16), grad[j], preferred_element_type=jnp.float32
                    )
                    added.append(
                        dq[j]
                        + jnp.dot(
                            keys_t[:, here], score_bf, preferred_element_type=jnp.float32
                        )
                    )
                return added

            dq = over_tiles(visit_grads, [jnp.zeros((HD, GROUP * BLK), jnp.float32)] * 2)
            for j in range(2):
                turned = (dq[j] * score_scale).T.astype(jnp.bfloat16)
                for h in range(GROUP):
                    dq_all[blocks[j], :, h * HD : (h + 1) * HD] = turned[h * BLK : (h + 1) * BLK]

        for fixed in range(1, UNROLLED + 1):

            @pl.when(count == fixed)
            def _(fixed=fixed):
                def over_tiles(visit, running):
                    for k in range(fixed):
                        running = visit(k, running)
                    return running

                run(over_tiles)

        @pl.when(count > UNROLLED)
        def _():
            run(lambda visit, running: lax.fori_loop(0, count, visit, running))

    for block in range(2 * parts):
        dq_refs[block // 2][pl.ds(block % 2 * BLK, BLK)] = dq_all[block]


def attend_first(lens_ref, *refs):
    row_refs, refs = refs[: GROUP - 1], refs[GROUP - 1 :]
    own_a, own_b, far_a, far_b, core_pairs, refs = *refs[:5], refs[5:]
    dq_refs, refs = refs[: GROUP - 1], refs[GROUP - 1 :]
    keys, keys_t, values, dk, dv, marks, refs = *refs[:6], refs[6:]
    scratch, (positions, semaphore) = refs[:5], refs[5:]
    reach = 2 * MARKED
    pair_refs = [own_a, own_b]
    pair_refs += [core_pairs.at[pl.ds(k * reach, reach)] for k in range(2)]
    pair_refs += [far_a, far_b]
    pair_refs += [core_pairs.at[pl.ds(k * reach, reach)] for k in range(2, 4)]
    for part in range(4 * GROUP):
        here = pl.ds(part % 2 * MARKED + ROWS, 16)
        row = pair_refs[part // 2][here, :HD].astype(jnp.float32).astype(jnp.int32)
        marks[part : part + 1] = row[:1]
    to_scalars = pltpu.make_async_copy(marks, positions, semaphore)
    to_scalars.start()
    dk[...] = jnp.zeros_like(dk)
    dv[...] = jnp.zeros_like(dv)
    to_scalars.wait()
    first_row = first_row_of(positions)
    for block in range(4 * Q_BLOCKS):
        part = block // 2
        here = pl.ds(part % 2 * MARKED + block % 2 * BLK, BLK)
        there = pl.ds(first_row(block), BLK)
        keys[there] = pair_refs[part // 2][here, :HD]
        values[there] = pair_refs[part // 2][here, HD:]
    beyond = pl.ds(4 * GROUP * ROWS, HD)
    keys[beyond] = jnp.zeros((HD, HD), jnp.bfloat16)
    keys_t[:, beyond] = jnp.zeros((HD, HD), jnp.bfloat16)
    values[beyond] = jnp.zeros((HD, HD), jnp.bfloat16)
    for tile in range(keys.shape[0] // TILE):
        here = pl.ds(tile * TILE, TILE)
        keys_t[:, here] = keys[here].astype(jnp.float32).T.astype(jnp.bfloat16)
    attend_rows(
        0, first_row, lens_ref, row_refs, dq_refs, keys, keys_t, values, dk, dv, scratch
    )


def attend_last(lens_ref, row_ref, keys, keys_t, values, dk_first, dv_first, marks, *refs):
    dq_ref, kept, sent, dk, dv, refs = *refs[:5], refs[5:]
    scratch, (positions, semaphore) = refs[:5], refs[5:]
    score_scale = 1.0 / math.sqrt(HD)
    to_scalars = pltpu.make_async_copy(marks, positions, semaphore)
    to_scalars.start()
    dk[...] = dk_first[...]
    dv[...] = dv_first[...]
    to_scalars.wait()
    first_row = first_row_of(positions)
    attend_rows(
        GROUP - 1, first_row, lens_ref, [row_ref], [dq_ref], keys, keys_t, values, dk, dv, scratch
    )
    for block in range(4 * Q_BLOCKS):
        quarter = block // Q_BLOCKS
        here = pl.ds(quarter // 2 * Q_BLOCKS * BLK + block % Q_BLOCKS * BLK, BLK)
        there = pl.ds(first_row(block), BLK)
        out_ref = sent if quarter % 2 else kept
        out_ref[here, :HD] = dk[there] * score_scale
        out_ref[here, HD:] = dv[there]


def weight_grad(own_ref, other_ref, *refs):
    grad_refs, (keep_ref, send_ref, grads) = refs[:GROUP], refs[GROUP:]
    head = own_head()
    for k, grad_ref in enumerate(grad_refs):
        for far in range(2):
            for m in range(GROUP):
                here = pl.ds((far * GROUP + m) * ROWS, ROWS)
                there = pl.ds((far * GROUP + (m ^ k)) * ROWS, ROWS)
                grads[here, columns(head ^ k, HD)] = grad_ref[there]
    own = jnp.dot(own_ref[...], grads[...], preferred_element_type=jnp.float32)
    other = jnp.dot(other_ref[...], grads[...], preferred_element_type=jnp.float32)
    crossed = (lax.axis_index("dp") & 1) ^ lax.axis_index("tensor")

    @pl.when(crossed == 0)
    def _():
        keep_ref[...] = own
        send_ref[...] = other

    @pl.when(crossed == 1)
    def _():
        keep_ref[...] = other
        send_ref[...] = own


def input_grad(own_ref, other_ref, w_own, w_near, w_far, out_ref, own_all, other_all):
    head = own_head()
    core = lax.axis_index("dp") & 1
    side = lax.axis_index("tensor")
    for k in range(GROUP):
        own_all[:, columns(head ^ k, HD)] = own_ref[k]
        other_all[:, columns(head ^ k, HD)] = other_ref[k]
    for k in range(4):
        chunk = 2 * (core ^ (k // 2)) + k % 2
        w_other = (w_near, w_far)[k // 2][pl.ds(k % 2 * PART, PART)]
        part = dot_nt(own_all[...], w_own[columns(side * 4 + chunk, PART)])
        part = part + dot_nt(other_all[...], w_other)
        out_ref[:, columns(chunk, PART)] = part.astype(jnp.bfloat16)


def sum_cores(kept_ref, arrived_ref, dk_ref, dk_bf_ref, *dv_refs):
    dk = kept_ref[:, :HD] + arrived_ref[:, :HD]
    dk_ref[...] = dk
    dk_bf_ref[...] = dk.astype(jnp.bfloat16)
    for m, dv_ref in enumerate(dv_refs):
        for far in range(2):
            here = pl.ds((far * GROUP + m) * ROWS, ROWS)
            dv_ref[far] = (kept_ref[here, HD:] + arrived_ref[here, HD:]).astype(jnp.bfloat16)


def sum_halves(near_ref, far_ref, out_ref):
    quarter = GROUP * ROWS
    for k in range(2):
        here, there = pl.ds(k * quarter, quarter), pl.ds((1 - k) * quarter, quarter)
        total = near_ref[here] + far_ref[there].astype(jnp.float32)
        out_ref[here] = total.astype(jnp.bfloat16)


def finish(keep_ref, arrived_ref, far_ref, *refs):
    row_refs, value_refs, refs = refs[:GROUP], refs[GROUP : 2 * GROUP], refs[2 * GROUP :]
    weight_out, query_out, value_out = refs
    head = own_head()
    weight_out[...] = keep_ref[...] + arrived_ref[...]
    for m in range(GROUP):
        query_out[:, columns(head ^ m, GROUP * HD)] = row_refs[m][...]
        value = value_refs[m][0].astype(jnp.float32) + far_ref[m].astype(jnp.float32)
        value_out[:, columns(head ^ m, HD)] = value.astype(jnp.bfloat16)


def shaped(shape, dtype=jnp.bfloat16):
    return jax.ShapeDtypeStruct(shape, dtype)


def limits(mebibytes):
    return pltpu.CompilerParams(vmem_limit_bytes=mebibytes << 20)


def with_partners(arrays):
    return [arrays[0]] + [swap(arrays[m], 2 * m) for m in range(1, len(arrays))]


def on_device_by_heads(inputs, w_key, values, queries, d_out, doc_lens, block_pos):
    features = inputs.shape[1]
    kv_columns = values.shape[1]
    total_rows = 16 * ROWS
    half = total_rows // 2
    vmem, smem, hbm = whole_spec(), whole_spec(SMEM), whole_spec(HBM)

    pairs = pl.pallas_call(
        project_keys,
        out_shape=[shaped((MARKED, 2 * HD))] * GROUP,
        in_specs=[smem, hbm, vmem, hbm],
        out_specs=[vmem] * GROUP,
        scratch_shapes=[
            VMEM((ROWS, features), jnp.bfloat16),
            VMEM((features, kv_columns), jnp.bfloat16),
            VMEM((ROWS, kv_columns), jnp.float32),
            DMA((1 + features // PART,)),
        ],
        compiler_params=limits(60),
        cost_estimate=pl.CostEstimate(
            flops=2 * ROWS * features * kv_columns,
            bytes_accessed=features * kv_columns * 2,
            transcendentals=0,
        ),
        name="project_keys",
    )(block_pos, inputs, values, w_key)

    packed_rows = pl.pallas_call(
        pack_rows,
        out_shape=[shaped((ROWS, 2 * GROUP * HD))] * GROUP,
        in_specs=[vmem] * 2,
        out_specs=[vmem] * GROUP,
        compiler_params=limits(8),
        name="pack_rows",
    )(after(queries, pairs[0]), d_out)

    pairs = [after(pairs[0], packed_rows[0])] + list(pairs[1:])
    pairs = with_partners(pairs)
    own_a = jnp.concatenate(pairs[:2], axis=0)
    own_b = jnp.concatenate(pairs[2:], axis=0)
    far_a = swap(own_a, Z_HI)
    far_b = swap(own_b, Z_HI)
    rows = with_partners(packed_rows)

    near_features, far_features = pl.pallas_call(
        pack_features,
        out_shape=[shaped((GROUP, ROWS, 256))] * 2,
        in_specs=[vmem],
        out_specs=[vmem] * 2,
        compiler_params=limits(8),
        name="pack_features",
    )(after(inputs, own_a))
    leaving = pl.pallas_call(
        pack_weights,
        out_shape=shaped((2 * PART, kv_columns)),
        in_specs=[hbm],
        out_specs=vmem,
        scratch_shapes=[DMA],
        compiler_params=limits(56),
        name="pack_weights",
    )(after(w_key, own_b))
    w_near = swap_tensor(leaving)
    near_pairs = jnp.concatenate([own_a, own_b, far_a, far_b], axis=0)
    core_pairs = swap(after(near_pairs, near_features, leaving, rows[1], rows[2]), CORE)
    far_features = swap(far_features, Z_HI)

    row_grad = shaped((ROWS, GROUP * HD))
    padded_rows = total_rows + HD
    sorted_rows = shaped((padded_rows, HD))
    sums = shaped((padded_rows, HD), jnp.float32)
    half_sums = shaped((half, 2 * HD), jnp.float32)

    def attend_scratch(blocks):
        stacked = VMEM((blocks, GROUP * BLK, HD), jnp.bfloat16)
        tiles = VMEM((2, total_rows // TILE, TILE, GROUP * BLK), jnp.float32)
        return [
            stacked,
            stacked,
            VMEM((blocks, BLK, GROUP * HD), jnp.bfloat16),
            tiles,
            tiles,
            SMEM((4 * GROUP, HD), jnp.int32),
            DMA,
        ]

    *row_grads, keys, keys_t, all_values, dk_first, dv_first, marks = pl.pallas_call(
        attend_first,
        out_shape=[row_grad] * (GROUP - 1)
        + [sorted_rows, shaped((HD, padded_rows)), sorted_rows, sums, sums]
        + [shaped((4 * GROUP, HD), jnp.int32)],
        in_specs=[smem] + [vmem] * (GROUP + 4),
        out_specs=[vmem] * (GROUP + 5),
        scratch_shapes=attend_scratch(Q_BLOCKS - 2),
        compiler_params=limits(24),
        cost_estimate=pl.CostEstimate(flops=ATTEND_COST, bytes_accessed=0, transcendentals=0),
        name="attend_first",
    )(doc_lens, *rows[:-1], own_a, own_b, far_a, far_b, core_pairs)
    last_grad, kept, sent = pl.pallas_call(
        attend_last,
        out_shape=[row_grad, half_sums, half_sums],
        in_specs=[smem] + [vmem] * 7,
        out_specs=[vmem] * 3,
        scratch_shapes=[VMEM((padded_rows, HD), jnp.float32)] * 2 + attend_scratch(2),
        compiler_params=limits(24),
        cost_estimate=pl.CostEstimate(flops=ATTEND_COST, bytes_accessed=0, transcendentals=0),
        name="attend_last",
    )(doc_lens, after(rows[-1], w_near), keys, keys_t, all_values, dk_first, dv_first, marks)

    row_grads = with_partners(row_grads)
    sent = after(sent, far_features, *row_grads)
    dk_sum, dk_near, *value_grads = pl.pallas_call(
        sum_cores,
        out_shape=[shaped((half, HD), jnp.float32), shaped((half, HD))]
        + [shaped((2, ROWS, HD))] * GROUP,
        in_specs=[vmem] * 2,
        out_specs=[vmem] * (2 + GROUP),
        compiler_params=limits(16),
        name="sum_cores",
    )(kept, swap(sent, CORE))
    dk_far = swap(dk_near, Z_HI)
    w_far = swap(after(w_near, sent), CORE)
    value_grads = with_partners(value_grads)
    value_far = jnp.stack([grad[1] for grad in value_grads])

    feature_parts = pl.pallas_call(
        join_features,
        out_shape=[shaped((2, ROWS, 256))] * GROUP,
        in_specs=[vmem] * 2,
        out_specs=[vmem] * GROUP,
        compiler_params=limits(16),
        name="join_features",
    )(after(near_features, sent), far_features)
    own_features = pl.pallas_call(
        turn_features,
        out_shape=shaped((256, half)),
        in_specs=[vmem] * GROUP,
        out_specs=vmem,
        compiler_params=limits(16),
        cost_estimate=pl.CostEstimate(flops=1_000_000_000, bytes_accessed=0, transcendentals=0),
        name="turn_features",
    )(*with_partners(feature_parts))
    other_features = swap_tensor(own_features)

    key_grad = pl.pallas_call(
        sum_halves,
        out_shape=shaped((half, HD)),
        in_specs=[vmem] * 2,
        out_specs=vmem,
        compiler_params=limits(8),
        cost_estimate=pl.CostEstimate(flops=1_000_000, bytes_accessed=0, transcendentals=0),
        name="sum_halves",
    )(dk_sum, dk_far)
    key_grad = after(key_grad, own_features, value_far, w_far)
    key_grads = with_partners([key_grad] * GROUP)
    own_key_grad = jnp.stack([key_grads[m][m * ROWS : (m + 1) * ROWS] for m in range(GROUP)])
    other_key_grad = swap_tensor(own_key_grad)

    value_far = swap(after(value_far, key_grad), Z_HI)
    last_grad = swap(after(last_grad, own_key_grad), 6)

    keep, send = pl.pallas_call(
        weight_grad,
        out_shape=[shaped((256, kv_columns), jnp.float32)] * 2,
        in_specs=[vmem] * (2 + GROUP),
        out_specs=[vmem] * 2,
        scratch_shapes=[VMEM((half, kv_columns), jnp.bfloat16)],
        compiler_params=limits(24),
        cost_estimate=pl.CostEstimate(
            flops=4 * 256 * half * kv_columns, bytes_accessed=4 << 20, transcendentals=0
        ),
        name="weight_grad",
    )(after(own_features, value_far), other_features, *key_grads)
    arrived = swap(send, CORE)

    d_input = pl.pallas_call(
        input_grad,
        out_shape=shaped((ROWS, features // 2)),
        in_specs=[vmem] * 5,
        out_specs=vmem,
        scratch_shapes=[VMEM((ROWS, kv_columns), jnp.bfloat16)] * 2,
        compiler_params=limits(16),
        cost_estimate=pl.CostEstimate(
            flops=8_000_000_000, bytes_accessed=5 << 20, transcendentals=0
        ),
        name="input_grad",
    )(after(own_key_grad, send), other_key_grad, w_key, w_near, w_far)

    d_wkey, d_query, d_value = pl.pallas_call(
        finish,
        out_shape=[
            shaped((256, kv_columns), jnp.float32),
            shaped(queries.shape),
            shaped(values.shape),
        ],
        in_specs=[vmem] * (3 + 2 * GROUP),
        out_specs=[vmem] * 3,
        compiler_params=limits(16),
        name="finish",
    )(after(keep, d_input), arrived, value_far, *row_grads, last_grad, *value_grads)
    return (d_query, d_value, d_input, d_wkey)


def solution(mesh):
    by_heads = mesh.shape["dp"] == 16 and mesh.shape["tensor"] == 2
    return jax.shard_map(
        on_device_by_heads if by_heads else on_device,
        mesh=mesh,
        in_specs=(
            P("dp", None),
            P(None, "tensor"),
            P("dp", "tensor"),
            P("dp", "tensor"),
            P("dp", "tensor"),
            P(),
            P("dp"),
        ),
        out_specs=(P("dp", "tensor"), P("dp", "tensor"), P("dp", "tensor"), P("dp", "tensor")),
        check_vma=False,
    )
```

```python
import math

import jax
import jax.numpy as jnp
from jax import lax
from jax.experimental import pallas as pl
from jax.experimental.pallas import tpu as pltpu
from jax.sharding import PartitionSpec as P

HD = 128
BLK = 64


masked_fill = -1e30


def row_positions(block_pos):
    within = jnp.tile(jnp.arange(BLK, dtype=jnp.int32), block_pos.shape[0])
    return jnp.repeat(block_pos, BLK) * BLK + within


def documents(positions, doc_lens):
    starts = jnp.cumsum(doc_lens) - doc_lens
    return jnp.sum((positions[:, None] >= starts[None, :]).astype(jnp.int32), axis=1) - 1


def split_heads(block_rows, kv_heads):
    return block_rows.reshape(block_rows.shape[0], kv_heads, HD)


def scored(query_heads, key_block, score_scale):
    key_split = split_heads(key_block, query_heads.shape[1])
    return (
        jnp.einsum("qcgd,kcd->cgqk", query_heads, key_split, preferred_element_type=jnp.float32)
        * score_scale
    )


def contributions(
    query_heads, grad_heads, key_block, value_block, allowed, row_max, row_sum, delta, score_scale
):
    kv_heads = query_heads.shape[1]
    key_split = split_heads(key_block, kv_heads)
    value_split = split_heads(value_block, kv_heads)
    scores = scored(query_heads, key_block, score_scale)
    mask_full = allowed[None, None]
    probabilities = (
        jnp.where(mask_full, jnp.exp(scores - row_max[..., None]), 0.0) / row_sum[..., None]
    )
    d_prob = jnp.einsum(
        "qcgd,kcd->cgqk", grad_heads, value_split, preferred_element_type=jnp.float32
    )
    d_score = probabilities * (d_prob - delta[..., None])
    prob_bf = probabilities.astype(jnp.bfloat16)
    score_bf = d_score.astype(jnp.bfloat16)
    query_part = score_scale * jnp.einsum(
        "cgqk,kcd->qcgd", score_bf, key_split, preferred_element_type=jnp.float32
    )
    key_part = score_scale * jnp.einsum(
        "cgqk,qcgd->kcd", score_bf, query_heads, preferred_element_type=jnp.float32
    )
    value_part = jnp.einsum(
        "cgqk,qcgd->kcd", prob_bf, grad_heads, preferred_element_type=jnp.float32
    )
    width_rows = key_block.shape[0]
    partial_value = jnp.concatenate(
        [key_part.reshape(width_rows, -1), value_part.reshape(width_rows, -1)], axis=1
    )
    return (query_part, partial_value)


def on_device(inputs, w_key, values, queries, d_out, doc_lens, block_pos):
    local_rows = inputs.shape[0]
    kv_heads = values.shape[1] // HD
    group_size = queries.shape[1] // (kv_heads * HD)
    kv_columns = kv_heads * HD
    score_scale = 1.0 / math.sqrt(HD)
    key_rows = jnp.dot(inputs, w_key, preferred_element_type=jnp.float32).astype(jnp.bfloat16)
    all_keys, all_values, all_blocks = (
        lax.all_gather(key_rows, "dp", axis=0, tiled=True),
        lax.all_gather(values, "dp", axis=0, tiled=True),
        lax.all_gather(block_pos, "dp", axis=0, tiled=True),
    )
    key_pos = row_positions(all_blocks)
    key_doc = documents(key_pos, doc_lens)
    query_pos = row_positions(block_pos)
    query_doc = documents(query_pos, doc_lens)
    query_heads = queries.reshape(local_rows, kv_heads, group_size, HD)
    grad_heads = d_out.reshape(local_rows, kv_heads, group_size, HD)
    total_rows = all_keys.shape[0]
    key_width = math.gcd(512, total_rows)
    stat_shape = (kv_heads, group_size, local_rows)

    def mask_for(first_row, width_rows):
        pos_here = lax.dynamic_slice_in_dim(key_pos, first_row, width_rows, 0)
        doc_here = lax.dynamic_slice_in_dim(key_doc, first_row, width_rows, 0)
        return (query_doc[:, None] == doc_here[None, :]) & (pos_here[None, :] <= query_pos[:, None])

    def visit_stats(block_index, running):
        first_row = block_index * key_width
        key_block = lax.dynamic_slice_in_dim(all_keys, first_row, key_width, 0)
        value_block = lax.dynamic_slice_in_dim(all_values, first_row, key_width, 0)
        allowed = mask_for(first_row, key_width)

        def visit_compute_live(state_now):
            row_max, row_sum, weighted = state_now
            scores = scored(query_heads, key_block, score_scale)
            mask_full = allowed[None, None]
            new_max = jnp.maximum(
                row_max, jnp.max(jnp.where(mask_full, scores, masked_fill), axis=3)
            )
            exp_terms = jnp.where(mask_full, jnp.exp(scores - new_max[..., None]), 0.0)
            d_prob = jnp.einsum(
                "qcgd,kcd->cgqk",
                grad_heads,
                split_heads(value_block, kv_heads),
                preferred_element_type=jnp.float32,
            )
            shrink = jnp.exp(row_max - new_max)
            return (
                new_max,
                row_sum * shrink + jnp.sum(exp_terms, axis=3),
                weighted * shrink + jnp.sum(exp_terms * d_prob, axis=3),
            )

        return lax.cond(jnp.any(allowed), visit_compute_live, lambda state_now: state_now, running)

    start_state = (
        jnp.full(stat_shape, masked_fill, jnp.float32),
        jnp.zeros(stat_shape, jnp.float32),
        jnp.zeros(stat_shape, jnp.float32),
    )
    row_max, row_sum, weighted = lax.fori_loop(0, total_rows // key_width, visit_stats, start_state)
    delta = weighted / row_sum

    def block_work(key_block, value_block, allowed):
        width_rows = key_block.shape[0]

        def block_compute_live(operands):
            return contributions(
                query_heads,
                grad_heads,
                operands[0],
                operands[1],
                operands[2],
                row_max,
                row_sum,
                delta,
                score_scale,
            )

        def dead_block(operands):
            return (
                jnp.zeros((local_rows, kv_heads, group_size, HD), jnp.float32),
                jnp.zeros((width_rows, 2 * kv_columns), jnp.float32),
            )

        return lax.cond(
            jnp.any(allowed), block_compute_live, dead_block, (key_block, value_block, allowed)
        )

    query_start = jnp.zeros((local_rows, kv_heads, group_size, HD), jnp.float32)

    def visit_block(block_index, running):
        query_sum, buffer_rows = running
        first_row = block_index * key_width
        key_block = lax.dynamic_slice_in_dim(all_keys, first_row, key_width, 0)
        value_block = lax.dynamic_slice_in_dim(all_values, first_row, key_width, 0)
        query_part, partial_value = block_work(
            key_block, value_block, mask_for(first_row, key_width)
        )
        return (
            query_sum + query_part,
            lax.dynamic_update_slice_in_dim(buffer_rows, partial_value, first_row, 0),
        )

    empty_buffer = jnp.zeros((total_rows, 2 * kv_columns), jnp.float32)
    query_sum, buffer_rows = lax.fori_loop(
        0, total_rows // key_width, visit_block, (query_start, empty_buffer)
    )
    arrived = lax.all_to_all(
        buffer_rows.astype(jnp.bfloat16), "dp", split_axis=0, concat_axis=0, tiled=True
    ).astype(buffer_rows.dtype)
    own_sums = jnp.sum(arrived.reshape(-1, local_rows, 2 * kv_columns), axis=0)
    d_query = query_sum.astype(jnp.bfloat16).reshape(local_rows, kv_columns * group_size)
    key_grad = own_sums[:, :kv_columns].astype(jnp.bfloat16)
    d_value = own_sums[:, kv_columns:].astype(jnp.bfloat16)
    d_wkey = lax.psum_scatter(
        lax.dot_general(
            inputs, key_grad, (((0,), (0,)), ((), ())), preferred_element_type=jnp.float32
        ),
        "dp",
        scatter_dimension=0,
        tiled=True,
    )
    partial_input = lax.dot_general(
        key_grad, w_key, (((1,), (1,)), ((), ())), preferred_element_type=jnp.float32
    )
    d_input = lax.psum_scatter(
        partial_input.astype(jnp.bfloat16), "tensor", scatter_dimension=1, tiled=True
    )
    return (d_query, d_value, d_input, d_wkey)


CORE, Z_HI = 1, 8
GROUP = 4
ROWS = 128
TILE = 256
UNROLLED = 5
ATTEND_COST = 4_000_000_000
PART = 512
MARKED = ROWS + 16
Q_BLOCKS = GROUP * ROWS // BLK
SMEM = pltpu.SMEM
VMEM = pltpu.VMEM
HBM = pltpu.HBM
DMA = pltpu.SemaphoreType.DMA


def swap(array, mask):
    return lax.ppermute(array, "dp", [(i, i ^ mask) for i in range(16)])


def swap_tensor(array):
    return lax.ppermute(array, "tensor", [(0, 1), (1, 0)])


def own_head():
    return (lax.axis_index("dp") >> 1) & 3


def columns(index, width):
    return pl.ds(pl.multiple_of(index * width, width), width)


def whole_spec(space=VMEM):
    return pl.BlockSpec(memory_space=space)


def after(array, *earlier):
    return lax.optimization_barrier((array,) + earlier)[0]


def copy_all(pairs, semaphores):
    copies = [
        pltpu.make_async_copy(source, target, semaphores.at[i])
        for i, (source, target) in enumerate(pairs)
    ]
    for copy in copies:
        copy.start()
    return copies


def project_keys(pos_ref, inputs_ref, values_ref, w_ref, *refs):
    pair_refs = refs[:GROUP]
    inputs, weights, total, semaphores = refs[GROUP:]
    head = own_head()
    spans = [pl.ds(k * PART, PART) for k in range(weights.shape[0] // PART)]
    copies = copy_all(
        [(inputs_ref, inputs)] + [(w_ref.at[span], weights.at[span]) for span in spans],
        semaphores,
    )
    lanes = lax.broadcasted_iota(jnp.int32, (16, 2 * HD), 1)
    marks = jnp.where(lanes == 0, pos_ref[0], jnp.where(lanes == 1, pos_ref[1], 0))
    for m in range(GROUP):
        pair_refs[m][:ROWS, HD:] = values_ref[:, columns(head ^ m, HD)]
        pair_refs[m][ROWS:] = marks.astype(jnp.float32).astype(jnp.bfloat16)
    copies[0].wait()
    for k, span in enumerate(spans):
        copies[1 + k].wait()
        part = jnp.dot(inputs[:, span], weights[span], preferred_element_type=jnp.float32)
        total[...] = part if k == 0 else total[...] + part
    for m in range(GROUP):
        pair_refs[m][:ROWS, :HD] = total[:, columns(head ^ m, HD)].astype(jnp.bfloat16)


def pack_rows(queries_ref, grads_ref, *out_refs):
    head = own_head()
    for m, out_ref in enumerate(out_refs):
        span = columns(head ^ m, GROUP * HD)
        out_ref[:, : GROUP * HD] = queries_ref[:, span]
        out_ref[:, GROUP * HD :] = grads_ref[:, span]


def pack_weights(w_ref, leaving_ref, semaphore):
    first = (1 - lax.axis_index("tensor")) * 2 + (lax.axis_index("dp") & 1)
    copy = pltpu.make_async_copy(w_ref.at[columns(first, 2 * PART)], leaving_ref, semaphore)
    copy.start()
    copy.wait()


def pack_features(inputs_ref, near_ref, far_ref):
    chip = lax.axis_index("dp") >> 1
    side = lax.axis_index("tensor")
    for m in range(GROUP):
        near_ref[m] = inputs_ref[:, columns(2 * (chip ^ m) + side, 256)]
        far_ref[m] = inputs_ref[:, columns(2 * (chip ^ (m + GROUP)) + side, 256)]


def join_features(near_ref, far_ref, *joined_refs):
    for m, joined_ref in enumerate(joined_refs):
        joined_ref[0] = near_ref[m]
        joined_ref[1] = far_ref[m]


def turn_features(*refs):
    for j in range(2 * GROUP):
        turned = refs[j % GROUP][j // GROUP].astype(jnp.float32).T
        refs[-1][:, j * ROWS : (j + 1) * ROWS] = turned.astype(jnp.bfloat16)


def dot_nt(left, right):
    return lax.dot_general(
        left, right, (((1,), (1,)), ((), ())), preferred_element_type=jnp.float32
    )


def folded(array, reduce):
    return reduce(array.reshape(-1, 8, array.shape[-1]), axis=0)


def first_row_of(positions):
    def first_row(block):
        return pl.multiple_of(positions[block // 2, block % 2] * BLK, BLK)

    return first_row


def attend_rows(
    member_of, first_row, lens_ref, row_refs, dq_refs, keys, keys_t, values, dk, dv, scratch
):
    q_rows, g_rows, dq_all, scores, d_prob = scratch
    score_scale = 1.0 / math.sqrt(HD)
    base_two = score_scale * math.log2(math.e)
    parts = len(row_refs)
    for block in range(2 * parts):
        here = pl.ds(block % 2 * BLK, BLK)
        for h in range(GROUP):
            there = pl.ds(h * BLK, BLK)
            q_rows[block, there] = row_refs[block // 2][here, h * HD : (h + 1) * HD]
            g_rows[block, there] = row_refs[block // 2][
                here, (GROUP + h) * HD : (GROUP + h + 1) * HD
            ]
    starts = [lens_ref[0]]
    for k in (1, 2):
        starts.append(starts[-1] + lens_ref[k])

    def document_start(position):
        found = jnp.zeros_like(position)
        for start in starts:
            found = jnp.where(start <= position, start, found)
        return found

    zeros = jnp.zeros((8, GROUP * BLK), jnp.float32)
    last_tile = keys.shape[0] - TILE

    @pl.loop(0, parts)
    def _(part):
        blocks = [2 * part, 2 * part + 1]
        firsts = [first_row(2 * member_of(part) + j) for j in range(2)]
        lanes = lax.broadcasted_iota(jnp.int32, (1, GROUP * BLK), 1)
        positions = [first + (lanes & (BLK - 1)) for first in firsts]
        row_starts = [document_start(position) for position in positions]
        lows = [document_start(first) // HD * HD for first in firsts]
        counts = [
            (first + BLK - low + TILE - 1) // TILE for first, low in zip(firsts, lows)
        ]
        count = jnp.maximum(*counts)

        def rows_of(j, k):
            offset = jnp.minimum(lows[j] + k * TILE, last_tile)
            return pl.ds(pl.multiple_of(offset, HD), TILE)

        def run(over_tiles):
            query = [q_rows[block] for block in blocks]
            grad = [g_rows[block] for block in blocks]

            def visit_scores(k, row_max):
                seen = []
                for j in range(2):
                    here = rows_of(j, k)
                    raw = dot_nt(keys[here], query[j])
                    row = lows[j] + k * TILE + lax.broadcasted_iota(jnp.int32, raw.shape, 0)
                    allowed = (row <= positions[j]) & (row >= row_starts[j])
                    raw = jnp.where(allowed, raw, masked_fill)
                    scores[j, k] = raw
                    d_prob[j, k] = dot_nt(values[here], grad[j])
                    seen.append(jnp.maximum(row_max[j], folded(raw, jnp.max)))
                return seen

            row_max = over_tiles(visit_scores, [zeros + masked_fill] * 2)
            row_max = [jnp.max(part_max, axis=0, keepdims=True) for part_max in row_max]

            def visit_sums(k, running):
                sums = []
                for j in range(2):
                    terms = jnp.exp2((scores[j, k] - row_max[j]) * base_two)
                    scores[j, k] = terms
                    sums.append(running[2 * j] + folded(terms, jnp.sum))
                    sums.append(running[2 * j + 1] + folded(terms * d_prob[j, k], jnp.sum))
                return sums

            sums = over_tiles(visit_sums, [zeros] * 4)
            sums = [jnp.sum(part_sum, axis=0, keepdims=True) for part_sum in sums]
            inverse = [1.0 / sums[2 * j] for j in range(2)]
            delta = [sums[2 * j + 1] * inverse[j] for j in range(2)]

            def visit_grads(k, dq):
                added = []
                for j in range(2):
                    here = rows_of(j, k)
                    prob = scores[j, k] * inverse[j]
                    score_bf = (prob * (d_prob[j, k] - delta[j])).astype(jnp.bfloat16)
                    dk[here] += jnp.dot(score_bf, query[j], preferred_element_type=jnp.float32)
                    dv[here] += jnp.dot(
                        prob.astype(jnp.bfloat16), grad[j], preferred_element_type=jnp.float32
                    )
                    added.append(
                        dq[j]
                        + jnp.dot(
                            keys_t[:, here], score_bf, preferred_element_type=jnp.float32
                        )
                    )
                return added

            dq = over_tiles(visit_grads, [jnp.zeros((HD, GROUP * BLK), jnp.float32)] * 2)
            for j in range(2):
                turned = (dq[j] * score_scale).T.astype(jnp.bfloat16)
                for h in range(GROUP):
                    dq_all[blocks[j], :, h * HD : (h + 1) * HD] = turned[h * BLK : (h + 1) * BLK]

        for fixed in range(1, UNROLLED + 1):

            @pl.when(count == fixed)
            def _(fixed=fixed):
                def over_tiles(visit, running):
                    for k in range(fixed):
                        running = visit(k, running)
                    return running

                run(over_tiles)

        @pl.when(count > UNROLLED)
        def _():
            run(lambda visit, running: lax.fori_loop(0, count, visit, running))

    for block in range(2 * parts):
        dq_refs[block // 2][pl.ds(block % 2 * BLK, BLK)] = dq_all[block]


def attend_first(lens_ref, *refs):
    row_refs, refs = refs[: GROUP - 1], refs[GROUP - 1 :]
    own_a, own_b, far_a, far_b, core_pairs, refs = *refs[:5], refs[5:]
    dq_refs, refs = refs[: GROUP - 1], refs[GROUP - 1 :]
    keys, keys_t, values, dk, dv, marks, refs = *refs[:6], refs[6:]
    scratch, (positions, semaphore) = refs[:5], refs[5:]
    reach = 2 * MARKED
    pair_refs = [own_a, own_b]
    pair_refs += [core_pairs.at[pl.ds(k * reach, reach)] for k in range(2)]
    pair_refs += [far_a, far_b]
    pair_refs += [core_pairs.at[pl.ds(k * reach, reach)] for k in range(2, 4)]
    for part in range(4 * GROUP):
        here = pl.ds(part % 2 * MARKED + ROWS, 16)
        row = pair_refs[part // 2][here, :HD].astype(jnp.float32).astype(jnp.int32)
        marks[part : part + 1] = row[:1]
    to_scalars = pltpu.make_async_copy(marks, positions, semaphore)
    to_scalars.start()
    dk[...] = jnp.zeros_like(dk)
    dv[...] = jnp.zeros_like(dv)
    to_scalars.wait()
    first_row = first_row_of(positions)
    for block in range(4 * Q_BLOCKS):
        part = block // 2
        here = pl.ds(part % 2 * MARKED + block % 2 * BLK, BLK)
        there = pl.ds(first_row(block), BLK)
        keys[there] = pair_refs[part // 2][here, :HD]
        values[there] = pair_refs[part // 2][here, HD:]
    beyond = pl.ds(4 * GROUP * ROWS, HD)
    keys[beyond] = jnp.zeros((HD, HD), jnp.bfloat16)
    keys_t[:, beyond] = jnp.zeros((HD, HD), jnp.bfloat16)
    values[beyond] = jnp.zeros((HD, HD), jnp.bfloat16)
    for tile in range(keys.shape[0] // TILE):
        here = pl.ds(tile * TILE, TILE)
        keys_t[:, here] = keys[here].astype(jnp.float32).T.astype(jnp.bfloat16)
    attend_rows(
        lambda part: part + jnp.minimum(part, 1),
        first_row,
        lens_ref,
        row_refs,
        dq_refs,
        keys,
        keys_t,
        values,
        dk,
        dv,
        scratch,
    )


def attend_last(lens_ref, row_ref, keys, keys_t, values, dk_first, dv_first, marks, *refs):
    dq_ref, kept, sent, dk, dv, refs = *refs[:5], refs[5:]
    scratch, (positions, semaphore) = refs[:5], refs[5:]
    score_scale = 1.0 / math.sqrt(HD)
    to_scalars = pltpu.make_async_copy(marks, positions, semaphore)
    to_scalars.start()
    dk[...] = dk_first[...]
    dv[...] = dv_first[...]
    to_scalars.wait()
    first_row = first_row_of(positions)
    attend_rows(
        lambda part: part + 1,
        first_row,
        lens_ref,
        [row_ref],
        [dq_ref],
        keys,
        keys_t,
        values,
        dk,
        dv,
        scratch,
    )
    for block in range(4 * Q_BLOCKS):
        quarter = block // Q_BLOCKS
        here = pl.ds(quarter // 2 * Q_BLOCKS * BLK + block % Q_BLOCKS * BLK, BLK)
        there = pl.ds(first_row(block), BLK)
        out_ref = sent if quarter % 2 else kept
        out_ref[here, :HD] = dk[there] * score_scale
        out_ref[here, HD:] = dv[there]


def weight_grad(own_ref, other_ref, *refs):
    grad_refs, (keep_ref, send_ref, grads) = refs[:GROUP], refs[GROUP:]
    head = own_head()
    for k, grad_ref in enumerate(grad_refs):
        for far in range(2):
            for m in range(GROUP):
                here = pl.ds((far * GROUP + m) * ROWS, ROWS)
                there = pl.ds((far * GROUP + (m ^ k)) * ROWS, ROWS)
                grads[here, columns(head ^ k, HD)] = grad_ref[there]
    own = jnp.dot(own_ref[...], grads[...], preferred_element_type=jnp.float32)
    other = jnp.dot(other_ref[...], grads[...], preferred_element_type=jnp.float32)
    crossed = (lax.axis_index("dp") & 1) ^ lax.axis_index("tensor")

    @pl.when(crossed == 0)
    def _():
        keep_ref[...] = own
        send_ref[...] = other

    @pl.when(crossed == 1)
    def _():
        keep_ref[...] = other
        send_ref[...] = own


def input_grad(own_ref, other_ref, w_own, w_near, w_far, out_ref, own_all, other_all):
    head = own_head()
    core = lax.axis_index("dp") & 1
    side = lax.axis_index("tensor")
    for k in range(GROUP):
        own_all[:, columns(head ^ k, HD)] = own_ref[k]
        other_all[:, columns(head ^ k, HD)] = other_ref[k]
    for k in range(4):
        chunk = 2 * (core ^ (k // 2)) + k % 2
        w_other = (w_near, w_far)[k // 2][pl.ds(k % 2 * PART, PART)]
        part = dot_nt(own_all[...], w_own[columns(side * 4 + chunk, PART)])
        part = part + dot_nt(other_all[...], w_other)
        out_ref[:, columns(chunk, PART)] = part.astype(jnp.bfloat16)


def sum_cores(kept_ref, arrived_ref, dk_ref, dk_bf_ref, *dv_refs):
    dk = kept_ref[:, :HD] + arrived_ref[:, :HD]
    dk_ref[...] = dk
    dk_bf_ref[...] = dk.astype(jnp.bfloat16)
    for m, dv_ref in enumerate(dv_refs):
        for far in range(2):
            here = pl.ds((far * GROUP + m) * ROWS, ROWS)
            dv_ref[far] = (kept_ref[here, HD:] + arrived_ref[here, HD:]).astype(jnp.bfloat16)


def sum_halves(near_ref, far_ref, out_ref):
    quarter = GROUP * ROWS
    for k in range(2):
        here, there = pl.ds(k * quarter, quarter), pl.ds((1 - k) * quarter, quarter)
        total = near_ref[here] + far_ref[there].astype(jnp.float32)
        out_ref[here] = total.astype(jnp.bfloat16)


def finish(keep_ref, arrived_ref, far_ref, *refs):
    row_refs, value_refs, refs = refs[:GROUP], refs[GROUP : 2 * GROUP], refs[2 * GROUP :]
    weight_out, query_out, value_out = refs
    head = own_head()
    weight_out[...] = keep_ref[...] + arrived_ref[...]
    for m in range(GROUP):
        query_out[:, columns(head ^ m, GROUP * HD)] = row_refs[m][...]
        value = value_refs[m][0].astype(jnp.float32) + far_ref[m].astype(jnp.float32)
        value_out[:, columns(head ^ m, HD)] = value.astype(jnp.bfloat16)


def shaped(shape, dtype=jnp.bfloat16):
    return jax.ShapeDtypeStruct(shape, dtype)


def limits(mebibytes):
    return pltpu.CompilerParams(vmem_limit_bytes=mebibytes << 20)


def with_partners(arrays):
    return [arrays[0]] + [swap(arrays[m], 2 * m) for m in range(1, len(arrays))]


def on_device_by_heads(inputs, w_key, values, queries, d_out, doc_lens, block_pos):
    features = inputs.shape[1]
    kv_columns = values.shape[1]
    total_rows = 16 * ROWS
    half = total_rows // 2
    vmem, smem, hbm = whole_spec(), whole_spec(SMEM), whole_spec(HBM)

    pairs = pl.pallas_call(
        project_keys,
        out_shape=[shaped((MARKED, 2 * HD))] * GROUP,
        in_specs=[smem, hbm, vmem, hbm],
        out_specs=[vmem] * GROUP,
        scratch_shapes=[
            VMEM((ROWS, features), jnp.bfloat16),
            VMEM((features, kv_columns), jnp.bfloat16),
            VMEM((ROWS, kv_columns), jnp.float32),
            DMA((1 + features // PART,)),
        ],
        compiler_params=limits(60),
        cost_estimate=pl.CostEstimate(
            flops=2 * ROWS * features * kv_columns,
            bytes_accessed=features * kv_columns * 2,
            transcendentals=0,
        ),
        name="project_keys",
    )(block_pos, inputs, values, w_key)

    packed_rows = pl.pallas_call(
        pack_rows,
        out_shape=[shaped((ROWS, 2 * GROUP * HD))] * GROUP,
        in_specs=[vmem] * 2,
        out_specs=[vmem] * GROUP,
        compiler_params=limits(8),
        name="pack_rows",
    )(after(queries, pairs[0]), d_out)

    pairs = [after(pairs[0], packed_rows[0])] + list(pairs[1:])
    pairs = with_partners(pairs)
    own_a = jnp.concatenate(pairs[:2], axis=0)
    own_b = jnp.concatenate(pairs[2:], axis=0)
    far_a = swap(own_a, Z_HI)
    far_b = swap(own_b, Z_HI)
    rows = with_partners(packed_rows)

    near_features, far_features = pl.pallas_call(
        pack_features,
        out_shape=[shaped((GROUP, ROWS, 256))] * 2,
        in_specs=[vmem],
        out_specs=[vmem] * 2,
        compiler_params=limits(8),
        name="pack_features",
    )(after(inputs, own_a))
    leaving = pl.pallas_call(
        pack_weights,
        out_shape=shaped((2 * PART, kv_columns)),
        in_specs=[hbm],
        out_specs=vmem,
        scratch_shapes=[DMA],
        compiler_params=limits(56),
        name="pack_weights",
    )(after(w_key, own_b))
    w_near = swap_tensor(leaving)
    near_pairs = jnp.concatenate([own_a, own_b, far_a, far_b], axis=0)
    core_pairs = swap(after(near_pairs, near_features, leaving, rows[2], rows[3]), CORE)
    far_features = swap(far_features, Z_HI)

    row_grad = shaped((ROWS, GROUP * HD))
    padded_rows = total_rows + HD
    sorted_rows = shaped((padded_rows, HD))
    sums = shaped((padded_rows, HD), jnp.float32)
    half_sums = shaped((half, 2 * HD), jnp.float32)

    def attend_scratch(blocks):
        stacked = VMEM((blocks, GROUP * BLK, HD), jnp.bfloat16)
        tiles = VMEM((2, total_rows // TILE, TILE, GROUP * BLK), jnp.float32)
        return [
            stacked,
            stacked,
            VMEM((blocks, BLK, GROUP * HD), jnp.bfloat16),
            tiles,
            tiles,
            SMEM((4 * GROUP, HD), jnp.int32),
            DMA,
        ]

    *row_grads, keys, keys_t, all_values, dk_first, dv_first, marks = pl.pallas_call(
        attend_first,
        out_shape=[row_grad] * (GROUP - 1)
        + [sorted_rows, shaped((HD, padded_rows)), sorted_rows, sums, sums]
        + [shaped((4 * GROUP, HD), jnp.int32)],
        in_specs=[smem] + [vmem] * (GROUP + 4),
        out_specs=[vmem] * (GROUP + 5),
        scratch_shapes=attend_scratch(Q_BLOCKS - 2),
        compiler_params=limits(24),
        cost_estimate=pl.CostEstimate(flops=ATTEND_COST, bytes_accessed=0, transcendentals=0),
        name="attend_first",
    )(doc_lens, rows[0], *rows[2:], own_a, own_b, far_a, far_b, core_pairs)
    last_grad, kept, sent = pl.pallas_call(
        attend_last,
        out_shape=[row_grad, half_sums, half_sums],
        in_specs=[smem] + [vmem] * 7,
        out_specs=[vmem] * 3,
        scratch_shapes=[VMEM((padded_rows, HD), jnp.float32)] * 2 + attend_scratch(2),
        compiler_params=limits(24),
        cost_estimate=pl.CostEstimate(flops=ATTEND_COST, bytes_accessed=0, transcendentals=0),
        name="attend_last",
    )(doc_lens, after(rows[1], w_near), keys, keys_t, all_values, dk_first, dv_first, marks)

    row_grads = [row_grads[0], swap(row_grads[1], 4), swap(row_grads[2], 6)]
    sent = after(sent, far_features, *row_grads)
    dk_sum, dk_near, *value_grads = pl.pallas_call(
        sum_cores,
        out_shape=[shaped((half, HD), jnp.float32), shaped((half, HD))]
        + [shaped((2, ROWS, HD))] * GROUP,
        in_specs=[vmem] * 2,
        out_specs=[vmem] * (2 + GROUP),
        compiler_params=limits(16),
        name="sum_cores",
    )(kept, swap(sent, CORE))
    dk_far = swap(dk_near, Z_HI)
    w_far = swap(after(w_near, sent), CORE)
    value_grads = with_partners(value_grads)
    value_far = jnp.stack([grad[1] for grad in value_grads])

    feature_parts = pl.pallas_call(
        join_features,
        out_shape=[shaped((2, ROWS, 256))] * GROUP,
        in_specs=[vmem] * 2,
        out_specs=[vmem] * GROUP,
        compiler_params=limits(16),
        name="join_features",
    )(after(near_features, sent), far_features)
    own_features = pl.pallas_call(
        turn_features,
        out_shape=shaped((256, half)),
        in_specs=[vmem] * GROUP,
        out_specs=vmem,
        compiler_params=limits(16),
        cost_estimate=pl.CostEstimate(flops=1_000_000_000, bytes_accessed=0, transcendentals=0),
        name="turn_features",
    )(*with_partners(feature_parts))
    other_features = swap_tensor(own_features)

    key_grad = pl.pallas_call(
        sum_halves,
        out_shape=shaped((half, HD)),
        in_specs=[vmem] * 2,
        out_specs=vmem,
        compiler_params=limits(8),
        cost_estimate=pl.CostEstimate(flops=1_000_000, bytes_accessed=0, transcendentals=0),
        name="sum_halves",
    )(dk_sum, dk_far)
    key_grad = after(key_grad, own_features, w_far)
    key_grads = with_partners([key_grad] * GROUP)
    own_key_grad = jnp.stack([key_grads[m][m * ROWS : (m + 1) * ROWS] for m in range(GROUP)])
    other_key_grad = swap_tensor(own_key_grad)

    value_far = swap(after(value_far, key_grad), Z_HI)
    last_grad = swap(after(last_grad, own_key_grad), 2)

    keep, send = pl.pallas_call(
        weight_grad,
        out_shape=[shaped((256, kv_columns), jnp.float32)] * 2,
        in_specs=[vmem] * (2 + GROUP),
        out_specs=[vmem] * 2,
        scratch_shapes=[VMEM((half, kv_columns), jnp.bfloat16)],
        compiler_params=limits(24),
        cost_estimate=pl.CostEstimate(
            flops=4 * 256 * half * kv_columns, bytes_accessed=4 << 20, transcendentals=0
        ),
        name="weight_grad",
    )(after(own_features, value_far), other_features, *key_grads)
    arrived = swap(send, CORE)

    d_input = pl.pallas_call(
        input_grad,
        out_shape=shaped((ROWS, features // 2)),
        in_specs=[vmem] * 5,
        out_specs=vmem,
        scratch_shapes=[VMEM((ROWS, kv_columns), jnp.bfloat16)] * 2,
        compiler_params=limits(16),
        cost_estimate=pl.CostEstimate(
            flops=8_000_000_000, bytes_accessed=5 << 20, transcendentals=0
        ),
        name="input_grad",
    )(after(own_key_grad, send), other_key_grad, w_key, w_near, w_far)

    d_wkey, d_query, d_value = pl.pallas_call(
        finish,
        out_shape=[
            shaped((256, kv_columns), jnp.float32),
            shaped(queries.shape),
            shaped(values.shape),
        ],
        in_specs=[vmem] * (3 + 2 * GROUP),
        out_specs=[vmem] * 3,
        compiler_params=limits(16),
        name="finish",
    )(after(keep, d_input), arrived, value_far, row_grads[0], last_grad, *row_grads[1:], *value_grads)
    return (d_query, d_value, d_input, d_wkey)


def solution(mesh):
    by_heads = mesh.shape["dp"] == 16 and mesh.shape["tensor"] == 2
    return jax.shard_map(
        on_device_by_heads if by_heads else on_device,
        mesh=mesh,
        in_specs=(
            P("dp", None),
            P(None, "tensor"),
            P("dp", "tensor"),
            P("dp", "tensor"),
            P("dp", "tensor"),
            P(),
            P("dp"),
        ),
        out_specs=(P("dp", "tensor"), P("dp", "tensor"), P("dp", "tensor"), P("dp", "tensor")),
        check_vma=False,
    )
```

```python
import math

import jax
import jax.numpy as jnp
from jax import lax
from jax.experimental import pallas as pl
from jax.experimental.pallas import tpu as pltpu
from jax.sharding import PartitionSpec as P

HD = 128
BLK = 64


masked_fill = -1e30


def row_positions(block_pos):
    within = jnp.tile(jnp.arange(BLK, dtype=jnp.int32), block_pos.shape[0])
    return jnp.repeat(block_pos, BLK) * BLK + within


def documents(positions, doc_lens):
    starts = jnp.cumsum(doc_lens) - doc_lens
    return jnp.sum((positions[:, None] >= starts[None, :]).astype(jnp.int32), axis=1) - 1


def split_heads(block_rows, kv_heads):
    return block_rows.reshape(block_rows.shape[0], kv_heads, HD)


def scored(query_heads, key_block, score_scale):
    key_split = split_heads(key_block, query_heads.shape[1])
    return (
        jnp.einsum("qcgd,kcd->cgqk", query_heads, key_split, preferred_element_type=jnp.float32)
        * score_scale
    )


def contributions(
    query_heads, grad_heads, key_block, value_block, allowed, row_max, row_sum, delta, score_scale
):
    kv_heads = query_heads.shape[1]
    key_split = split_heads(key_block, kv_heads)
    value_split = split_heads(value_block, kv_heads)
    scores = scored(query_heads, key_block, score_scale)
    mask_full = allowed[None, None]
    probabilities = (
        jnp.where(mask_full, jnp.exp(scores - row_max[..., None]), 0.0) / row_sum[..., None]
    )
    d_prob = jnp.einsum(
        "qcgd,kcd->cgqk", grad_heads, value_split, preferred_element_type=jnp.float32
    )
    d_score = probabilities * (d_prob - delta[..., None])
    prob_bf = probabilities.astype(jnp.bfloat16)
    score_bf = d_score.astype(jnp.bfloat16)
    query_part = score_scale * jnp.einsum(
        "cgqk,kcd->qcgd", score_bf, key_split, preferred_element_type=jnp.float32
    )
    key_part = score_scale * jnp.einsum(
        "cgqk,qcgd->kcd", score_bf, query_heads, preferred_element_type=jnp.float32
    )
    value_part = jnp.einsum(
        "cgqk,qcgd->kcd", prob_bf, grad_heads, preferred_element_type=jnp.float32
    )
    width_rows = key_block.shape[0]
    partial_value = jnp.concatenate(
        [key_part.reshape(width_rows, -1), value_part.reshape(width_rows, -1)], axis=1
    )
    return (query_part, partial_value)


def on_device(inputs, w_key, values, queries, d_out, doc_lens, block_pos):
    local_rows = inputs.shape[0]
    kv_heads = values.shape[1] // HD
    group_size = queries.shape[1] // (kv_heads * HD)
    kv_columns = kv_heads * HD
    score_scale = 1.0 / math.sqrt(HD)
    key_rows = jnp.dot(inputs, w_key, preferred_element_type=jnp.float32).astype(jnp.bfloat16)
    all_keys, all_values, all_blocks = (
        lax.all_gather(key_rows, "dp", axis=0, tiled=True),
        lax.all_gather(values, "dp", axis=0, tiled=True),
        lax.all_gather(block_pos, "dp", axis=0, tiled=True),
    )
    key_pos = row_positions(all_blocks)
    key_doc = documents(key_pos, doc_lens)
    query_pos = row_positions(block_pos)
    query_doc = documents(query_pos, doc_lens)
    query_heads = queries.reshape(local_rows, kv_heads, group_size, HD)
    grad_heads = d_out.reshape(local_rows, kv_heads, group_size, HD)
    total_rows = all_keys.shape[0]
    key_width = math.gcd(512, total_rows)
    stat_shape = (kv_heads, group_size, local_rows)

    def mask_for(first_row, width_rows):
        pos_here = lax.dynamic_slice_in_dim(key_pos, first_row, width_rows, 0)
        doc_here = lax.dynamic_slice_in_dim(key_doc, first_row, width_rows, 0)
        return (query_doc[:, None] == doc_here[None, :]) & (pos_here[None, :] <= query_pos[:, None])

    def visit_stats(block_index, running):
        first_row = block_index * key_width
        key_block = lax.dynamic_slice_in_dim(all_keys, first_row, key_width, 0)
        value_block = lax.dynamic_slice_in_dim(all_values, first_row, key_width, 0)
        allowed = mask_for(first_row, key_width)

        def visit_compute_live(state_now):
            row_max, row_sum, weighted = state_now
            scores = scored(query_heads, key_block, score_scale)
            mask_full = allowed[None, None]
            new_max = jnp.maximum(
                row_max, jnp.max(jnp.where(mask_full, scores, masked_fill), axis=3)
            )
            exp_terms = jnp.where(mask_full, jnp.exp(scores - new_max[..., None]), 0.0)
            d_prob = jnp.einsum(
                "qcgd,kcd->cgqk",
                grad_heads,
                split_heads(value_block, kv_heads),
                preferred_element_type=jnp.float32,
            )
            shrink = jnp.exp(row_max - new_max)
            return (
                new_max,
                row_sum * shrink + jnp.sum(exp_terms, axis=3),
                weighted * shrink + jnp.sum(exp_terms * d_prob, axis=3),
            )

        return lax.cond(jnp.any(allowed), visit_compute_live, lambda state_now: state_now, running)

    start_state = (
        jnp.full(stat_shape, masked_fill, jnp.float32),
        jnp.zeros(stat_shape, jnp.float32),
        jnp.zeros(stat_shape, jnp.float32),
    )
    row_max, row_sum, weighted = lax.fori_loop(0, total_rows // key_width, visit_stats, start_state)
    delta = weighted / row_sum

    def block_work(key_block, value_block, allowed):
        width_rows = key_block.shape[0]

        def block_compute_live(operands):
            return contributions(
                query_heads,
                grad_heads,
                operands[0],
                operands[1],
                operands[2],
                row_max,
                row_sum,
                delta,
                score_scale,
            )

        def dead_block(operands):
            return (
                jnp.zeros((local_rows, kv_heads, group_size, HD), jnp.float32),
                jnp.zeros((width_rows, 2 * kv_columns), jnp.float32),
            )

        return lax.cond(
            jnp.any(allowed), block_compute_live, dead_block, (key_block, value_block, allowed)
        )

    query_start = jnp.zeros((local_rows, kv_heads, group_size, HD), jnp.float32)

    def visit_block(block_index, running):
        query_sum, buffer_rows = running
        first_row = block_index * key_width
        key_block = lax.dynamic_slice_in_dim(all_keys, first_row, key_width, 0)
        value_block = lax.dynamic_slice_in_dim(all_values, first_row, key_width, 0)
        query_part, partial_value = block_work(
            key_block, value_block, mask_for(first_row, key_width)
        )
        return (
            query_sum + query_part,
            lax.dynamic_update_slice_in_dim(buffer_rows, partial_value, first_row, 0),
        )

    empty_buffer = jnp.zeros((total_rows, 2 * kv_columns), jnp.float32)
    query_sum, buffer_rows = lax.fori_loop(
        0, total_rows // key_width, visit_block, (query_start, empty_buffer)
    )
    arrived = lax.all_to_all(
        buffer_rows.astype(jnp.bfloat16), "dp", split_axis=0, concat_axis=0, tiled=True
    ).astype(buffer_rows.dtype)
    own_sums = jnp.sum(arrived.reshape(-1, local_rows, 2 * kv_columns), axis=0)
    d_query = query_sum.astype(jnp.bfloat16).reshape(local_rows, kv_columns * group_size)
    key_grad = own_sums[:, :kv_columns].astype(jnp.bfloat16)
    d_value = own_sums[:, kv_columns:].astype(jnp.bfloat16)
    d_wkey = lax.psum_scatter(
        lax.dot_general(
            inputs, key_grad, (((0,), (0,)), ((), ())), preferred_element_type=jnp.float32
        ),
        "dp",
        scatter_dimension=0,
        tiled=True,
    )
    partial_input = lax.dot_general(
        key_grad, w_key, (((1,), (1,)), ((), ())), preferred_element_type=jnp.float32
    )
    d_input = lax.psum_scatter(
        partial_input.astype(jnp.bfloat16), "tensor", scatter_dimension=1, tiled=True
    )
    return (d_query, d_value, d_input, d_wkey)


CORE, Z_HI = 1, 8
GROUP = 4
ROWS = 128
TILE = 256
UNROLLED = 5
ATTEND_COST = 4_000_000_000
PART = 512
MARKED = ROWS + 16
Q_BLOCKS = GROUP * ROWS // BLK
SMEM = pltpu.SMEM
VMEM = pltpu.VMEM
HBM = pltpu.HBM
DMA = pltpu.SemaphoreType.DMA


def swap(array, mask):
    return lax.ppermute(array, "dp", [(i, i ^ mask) for i in range(16)])


def swap_tensor(array):
    return lax.ppermute(array, "tensor", [(0, 1), (1, 0)])


def own_head():
    return (lax.axis_index("dp") >> 1) & 3


def columns(index, width):
    return pl.ds(pl.multiple_of(index * width, width), width)


def whole_spec(space=VMEM):
    return pl.BlockSpec(memory_space=space)


def after(array, *earlier):
    return lax.optimization_barrier((array,) + earlier)[0]


def copy_all(pairs, semaphores):
    copies = [
        pltpu.make_async_copy(source, target, semaphores.at[i])
        for i, (source, target) in enumerate(pairs)
    ]
    for copy in copies:
        copy.start()
    return copies


def project_keys(pos_ref, inputs_ref, values_ref, w_ref, *refs):
    pair_refs = refs[:GROUP]
    inputs, weights, total, semaphores = refs[GROUP:]
    head = own_head()
    spans = [pl.ds(k * PART, PART) for k in range(weights.shape[0] // PART)]
    copies = copy_all(
        [(inputs_ref, inputs)] + [(w_ref.at[span], weights.at[span]) for span in spans],
        semaphores,
    )
    lanes = lax.broadcasted_iota(jnp.int32, (16, 2 * HD), 1)
    marks = jnp.where(lanes == 0, pos_ref[0], jnp.where(lanes == 1, pos_ref[1], 0))
    for m in range(GROUP):
        pair_refs[m][:ROWS, HD:] = values_ref[:, columns(head ^ m, HD)]
        pair_refs[m][ROWS:] = marks.astype(jnp.float32).astype(jnp.bfloat16)
    copies[0].wait()
    for k, span in enumerate(spans):
        copies[1 + k].wait()
        part = jnp.dot(inputs[:, span], weights[span], preferred_element_type=jnp.float32)
        total[...] = part if k == 0 else total[...] + part
    for m in range(GROUP):
        pair_refs[m][:ROWS, :HD] = total[:, columns(head ^ m, HD)].astype(jnp.bfloat16)


def pack_rows(queries_ref, grads_ref, *out_refs):
    head = own_head()
    for m, out_ref in enumerate(out_refs):
        span = columns(head ^ m, GROUP * HD)
        out_ref[:, : GROUP * HD] = queries_ref[:, span]
        out_ref[:, GROUP * HD :] = grads_ref[:, span]


def pack_weights(w_ref, leaving_ref, semaphore):
    first = (1 - lax.axis_index("tensor")) * 2 + (lax.axis_index("dp") & 1)
    copy = pltpu.make_async_copy(w_ref.at[columns(first, 2 * PART)], leaving_ref, semaphore)
    copy.start()
    copy.wait()


def pack_features(inputs_ref, near_ref, far_ref):
    chip = lax.axis_index("dp") >> 1
    side = lax.axis_index("tensor")
    for m in range(GROUP):
        near_ref[m] = inputs_ref[:, columns(2 * (chip ^ m) + side, 256)]
        far_ref[m] = inputs_ref[:, columns(2 * (chip ^ (m + GROUP)) + side, 256)]


def join_features(near_ref, far_ref, *joined_refs):
    for m, joined_ref in enumerate(joined_refs):
        joined_ref[0] = near_ref[m]
        joined_ref[1] = far_ref[m]


def turn_features(*refs):
    for j in range(2 * GROUP):
        turned = refs[j % GROUP][j // GROUP].astype(jnp.float32).T
        refs[-1][:, j * ROWS : (j + 1) * ROWS] = turned.astype(jnp.bfloat16)


def dot_nt(left, right):
    return lax.dot_general(
        left, right, (((1,), (1,)), ((), ())), preferred_element_type=jnp.float32
    )


def folded(array, reduce):
    return reduce(array.reshape(-1, 8, array.shape[-1]), axis=0)


def first_row_of(positions):
    def first_row(block):
        return pl.multiple_of(positions[block // 2, block % 2] * BLK, BLK)

    return first_row


def attend_rows(
    first_part, first_row, lens_ref, row_refs, dq_refs, keys, keys_t, values, dk, dv, scratch
):
    q_rows, g_rows, dq_all, scores, d_prob = scratch
    score_scale = 1.0 / math.sqrt(HD)
    base_two = score_scale * math.log2(math.e)
    parts = len(row_refs)
    for block in range(2 * parts):
        here = pl.ds(block % 2 * BLK, BLK)
        for h in range(GROUP):
            there = pl.ds(h * BLK, BLK)
            q_rows[block, there] = row_refs[block // 2][here, h * HD : (h + 1) * HD]
            g_rows[block, there] = row_refs[block // 2][
                here, (GROUP + h) * HD : (GROUP + h + 1) * HD
            ]
    starts = [lens_ref[0]]
    for k in (1, 2):
        starts.append(starts[-1] + lens_ref[k])

    def document_start(position):
        found = jnp.zeros_like(position)
        for start in starts:
            found = jnp.where(start <= position, start, found)
        return found

    zeros = jnp.zeros((8, GROUP * BLK), jnp.float32)
    last_tile = keys.shape[0] - TILE

    @pl.loop(0, parts)
    def _(part):
        blocks = [2 * part, 2 * part + 1]
        firsts = [first_row(2 * first_part + block) for block in blocks]
        lanes = lax.broadcasted_iota(jnp.int32, (1, GROUP * BLK), 1)
        positions = [first + (lanes & (BLK - 1)) for first in firsts]
        row_starts = [document_start(position) for position in positions]
        lows = [document_start(first) // HD * HD for first in firsts]
        counts = [
            (first + BLK - low + TILE - 1) // TILE for first, low in zip(firsts, lows)
        ]
        count = jnp.maximum(*counts)

        def rows_of(j, k):
            offset = jnp.minimum(lows[j] + k * TILE, last_tile)
            return pl.ds(pl.multiple_of(offset, HD), TILE)

        def run(over_tiles):
            query = [q_rows[block] for block in blocks]
            grad = [g_rows[block] for block in blocks]

            def visit_scores(k, row_max):
                seen = []
                for j in range(2):
                    here = rows_of(j, k)
                    raw = dot_nt(keys[here], query[j])
                    row = lows[j] + k * TILE + lax.broadcasted_iota(jnp.int32, raw.shape, 0)
                    allowed = (row <= positions[j]) & (row >= row_starts[j])
                    raw = jnp.where(allowed, raw, masked_fill)
                    scores[j, k] = raw
                    d_prob[j, k] = dot_nt(values[here], grad[j])
                    seen.append(jnp.maximum(row_max[j], folded(raw, jnp.max)))
                return seen

            row_max = over_tiles(visit_scores, [zeros + masked_fill] * 2)
            row_max = [jnp.max(part_max, axis=0, keepdims=True) for part_max in row_max]

            def visit_sums(k, running):
                sums = []
                for j in range(2):
                    terms = jnp.exp2((scores[j, k] - row_max[j]) * base_two)
                    scores[j, k] = terms
                    sums.append(running[2 * j] + folded(terms, jnp.sum))
                    sums.append(running[2 * j + 1] + folded(terms * d_prob[j, k], jnp.sum))
                return sums

            sums = over_tiles(visit_sums, [zeros] * 4)
            sums = [jnp.sum(part_sum, axis=0, keepdims=True) for part_sum in sums]
            inverse = [1.0 / sums[2 * j] for j in range(2)]
            delta = [sums[2 * j + 1] * inverse[j] for j in range(2)]

            def visit_grads(k, dq):
                added = []
                for j in range(2):
                    here = rows_of(j, k)
                    prob = scores[j, k] * inverse[j]
                    score_bf = (prob * (d_prob[j, k] - delta[j])).astype(jnp.bfloat16)
                    dk[here] += jnp.dot(score_bf, query[j], preferred_element_type=jnp.float32)
                    dv[here] += jnp.dot(
                        prob.astype(jnp.bfloat16), grad[j], preferred_element_type=jnp.float32
                    )
                    added.append(
                        dq[j]
                        + jnp.dot(
                            keys_t[:, here], score_bf, preferred_element_type=jnp.float32
                        )
                    )
                return added

            dq = over_tiles(visit_grads, [jnp.zeros((HD, GROUP * BLK), jnp.float32)] * 2)
            for j in range(2):
                turned = (dq[j] * score_scale).T.astype(jnp.bfloat16)
                for h in range(GROUP):
                    dq_all[blocks[j], :, h * HD : (h + 1) * HD] = turned[h * BLK : (h + 1) * BLK]

        for fixed in range(1, UNROLLED + 1):

            @pl.when(count == fixed)
            def _(fixed=fixed):
                def over_tiles(visit, running):
                    for k in range(fixed):
                        running = visit(k, running)
                    return running

                run(over_tiles)

        @pl.when(count > UNROLLED)
        def _():
            run(lambda visit, running: lax.fori_loop(0, count, visit, running))

    for block in range(2 * parts):
        dq_refs[block // 2][pl.ds(block % 2 * BLK, BLK)] = dq_all[block]


def attend_first(lens_ref, *refs):
    row_refs, refs = refs[: GROUP - 1], refs[GROUP - 1 :]
    own_a, own_b, far_a, far_b, core_pairs, refs = *refs[:5], refs[5:]
    dq_refs, refs = refs[: GROUP - 1], refs[GROUP - 1 :]
    keys, keys_t, values, dk, dv, marks, refs = *refs[:6], refs[6:]
    scratch, (positions, semaphore) = refs[:5], refs[5:]
    reach = 2 * MARKED
    pair_refs = [own_a, own_b]
    pair_refs += [core_pairs.at[pl.ds(k * reach, reach)] for k in range(2)]
    pair_refs += [far_a, far_b]
    pair_refs += [core_pairs.at[pl.ds(k * reach, reach)] for k in range(2, 4)]
    for part in range(4 * GROUP):
        here = pl.ds(part % 2 * MARKED + ROWS, 16)
        row = pair_refs[part // 2][here, :HD].astype(jnp.float32).astype(jnp.int32)
        marks[part : part + 1] = row[:1]
    to_scalars = pltpu.make_async_copy(marks, positions, semaphore)
    to_scalars.start()
    dk[...] = jnp.zeros_like(dk)
    dv[...] = jnp.zeros_like(dv)
    to_scalars.wait()
    first_row = first_row_of(positions)
    for block in range(4 * Q_BLOCKS):
        part = block // 2
        here = pl.ds(part % 2 * MARKED + block % 2 * BLK, BLK)
        there = pl.ds(first_row(block), BLK)
        keys[there] = pair_refs[part // 2][here, :HD]
        values[there] = pair_refs[part // 2][here, HD:]
    beyond = pl.ds(4 * GROUP * ROWS, HD)
    keys[beyond] = jnp.zeros((HD, HD), jnp.bfloat16)
    keys_t[:, beyond] = jnp.zeros((HD, HD), jnp.bfloat16)
    values[beyond] = jnp.zeros((HD, HD), jnp.bfloat16)
    for tile in range(keys.shape[0] // TILE):
        here = pl.ds(tile * TILE, TILE)
        keys_t[:, here] = keys[here].astype(jnp.float32).T.astype(jnp.bfloat16)
    attend_rows(
        0, first_row, lens_ref, row_refs, dq_refs, keys, keys_t, values, dk, dv, scratch
    )


def attend_last(lens_ref, row_ref, keys, keys_t, values, dk_first, dv_first, marks, *refs):
    dq_ref, kept, sent, dk, dv, refs = *refs[:5], refs[5:]
    scratch, (positions, semaphore) = refs[:5], refs[5:]
    score_scale = 1.0 / math.sqrt(HD)
    to_scalars = pltpu.make_async_copy(marks, positions, semaphore)
    to_scalars.start()
    dk[...] = dk_first[...]
    dv[...] = dv_first[...]
    to_scalars.wait()
    first_row = first_row_of(positions)
    attend_rows(
        GROUP - 1, first_row, lens_ref, [row_ref], [dq_ref], keys, keys_t, values, dk, dv, scratch
    )
    for block in range(4 * Q_BLOCKS):
        quarter = block // Q_BLOCKS
        here = pl.ds(quarter // 2 * Q_BLOCKS * BLK + block % Q_BLOCKS * BLK, BLK)
        there = pl.ds(first_row(block), BLK)
        out_ref = sent if quarter % 2 else kept
        out_ref[here, :HD] = dk[there] * score_scale
        out_ref[here, HD:] = dv[there]


def weight_grad(own_ref, other_ref, *refs):
    grad_refs, (keep_ref, send_ref, grads) = refs[:GROUP], refs[GROUP:]
    head = own_head()
    for k, grad_ref in enumerate(grad_refs):
        for far in range(2):
            for m in range(GROUP):
                here = pl.ds((far * GROUP + m) * ROWS, ROWS)
                there = pl.ds((far * GROUP + (m ^ k)) * ROWS, ROWS)
                grads[here, columns(head ^ k, HD)] = grad_ref[there]
    own = jnp.dot(own_ref[...], grads[...], preferred_element_type=jnp.float32)
    other = jnp.dot(other_ref[...], grads[...], preferred_element_type=jnp.float32)
    crossed = (lax.axis_index("dp") & 1) ^ lax.axis_index("tensor")

    @pl.when(crossed == 0)
    def _():
        keep_ref[...] = own
        send_ref[...] = other

    @pl.when(crossed == 1)
    def _():
        keep_ref[...] = other
        send_ref[...] = own


def input_grad(own_ref, other_ref, w_own, w_near, w_far, out_ref, own_all, other_all):
    head = own_head()
    core = lax.axis_index("dp") & 1
    side = lax.axis_index("tensor")
    for k in range(GROUP):
        own_all[:, columns(head ^ k, HD)] = own_ref[k]
        other_all[:, columns(head ^ k, HD)] = other_ref[k]
    for k in range(4):
        chunk = 2 * (core ^ (k // 2)) + k % 2
        w_other = (w_near, w_far)[k // 2][pl.ds(k % 2 * PART, PART)]
        part = dot_nt(own_all[...], w_own[columns(side * 4 + chunk, PART)])
        part = part + dot_nt(other_all[...], w_other)
        out_ref[:, columns(chunk, PART)] = part.astype(jnp.bfloat16)


def pack_grads(value_ref, row_ref, *refs):
    for m, out_ref in enumerate(refs):
        out_ref[:, :HD] = value_ref[m * ROWS : (m + 1) * ROWS]
    refs[-1][:, HD:] = row_ref[...]


def finish(keep_ref, arrived_ref, *refs):
    row_refs, grad_refs, refs = refs[: GROUP - 1], refs[GROUP - 1 : 2 * GROUP - 1], refs[2 * GROUP - 1 :]
    weight_out, query_out, value_out = refs
    head = own_head()
    weight_out[...] = keep_ref[...] + arrived_ref[...]
    for m in range(GROUP):
        row = row_refs[m][...] if m < GROUP - 1 else grad_refs[m][:, HD:]
        query_out[:, columns(head ^ m, GROUP * HD)] = row
        value_out[:, columns(head ^ m, HD)] = grad_refs[m][:, :HD]


def shaped(shape, dtype=jnp.bfloat16):
    return jax.ShapeDtypeStruct(shape, dtype)


def limits(mebibytes):
    return pltpu.CompilerParams(vmem_limit_bytes=mebibytes << 20)


def with_partners(arrays):
    return [arrays[0]] + [swap(arrays[m], 2 * m) for m in range(1, len(arrays))]


def on_device_by_heads(inputs, w_key, values, queries, d_out, doc_lens, block_pos):
    features = inputs.shape[1]
    kv_columns = values.shape[1]
    total_rows = 16 * ROWS
    half, quarter = total_rows // 2, total_rows // 4
    vmem, smem, hbm = whole_spec(), whole_spec(SMEM), whole_spec(HBM)

    pairs = pl.pallas_call(
        project_keys,
        out_shape=[shaped((MARKED, 2 * HD))] * GROUP,
        in_specs=[smem, hbm, vmem, hbm],
        out_specs=[vmem] * GROUP,
        scratch_shapes=[
            VMEM((ROWS, features), jnp.bfloat16),
            VMEM((features, kv_columns), jnp.bfloat16),
            VMEM((ROWS, kv_columns), jnp.float32),
            DMA((1 + features // PART,)),
        ],
        compiler_params=limits(60),
        cost_estimate=pl.CostEstimate(
            flops=2 * ROWS * features * kv_columns,
            bytes_accessed=features * kv_columns * 2,
            transcendentals=0,
        ),
        name="project_keys",
    )(block_pos, inputs, values, w_key)

    packed_rows = pl.pallas_call(
        pack_rows,
        out_shape=[shaped((ROWS, 2 * GROUP * HD))] * GROUP,
        in_specs=[vmem] * 2,
        out_specs=[vmem] * GROUP,
        compiler_params=limits(8),
        name="pack_rows",
    )(after(queries, pairs[0]), d_out)

    pairs = [after(pairs[0], packed_rows[0])] + list(pairs[1:])
    pairs = with_partners(pairs)
    own_a = jnp.concatenate(pairs[:2], axis=0)
    own_b = jnp.concatenate(pairs[2:], axis=0)
    far_a = swap(own_a, Z_HI)
    far_b = swap(own_b, Z_HI)
    rows = with_partners(packed_rows)

    near_features, far_features = pl.pallas_call(
        pack_features,
        out_shape=[shaped((GROUP, ROWS, 256))] * 2,
        in_specs=[vmem],
        out_specs=[vmem] * 2,
        compiler_params=limits(8),
        name="pack_features",
    )(after(inputs, own_a))
    leaving = pl.pallas_call(
        pack_weights,
        out_shape=shaped((2 * PART, kv_columns)),
        in_specs=[hbm],
        out_specs=vmem,
        scratch_shapes=[DMA],
        compiler_params=limits(56),
        name="pack_weights",
    )(after(w_key, own_b))
    w_near = swap_tensor(leaving)
    near_pairs = jnp.concatenate([own_a, own_b, far_a, far_b], axis=0)
    core_pairs = swap(after(near_pairs, near_features, leaving, rows[1], rows[2]), CORE)
    far_features = swap(far_features, Z_HI)

    row_grad = shaped((ROWS, GROUP * HD))
    padded_rows = total_rows + HD
    sorted_rows = shaped((padded_rows, HD))
    sums = shaped((padded_rows, HD), jnp.float32)
    half_sums = shaped((half, 2 * HD), jnp.float32)

    def attend_scratch(blocks):
        stacked = VMEM((blocks, GROUP * BLK, HD), jnp.bfloat16)
        tiles = VMEM((2, total_rows // TILE, TILE, GROUP * BLK), jnp.float32)
        return [
            stacked,
            stacked,
            VMEM((blocks, BLK, GROUP * HD), jnp.bfloat16),
            tiles,
            tiles,
            SMEM((4 * GROUP, HD), jnp.int32),
            DMA,
        ]

    *row_grads, keys, keys_t, all_values, dk_first, dv_first, marks = pl.pallas_call(
        attend_first,
        out_shape=[row_grad] * (GROUP - 1)
        + [sorted_rows, shaped((HD, padded_rows)), sorted_rows, sums, sums]
        + [shaped((4 * GROUP, HD), jnp.int32)],
        in_specs=[smem] + [vmem] * (GROUP + 4),
        out_specs=[vmem] * (GROUP + 5),
        scratch_shapes=attend_scratch(Q_BLOCKS - 2),
        compiler_params=limits(24),
        cost_estimate=pl.CostEstimate(flops=ATTEND_COST, bytes_accessed=0, transcendentals=0),
        name="attend_first",
    )(doc_lens, *rows[:-1], own_a, own_b, far_a, far_b, core_pairs)
    last_grad, kept, sent = pl.pallas_call(
        attend_last,
        out_shape=[row_grad, half_sums, half_sums],
        in_specs=[smem] + [vmem] * 7,
        out_specs=[vmem] * 3,
        scratch_shapes=[VMEM((padded_rows, HD), jnp.float32)] * 2 + attend_scratch(2),
        compiler_params=limits(24),
        cost_estimate=pl.CostEstimate(flops=ATTEND_COST, bytes_accessed=0, transcendentals=0),
        name="attend_last",
    )(doc_lens, after(rows[-1], w_near), keys, keys_t, all_values, dk_first, dv_first, marks)

    row_grads = with_partners(row_grads)
    sent = after(sent, far_features, *row_grads)
    grads = kept + swap(sent, CORE)
    dk_sum, dv_sum = grads[:, :HD], grads[:, HD:]
    dk_far = swap(dk_sum.astype(jnp.bfloat16), Z_HI)
    w_far = swap(after(w_near, dk_sum), CORE)

    feature_parts = pl.pallas_call(
        join_features,
        out_shape=[shaped((2, ROWS, 256))] * GROUP,
        in_specs=[vmem] * 2,
        out_specs=[vmem] * GROUP,
        compiler_params=limits(16),
        name="join_features",
    )(after(near_features, sent), far_features)
    own_features = pl.pallas_call(
        turn_features,
        out_shape=shaped((256, half)),
        in_specs=[vmem] * GROUP,
        out_specs=vmem,
        compiler_params=limits(16),
        cost_estimate=pl.CostEstimate(flops=4_000_000_000, bytes_accessed=0, transcendentals=0),
        name="turn_features",
    )(*with_partners(feature_parts))
    other_features = swap_tensor(own_features)

    dk_far = jnp.concatenate([dk_far[quarter:], dk_far[:quarter]], axis=0)
    key_grad = (dk_sum + dk_far.astype(jnp.float32)).astype(jnp.bfloat16)
    key_grad = after(key_grad, own_features, w_far)
    key_grads = with_partners([key_grad] * GROUP)
    own_key_grad = jnp.stack([key_grads[m][m * ROWS : (m + 1) * ROWS] for m in range(GROUP)])
    other_key_grad = swap_tensor(own_key_grad)

    dv_far = swap(after(dv_sum[quarter:].astype(jnp.bfloat16), key_grad), Z_HI)
    value_grad = (dv_sum[:quarter] + dv_far.astype(jnp.float32)).astype(jnp.bfloat16)
    packed_grads = pl.pallas_call(
        pack_grads,
        out_shape=[shaped((ROWS, HD))] * (GROUP - 1) + [shaped((ROWS, (GROUP + 1) * HD))],
        in_specs=[vmem] * 2,
        out_specs=[vmem] * GROUP,
        compiler_params=limits(16),
        name="pack_grads",
    )(value_grad, last_grad)
    packed_grads = [after(packed_grads[0], own_key_grad)] + [
        after(grad, own_key_grad) for grad in packed_grads[1:]
    ]

    keep, send = pl.pallas_call(
        weight_grad,
        out_shape=[shaped((256, kv_columns), jnp.float32)] * 2,
        in_specs=[vmem] * (2 + GROUP),
        out_specs=[vmem] * 2,
        scratch_shapes=[VMEM((half, kv_columns), jnp.bfloat16)],
        compiler_params=limits(24),
        cost_estimate=pl.CostEstimate(
            flops=4 * 256 * half * kv_columns, bytes_accessed=4 << 20, transcendentals=0
        ),
        name="weight_grad",
    )(own_features, other_features, *key_grads)
    arrived = swap(send, CORE)

    d_input = pl.pallas_call(
        input_grad,
        out_shape=shaped((ROWS, features // 2)),
        in_specs=[vmem] * 5,
        out_specs=vmem,
        scratch_shapes=[VMEM((ROWS, kv_columns), jnp.bfloat16)] * 2,
        compiler_params=limits(16),
        cost_estimate=pl.CostEstimate(
            flops=8_000_000_000, bytes_accessed=5 << 20, transcendentals=0
        ),
        name="input_grad",
    )(after(own_key_grad, send), other_key_grad, w_key, w_near, w_far)

    d_wkey, d_query, d_value = pl.pallas_call(
        finish,
        out_shape=[
            shaped((256, kv_columns), jnp.float32),
            shaped(queries.shape),
            shaped(values.shape),
        ],
        in_specs=[vmem] * (1 + 2 * GROUP),
        out_specs=[vmem] * 3,
        compiler_params=limits(16),
        name="finish",
    )(keep, arrived, *row_grads, *with_partners(packed_grads))
    return (d_query, d_value, d_input, d_wkey)


def solution(mesh):
    by_heads = mesh.shape["dp"] == 16 and mesh.shape["tensor"] == 2
    return jax.shard_map(
        on_device_by_heads if by_heads else on_device,
        mesh=mesh,
        in_specs=(
            P("dp", None),
            P(None, "tensor"),
            P("dp", "tensor"),
            P("dp", "tensor"),
            P("dp", "tensor"),
            P(),
            P("dp"),
        ),
        out_specs=(P("dp", "tensor"), P("dp", "tensor"), P("dp", "tensor"), P("dp", "tensor")),
        check_vma=False,
    )
```

```python
import math

import jax
import jax.numpy as jnp
from jax import lax
from jax.experimental import pallas as pl
from jax.experimental.pallas import tpu as pltpu
from jax.sharding import PartitionSpec as P

HD = 128
BLK = 64


masked_fill = -1e30


def row_positions(block_pos):
    within = jnp.tile(jnp.arange(BLK, dtype=jnp.int32), block_pos.shape[0])
    return jnp.repeat(block_pos, BLK) * BLK + within


def documents(positions, doc_lens):
    starts = jnp.cumsum(doc_lens) - doc_lens
    return jnp.sum((positions[:, None] >= starts[None, :]).astype(jnp.int32), axis=1) - 1


def split_heads(block_rows, kv_heads):
    return block_rows.reshape(block_rows.shape[0], kv_heads, HD)


def scored(query_heads, key_block, score_scale):
    key_split = split_heads(key_block, query_heads.shape[1])
    return (
        jnp.einsum("qcgd,kcd->cgqk", query_heads, key_split, preferred_element_type=jnp.float32)
        * score_scale
    )


def contributions(
    query_heads, grad_heads, key_block, value_block, allowed, row_max, row_sum, delta, score_scale
):
    kv_heads = query_heads.shape[1]
    key_split = split_heads(key_block, kv_heads)
    value_split = split_heads(value_block, kv_heads)
    scores = scored(query_heads, key_block, score_scale)
    mask_full = allowed[None, None]
    probabilities = (
        jnp.where(mask_full, jnp.exp(scores - row_max[..., None]), 0.0) / row_sum[..., None]
    )
    d_prob = jnp.einsum(
        "qcgd,kcd->cgqk", grad_heads, value_split, preferred_element_type=jnp.float32
    )
    d_score = probabilities * (d_prob - delta[..., None])
    prob_bf = probabilities.astype(jnp.bfloat16)
    score_bf = d_score.astype(jnp.bfloat16)
    query_part = score_scale * jnp.einsum(
        "cgqk,kcd->qcgd", score_bf, key_split, preferred_element_type=jnp.float32
    )
    key_part = score_scale * jnp.einsum(
        "cgqk,qcgd->kcd", score_bf, query_heads, preferred_element_type=jnp.float32
    )
    value_part = jnp.einsum(
        "cgqk,qcgd->kcd", prob_bf, grad_heads, preferred_element_type=jnp.float32
    )
    width_rows = key_block.shape[0]
    partial_value = jnp.concatenate(
        [key_part.reshape(width_rows, -1), value_part.reshape(width_rows, -1)], axis=1
    )
    return (query_part, partial_value)


def on_device(inputs, w_key, values, queries, d_out, doc_lens, block_pos):
    local_rows = inputs.shape[0]
    kv_heads = values.shape[1] // HD
    group_size = queries.shape[1] // (kv_heads * HD)
    kv_columns = kv_heads * HD
    score_scale = 1.0 / math.sqrt(HD)
    key_rows = jnp.dot(inputs, w_key, preferred_element_type=jnp.float32).astype(jnp.bfloat16)
    all_keys, all_values, all_blocks = (
        lax.all_gather(key_rows, "dp", axis=0, tiled=True),
        lax.all_gather(values, "dp", axis=0, tiled=True),
        lax.all_gather(block_pos, "dp", axis=0, tiled=True),
    )
    key_pos = row_positions(all_blocks)
    key_doc = documents(key_pos, doc_lens)
    query_pos = row_positions(block_pos)
    query_doc = documents(query_pos, doc_lens)
    query_heads = queries.reshape(local_rows, kv_heads, group_size, HD)
    grad_heads = d_out.reshape(local_rows, kv_heads, group_size, HD)
    total_rows = all_keys.shape[0]
    key_width = math.gcd(512, total_rows)
    stat_shape = (kv_heads, group_size, local_rows)

    def mask_for(first_row, width_rows):
        pos_here = lax.dynamic_slice_in_dim(key_pos, first_row, width_rows, 0)
        doc_here = lax.dynamic_slice_in_dim(key_doc, first_row, width_rows, 0)
        return (query_doc[:, None] == doc_here[None, :]) & (pos_here[None, :] <= query_pos[:, None])

    def visit_stats(block_index, running):
        first_row = block_index * key_width
        key_block = lax.dynamic_slice_in_dim(all_keys, first_row, key_width, 0)
        value_block = lax.dynamic_slice_in_dim(all_values, first_row, key_width, 0)
        allowed = mask_for(first_row, key_width)

        def visit_compute_live(state_now):
            row_max, row_sum, weighted = state_now
            scores = scored(query_heads, key_block, score_scale)
            mask_full = allowed[None, None]
            new_max = jnp.maximum(
                row_max, jnp.max(jnp.where(mask_full, scores, masked_fill), axis=3)
            )
            exp_terms = jnp.where(mask_full, jnp.exp(scores - new_max[..., None]), 0.0)
            d_prob = jnp.einsum(
                "qcgd,kcd->cgqk",
                grad_heads,
                split_heads(value_block, kv_heads),
                preferred_element_type=jnp.float32,
            )
            shrink = jnp.exp(row_max - new_max)
            return (
                new_max,
                row_sum * shrink + jnp.sum(exp_terms, axis=3),
                weighted * shrink + jnp.sum(exp_terms * d_prob, axis=3),
            )

        return lax.cond(jnp.any(allowed), visit_compute_live, lambda state_now: state_now, running)

    start_state = (
        jnp.full(stat_shape, masked_fill, jnp.float32),
        jnp.zeros(stat_shape, jnp.float32),
        jnp.zeros(stat_shape, jnp.float32),
    )
    row_max, row_sum, weighted = lax.fori_loop(0, total_rows // key_width, visit_stats, start_state)
    delta = weighted / row_sum

    def block_work(key_block, value_block, allowed):
        width_rows = key_block.shape[0]

        def block_compute_live(operands):
            return contributions(
                query_heads,
                grad_heads,
                operands[0],
                operands[1],
                operands[2],
                row_max,
                row_sum,
                delta,
                score_scale,
            )

        def dead_block(operands):
            return (
                jnp.zeros((local_rows, kv_heads, group_size, HD), jnp.float32),
                jnp.zeros((width_rows, 2 * kv_columns), jnp.float32),
            )

        return lax.cond(
            jnp.any(allowed), block_compute_live, dead_block, (key_block, value_block, allowed)
        )

    query_start = jnp.zeros((local_rows, kv_heads, group_size, HD), jnp.float32)

    def visit_block(block_index, running):
        query_sum, buffer_rows = running
        first_row = block_index * key_width
        key_block = lax.dynamic_slice_in_dim(all_keys, first_row, key_width, 0)
        value_block = lax.dynamic_slice_in_dim(all_values, first_row, key_width, 0)
        query_part, partial_value = block_work(
            key_block, value_block, mask_for(first_row, key_width)
        )
        return (
            query_sum + query_part,
            lax.dynamic_update_slice_in_dim(buffer_rows, partial_value, first_row, 0),
        )

    empty_buffer = jnp.zeros((total_rows, 2 * kv_columns), jnp.float32)
    query_sum, buffer_rows = lax.fori_loop(
        0, total_rows // key_width, visit_block, (query_start, empty_buffer)
    )
    arrived = lax.all_to_all(
        buffer_rows.astype(jnp.bfloat16), "dp", split_axis=0, concat_axis=0, tiled=True
    ).astype(buffer_rows.dtype)
    own_sums = jnp.sum(arrived.reshape(-1, local_rows, 2 * kv_columns), axis=0)
    d_query = query_sum.astype(jnp.bfloat16).reshape(local_rows, kv_columns * group_size)
    key_grad = own_sums[:, :kv_columns].astype(jnp.bfloat16)
    d_value = own_sums[:, kv_columns:].astype(jnp.bfloat16)
    d_wkey = lax.psum_scatter(
        lax.dot_general(
            inputs, key_grad, (((0,), (0,)), ((), ())), preferred_element_type=jnp.float32
        ),
        "dp",
        scatter_dimension=0,
        tiled=True,
    )
    partial_input = lax.dot_general(
        key_grad, w_key, (((1,), (1,)), ((), ())), preferred_element_type=jnp.float32
    )
    d_input = lax.psum_scatter(
        partial_input.astype(jnp.bfloat16), "tensor", scatter_dimension=1, tiled=True
    )
    return (d_query, d_value, d_input, d_wkey)


CORE, Z_HI = 1, 8
GROUP = 4
ROWS = 128
TILE = 256
UNROLLED = 5
ATTEND_COST = 4_000_000_000
PART = 512
MARKED = ROWS + 16
Q_BLOCKS = GROUP * ROWS // BLK
SMEM = pltpu.SMEM
VMEM = pltpu.VMEM
HBM = pltpu.HBM
DMA = pltpu.SemaphoreType.DMA


def swap(array, mask):
    return lax.ppermute(array, "dp", [(i, i ^ mask) for i in range(16)])


def swap_tensor(array):
    return lax.ppermute(array, "tensor", [(0, 1), (1, 0)])


def own_head():
    return (lax.axis_index("dp") >> 1) & 3


def columns(index, width):
    return pl.ds(pl.multiple_of(index * width, width), width)


def whole_spec(space=VMEM):
    return pl.BlockSpec(memory_space=space)


def after(array, *earlier):
    return lax.optimization_barrier((array,) + earlier)[0]


def copy_all(pairs, semaphores):
    copies = [
        pltpu.make_async_copy(source, target, semaphores.at[i])
        for i, (source, target) in enumerate(pairs)
    ]
    for copy in copies:
        copy.start()
    return copies


def project_keys(pos_ref, inputs_ref, values_ref, w_ref, *refs):
    pair_refs = refs[:GROUP]
    inputs, weights, total, semaphores = refs[GROUP:]
    head = own_head()
    spans = [pl.ds(k * PART, PART) for k in range(weights.shape[0] // PART)]
    copies = copy_all(
        [(inputs_ref, inputs)] + [(w_ref.at[span], weights.at[span]) for span in spans],
        semaphores,
    )
    lanes = lax.broadcasted_iota(jnp.int32, (16, 2 * HD), 1)
    marks = jnp.where(lanes == 0, pos_ref[0], jnp.where(lanes == 1, pos_ref[1], 0))
    for m in range(GROUP):
        pair_refs[m][:ROWS, HD:] = values_ref[:, columns(head ^ m, HD)]
        pair_refs[m][ROWS:] = marks.astype(jnp.float32).astype(jnp.bfloat16)
    copies[0].wait()
    for k, span in enumerate(spans):
        copies[1 + k].wait()
        part = jnp.dot(inputs[:, span], weights[span], preferred_element_type=jnp.float32)
        total[...] = part if k == 0 else total[...] + part
    for m in range(GROUP):
        pair_refs[m][:ROWS, :HD] = total[:, columns(head ^ m, HD)].astype(jnp.bfloat16)


def pack_rows(queries_ref, grads_ref, *out_refs):
    head = own_head()
    for m, out_ref in enumerate(out_refs):
        span = columns(head ^ m, GROUP * HD)
        out_ref[:, : GROUP * HD] = queries_ref[:, span]
        out_ref[:, GROUP * HD :] = grads_ref[:, span]


def pack_weights(w_ref, leaving_ref, semaphore):
    first = (1 - lax.axis_index("tensor")) * 2 + (lax.axis_index("dp") & 1)
    copy = pltpu.make_async_copy(w_ref.at[columns(first, 2 * PART)], leaving_ref, semaphore)
    copy.start()
    copy.wait()


def pack_features(inputs_ref, near_ref, far_ref):
    chip = lax.axis_index("dp") >> 1
    side = lax.axis_index("tensor")
    for m in range(GROUP):
        near_ref[m] = inputs_ref[:, columns(2 * (chip ^ m) + side, 256)]
        far_ref[m] = inputs_ref[:, columns(2 * (chip ^ (m + GROUP)) + side, 256)]


def join_features(near_ref, far_ref, *joined_refs):
    for m, joined_ref in enumerate(joined_refs):
        joined_ref[0] = near_ref[m]
        joined_ref[1] = far_ref[m]


def turn_features(*refs):
    for j in range(2 * GROUP):
        turned = refs[j % GROUP][j // GROUP].astype(jnp.float32).T
        refs[-1][:, j * ROWS : (j + 1) * ROWS] = turned.astype(jnp.bfloat16)


def dot_nt(left, right):
    return lax.dot_general(
        left, right, (((1,), (1,)), ((), ())), preferred_element_type=jnp.float32
    )


def folded(array, reduce):
    return reduce(array.reshape(-1, 8, array.shape[-1]), axis=0)


def first_row_of(positions):
    def first_row(block):
        return pl.multiple_of(positions[block // 2, block % 2] * BLK, BLK)

    return first_row


def attend_rows(
    first_part, first_row, lens_ref, row_refs, dq_refs, keys, keys_t, values, dk, dv, scratch
):
    q_rows, g_rows, dq_all, scores, d_prob = scratch
    score_scale = 1.0 / math.sqrt(HD)
    base_two = score_scale * math.log2(math.e)
    parts = len(row_refs)
    for block in range(2 * parts):
        here = pl.ds(block % 2 * BLK, BLK)
        for h in range(GROUP):
            there = pl.ds(h * BLK, BLK)
            q_rows[block, there] = row_refs[block // 2][here, h * HD : (h + 1) * HD]
            g_rows[block, there] = row_refs[block // 2][
                here, (GROUP + h) * HD : (GROUP + h + 1) * HD
            ]
    starts = [lens_ref[0]]
    for k in (1, 2):
        starts.append(starts[-1] + lens_ref[k])

    def document_start(position):
        found = jnp.zeros_like(position)
        for start in starts:
            found = jnp.where(start <= position, start, found)
        return found

    zeros = jnp.zeros((8, GROUP * BLK), jnp.float32)
    last_tile = keys.shape[0] - TILE

    @pl.loop(0, parts)
    def _(part):
        blocks = [2 * part, 2 * part + 1]
        firsts = [first_row(2 * first_part + block) for block in blocks]
        lanes = lax.broadcasted_iota(jnp.int32, (1, GROUP * BLK), 1)
        positions = [first + (lanes & (BLK - 1)) for first in firsts]
        row_starts = [document_start(position) for position in positions]
        lows = [document_start(first) // HD * HD for first in firsts]
        counts = [
            (first + BLK - low + TILE - 1) // TILE for first, low in zip(firsts, lows)
        ]
        count = jnp.maximum(*counts)

        def rows_of(j, k):
            offset = jnp.minimum(lows[j] + k * TILE, last_tile)
            return pl.ds(pl.multiple_of(offset, HD), TILE)

        def run(over_tiles):
            query = [q_rows[block] for block in blocks]
            grad = [g_rows[block] for block in blocks]

            def visit_scores(k, row_max):
                seen = []
                for j in range(2):
                    here = rows_of(j, k)
                    raw = dot_nt(keys[here], query[j])
                    row = lows[j] + k * TILE + lax.broadcasted_iota(jnp.int32, raw.shape, 0)
                    allowed = (row <= positions[j]) & (row >= row_starts[j])
                    raw = jnp.where(allowed, raw, masked_fill)
                    scores[j, k] = raw
                    d_prob[j, k] = dot_nt(values[here], grad[j])
                    seen.append(jnp.maximum(row_max[j], folded(raw, jnp.max)))
                return seen

            row_max = over_tiles(visit_scores, [zeros + masked_fill] * 2)
            row_max = [jnp.max(part_max, axis=0, keepdims=True) for part_max in row_max]

            def visit_sums(k, running):
                sums = []
                for j in range(2):
                    terms = jnp.exp2((scores[j, k] - row_max[j]) * base_two)
                    scores[j, k] = terms
                    sums.append(running[2 * j] + folded(terms, jnp.sum))
                    sums.append(running[2 * j + 1] + folded(terms * d_prob[j, k], jnp.sum))
                return sums

            sums = over_tiles(visit_sums, [zeros] * 4)
            sums = [jnp.sum(part_sum, axis=0, keepdims=True) for part_sum in sums]
            inverse = [1.0 / sums[2 * j] for j in range(2)]
            delta = [sums[2 * j + 1] * inverse[j] for j in range(2)]

            def visit_grads(k, dq):
                added = []
                for j in range(2):
                    here = rows_of(j, k)
                    prob = scores[j, k] * inverse[j]
                    score_bf = (prob * (d_prob[j, k] - delta[j])).astype(jnp.bfloat16)
                    dk[here] += jnp.dot(score_bf, query[j], preferred_element_type=jnp.float32)
                    dv[here] += jnp.dot(
                        prob.astype(jnp.bfloat16), grad[j], preferred_element_type=jnp.float32
                    )
                    added.append(
                        dq[j]
                        + jnp.dot(
                            keys_t[:, here], score_bf, preferred_element_type=jnp.float32
                        )
                    )
                return added

            dq = over_tiles(visit_grads, [jnp.zeros((HD, GROUP * BLK), jnp.float32)] * 2)
            for j in range(2):
                turned = (dq[j] * score_scale).T.astype(jnp.bfloat16)
                for h in range(GROUP):
                    dq_all[blocks[j], :, h * HD : (h + 1) * HD] = turned[h * BLK : (h + 1) * BLK]

        for fixed in range(1, UNROLLED + 1):

            @pl.when(count == fixed)
            def _(fixed=fixed):
                def over_tiles(visit, running):
                    for k in range(fixed):
                        running = visit(k, running)
                    return running

                run(over_tiles)

        @pl.when(count > UNROLLED)
        def _():
            run(lambda visit, running: lax.fori_loop(0, count, visit, running))

    for block in range(2 * parts):
        dq_refs[block // 2][pl.ds(block % 2 * BLK, BLK)] = dq_all[block]


def attend_first(lens_ref, *refs):
    row_refs, refs = refs[: GROUP - 1], refs[GROUP - 1 :]
    own_a, own_b, far_a, far_b, core_pairs, refs = *refs[:5], refs[5:]
    dq_refs, refs = refs[: GROUP - 1], refs[GROUP - 1 :]
    keys, keys_t, values, dk, dv, marks, refs = *refs[:6], refs[6:]
    scratch, (positions, semaphore) = refs[:5], refs[5:]
    reach = 2 * MARKED
    pair_refs = [own_a, own_b]
    pair_refs += [core_pairs.at[pl.ds(k * reach, reach)] for k in range(2)]
    pair_refs += [far_a, far_b]
    pair_refs += [core_pairs.at[pl.ds(k * reach, reach)] for k in range(2, 4)]
    for part in range(4 * GROUP):
        here = pl.ds(part % 2 * MARKED + ROWS, 16)
        row = pair_refs[part // 2][here, :HD].astype(jnp.float32).astype(jnp.int32)
        marks[part : part + 1] = row[:1]
    to_scalars = pltpu.make_async_copy(marks, positions, semaphore)
    to_scalars.start()
    dk[...] = jnp.zeros_like(dk)
    dv[...] = jnp.zeros_like(dv)
    to_scalars.wait()
    first_row = first_row_of(positions)
    for block in range(4 * Q_BLOCKS):
        part = block // 2
        here = pl.ds(part % 2 * MARKED + block % 2 * BLK, BLK)
        there = pl.ds(first_row(block), BLK)
        keys[there] = pair_refs[part // 2][here, :HD]
        values[there] = pair_refs[part // 2][here, HD:]
    beyond = pl.ds(4 * GROUP * ROWS, HD)
    keys[beyond] = jnp.zeros((HD, HD), jnp.bfloat16)
    keys_t[:, beyond] = jnp.zeros((HD, HD), jnp.bfloat16)
    values[beyond] = jnp.zeros((HD, HD), jnp.bfloat16)
    for tile in range(keys.shape[0] // TILE):
        here = pl.ds(tile * TILE, TILE)
        keys_t[:, here] = keys[here].astype(jnp.float32).T.astype(jnp.bfloat16)
    attend_rows(
        0, first_row, lens_ref, row_refs, dq_refs, keys, keys_t, values, dk, dv, scratch
    )


def attend_last(lens_ref, row_ref, keys, keys_t, values, dk_first, dv_first, marks, *refs):
    dq_ref, kept, sent, dk, dv, refs = *refs[:5], refs[5:]
    scratch, (positions, semaphore) = refs[:5], refs[5:]
    score_scale = 1.0 / math.sqrt(HD)
    to_scalars = pltpu.make_async_copy(marks, positions, semaphore)
    to_scalars.start()
    dk[...] = dk_first[...]
    dv[...] = dv_first[...]
    to_scalars.wait()
    first_row = first_row_of(positions)
    attend_rows(
        GROUP - 1, first_row, lens_ref, [row_ref], [dq_ref], keys, keys_t, values, dk, dv, scratch
    )
    for block in range(4 * Q_BLOCKS):
        quarter = block // Q_BLOCKS
        here = pl.ds(quarter // 2 * Q_BLOCKS * BLK + block % Q_BLOCKS * BLK, BLK)
        there = pl.ds(first_row(block), BLK)
        out_ref = sent if quarter % 2 else kept
        out_ref[here, :HD] = dk[there] * score_scale
        out_ref[here, HD:] = dv[there]


def weight_grad(own_ref, other_ref, *refs):
    grad_refs, (keep_ref, send_ref, grads) = refs[:GROUP], refs[GROUP:]
    head = own_head()
    for k, grad_ref in enumerate(grad_refs):
        for far in range(2):
            for m in range(GROUP):
                here = pl.ds((far * GROUP + m) * ROWS, ROWS)
                there = pl.ds((far * GROUP + (m ^ k)) * ROWS, ROWS)
                grads[here, columns(head ^ k, HD)] = grad_ref[there]
    own = jnp.dot(own_ref[...], grads[...], preferred_element_type=jnp.float32)
    other = jnp.dot(other_ref[...], grads[...], preferred_element_type=jnp.float32)
    crossed = (lax.axis_index("dp") & 1) ^ lax.axis_index("tensor")

    @pl.when(crossed == 0)
    def _():
        keep_ref[...] = own
        send_ref[...] = other

    @pl.when(crossed == 1)
    def _():
        keep_ref[...] = other
        send_ref[...] = own


def input_grad(own_ref, other_ref, w_own, w_near, w_far, out_ref, own_all, other_all):
    head = own_head()
    core = lax.axis_index("dp") & 1
    side = lax.axis_index("tensor")
    for k in range(GROUP):
        own_all[:, columns(head ^ k, HD)] = own_ref[k]
        other_all[:, columns(head ^ k, HD)] = other_ref[k]
    for k in range(4):
        chunk = 2 * (core ^ (k // 2)) + k % 2
        w_other = (w_near, w_far)[k // 2][pl.ds(k % 2 * PART, PART)]
        part = dot_nt(own_all[...], w_own[columns(side * 4 + chunk, PART)])
        part = part + dot_nt(other_all[...], w_other)
        out_ref[:, columns(chunk, PART)] = part.astype(jnp.bfloat16)


def pack_grads(value_ref, *refs):
    for m, out_ref in enumerate(refs):
        out_ref[...] = value_ref[m * ROWS : (m + 1) * ROWS]


def finish(keep_ref, arrived_ref, *refs):
    row_refs, value_refs, refs = refs[:GROUP], refs[GROUP : 2 * GROUP], refs[2 * GROUP :]
    weight_out, query_out, value_out = refs
    head = own_head()
    weight_out[...] = keep_ref[...] + arrived_ref[...]
    for m in range(GROUP):
        query_out[:, columns(head ^ m, GROUP * HD)] = row_refs[m][...]
        value_out[:, columns(head ^ m, HD)] = value_refs[m][...]


def shaped(shape, dtype=jnp.bfloat16):
    return jax.ShapeDtypeStruct(shape, dtype)


def limits(mebibytes):
    return pltpu.CompilerParams(vmem_limit_bytes=mebibytes << 20)


def with_partners(arrays):
    return [arrays[0]] + [swap(arrays[m], 2 * m) for m in range(1, len(arrays))]


def on_device_by_heads(inputs, w_key, values, queries, d_out, doc_lens, block_pos):
    features = inputs.shape[1]
    kv_columns = values.shape[1]
    total_rows = 16 * ROWS
    half, quarter = total_rows // 2, total_rows // 4
    vmem, smem, hbm = whole_spec(), whole_spec(SMEM), whole_spec(HBM)

    pairs = pl.pallas_call(
        project_keys,
        out_shape=[shaped((MARKED, 2 * HD))] * GROUP,
        in_specs=[smem, hbm, vmem, hbm],
        out_specs=[vmem] * GROUP,
        scratch_shapes=[
            VMEM((ROWS, features), jnp.bfloat16),
            VMEM((features, kv_columns), jnp.bfloat16),
            VMEM((ROWS, kv_columns), jnp.float32),
            DMA((1 + features // PART,)),
        ],
        compiler_params=limits(60),
        cost_estimate=pl.CostEstimate(
            flops=2 * ROWS * features * kv_columns,
            bytes_accessed=features * kv_columns * 2,
            transcendentals=0,
        ),
        name="project_keys",
    )(block_pos, inputs, values, w_key)

    packed_rows = pl.pallas_call(
        pack_rows,
        out_shape=[shaped((ROWS, 2 * GROUP * HD))] * GROUP,
        in_specs=[vmem] * 2,
        out_specs=[vmem] * GROUP,
        compiler_params=limits(8),
        name="pack_rows",
    )(after(queries, pairs[0]), d_out)

    pairs = [after(pairs[0], packed_rows[0])] + list(pairs[1:])
    pairs = with_partners(pairs)
    own_a = jnp.concatenate(pairs[:2], axis=0)
    own_b = jnp.concatenate(pairs[2:], axis=0)
    far_a = swap(own_a, Z_HI)
    far_b = swap(own_b, Z_HI)
    rows = with_partners(packed_rows)

    near_features, far_features = pl.pallas_call(
        pack_features,
        out_shape=[shaped((GROUP, ROWS, 256))] * 2,
        in_specs=[vmem],
        out_specs=[vmem] * 2,
        compiler_params=limits(8),
        name="pack_features",
    )(after(inputs, own_a))
    leaving = pl.pallas_call(
        pack_weights,
        out_shape=shaped((2 * PART, kv_columns)),
        in_specs=[hbm],
        out_specs=vmem,
        scratch_shapes=[DMA],
        compiler_params=limits(56),
        name="pack_weights",
    )(after(w_key, own_b))
    w_near = swap_tensor(leaving)
    near_pairs = jnp.concatenate([own_a, own_b, far_a, far_b], axis=0)
    core_pairs = swap(after(near_pairs, near_features, leaving, rows[1], rows[2]), CORE)
    far_features = swap(far_features, Z_HI)

    row_grad = shaped((ROWS, GROUP * HD))
    padded_rows = total_rows + HD
    sorted_rows = shaped((padded_rows, HD))
    sums = shaped((padded_rows, HD), jnp.float32)
    half_sums = shaped((half, 2 * HD), jnp.float32)

    def attend_scratch(blocks):
        stacked = VMEM((blocks, GROUP * BLK, HD), jnp.bfloat16)
        tiles = VMEM((2, total_rows // TILE, TILE, GROUP * BLK), jnp.float32)
        return [
            stacked,
            stacked,
            VMEM((blocks, BLK, GROUP * HD), jnp.bfloat16),
            tiles,
            tiles,
            SMEM((4 * GROUP, HD), jnp.int32),
            DMA,
        ]

    *row_grads, keys, keys_t, all_values, dk_first, dv_first, marks = pl.pallas_call(
        attend_first,
        out_shape=[row_grad] * (GROUP - 1)
        + [sorted_rows, shaped((HD, padded_rows)), sorted_rows, sums, sums]
        + [shaped((4 * GROUP, HD), jnp.int32)],
        in_specs=[smem] + [vmem] * (GROUP + 4),
        out_specs=[vmem] * (GROUP + 5),
        scratch_shapes=attend_scratch(Q_BLOCKS - 2),
        compiler_params=limits(24),
        cost_estimate=pl.CostEstimate(flops=ATTEND_COST, bytes_accessed=0, transcendentals=0),
        name="attend_first",
    )(doc_lens, *rows[:-1], own_a, own_b, far_a, far_b, core_pairs)
    last_grad, kept, sent = pl.pallas_call(
        attend_last,
        out_shape=[row_grad, half_sums, half_sums],
        in_specs=[smem] + [vmem] * 7,
        out_specs=[vmem] * 3,
        scratch_shapes=[VMEM((padded_rows, HD), jnp.float32)] * 2 + attend_scratch(2),
        compiler_params=limits(24),
        cost_estimate=pl.CostEstimate(flops=ATTEND_COST, bytes_accessed=0, transcendentals=0),
        name="attend_last",
    )(doc_lens, after(rows[-1], w_near), keys, keys_t, all_values, dk_first, dv_first, marks)

    row_grads = with_partners(row_grads)
    sent = after(sent, far_features, *row_grads)
    grads = kept + swap(sent, CORE)
    dk_sum, dv_sum = grads[:, :HD], grads[:, HD:]
    dk_far = swap(dk_sum.astype(jnp.bfloat16), Z_HI)
    w_far = swap(after(w_near, sent), CORE)

    feature_parts = pl.pallas_call(
        join_features,
        out_shape=[shaped((2, ROWS, 256))] * GROUP,
        in_specs=[vmem] * 2,
        out_specs=[vmem] * GROUP,
        compiler_params=limits(16),
        name="join_features",
    )(after(near_features, sent), far_features)
    own_features = pl.pallas_call(
        turn_features,
        out_shape=shaped((256, half)),
        in_specs=[vmem] * GROUP,
        out_specs=vmem,
        compiler_params=limits(16),
        cost_estimate=pl.CostEstimate(flops=2_000_000_000, bytes_accessed=0, transcendentals=0),
        name="turn_features",
    )(*with_partners(feature_parts))
    other_features = swap_tensor(own_features)

    dk_far = jnp.concatenate([dk_far[quarter:], dk_far[:quarter]], axis=0)
    key_grad = (dk_sum + dk_far.astype(jnp.float32)).astype(jnp.bfloat16)
    last_grad = swap(after(last_grad, dk_sum), 6)
    key_grad = after(key_grad, own_features, w_far, last_grad)
    key_grads = with_partners([key_grad] * GROUP)
    own_key_grad = jnp.stack([key_grads[m][m * ROWS : (m + 1) * ROWS] for m in range(GROUP)])
    other_key_grad = swap_tensor(own_key_grad)

    dv_far = swap(after(dv_sum[quarter:].astype(jnp.bfloat16), key_grad), Z_HI)
    value_grad = (dv_sum[:quarter] + dv_far.astype(jnp.float32)).astype(jnp.bfloat16)
    packed_grads = pl.pallas_call(
        pack_grads,
        out_shape=[shaped((ROWS, HD))] * GROUP,
        in_specs=[vmem],
        out_specs=[vmem] * GROUP,
        compiler_params=limits(16),
        name="pack_grads",
    )(value_grad)
    packed_grads = [after(packed_grads[0], own_key_grad)] + [
        after(grad, own_key_grad) for grad in packed_grads[1:]
    ]

    keep, send = pl.pallas_call(
        weight_grad,
        out_shape=[shaped((256, kv_columns), jnp.float32)] * 2,
        in_specs=[vmem] * (2 + GROUP),
        out_specs=[vmem] * 2,
        scratch_shapes=[VMEM((half, kv_columns), jnp.bfloat16)],
        compiler_params=limits(24),
        cost_estimate=pl.CostEstimate(
            flops=4 * 256 * half * kv_columns, bytes_accessed=4 << 20, transcendentals=0
        ),
        name="weight_grad",
    )(own_features, other_features, *key_grads)
    arrived = swap(send, CORE)

    d_input = pl.pallas_call(
        input_grad,
        out_shape=shaped((ROWS, features // 2)),
        in_specs=[vmem] * 5,
        out_specs=vmem,
        scratch_shapes=[VMEM((ROWS, kv_columns), jnp.bfloat16)] * 2,
        compiler_params=limits(16),
        cost_estimate=pl.CostEstimate(
            flops=8_000_000_000, bytes_accessed=5 << 20, transcendentals=0
        ),
        name="input_grad",
    )(after(own_key_grad, send), other_key_grad, w_key, w_near, w_far)

    d_wkey, d_query, d_value = pl.pallas_call(
        finish,
        out_shape=[
            shaped((256, kv_columns), jnp.float32),
            shaped(queries.shape),
            shaped(values.shape),
        ],
        in_specs=[vmem] * (2 + 2 * GROUP),
        out_specs=[vmem] * 3,
        compiler_params=limits(16),
        name="finish",
    )(keep, arrived, *row_grads, last_grad, *with_partners(packed_grads))
    return (d_query, d_value, d_input, d_wkey)


def solution(mesh):
    by_heads = mesh.shape["dp"] == 16 and mesh.shape["tensor"] == 2
    return jax.shard_map(
        on_device_by_heads if by_heads else on_device,
        mesh=mesh,
        in_specs=(
            P("dp", None),
            P(None, "tensor"),
            P("dp", "tensor"),
            P("dp", "tensor"),
            P("dp", "tensor"),
            P(),
            P("dp"),
        ),
        out_specs=(P("dp", "tensor"), P("dp", "tensor"), P("dp", "tensor"), P("dp", "tensor")),
        check_vma=False,
    )
```

```python
import math

import jax
import jax.numpy as jnp
from jax import lax
from jax.experimental import pallas as pl
from jax.experimental.pallas import tpu as pltpu
from jax.sharding import PartitionSpec as P

HD = 128
BLK = 64


masked_fill = -1e30


def row_positions(block_pos):
    within = jnp.tile(jnp.arange(BLK, dtype=jnp.int32), block_pos.shape[0])
    return jnp.repeat(block_pos, BLK) * BLK + within


def documents(positions, doc_lens):
    starts = jnp.cumsum(doc_lens) - doc_lens
    return jnp.sum((positions[:, None] >= starts[None, :]).astype(jnp.int32), axis=1) - 1


def split_heads(block_rows, kv_heads):
    return block_rows.reshape(block_rows.shape[0], kv_heads, HD)


def scored(query_heads, key_block, score_scale):
    key_split = split_heads(key_block, query_heads.shape[1])
    return (
        jnp.einsum("qcgd,kcd->cgqk", query_heads, key_split, preferred_element_type=jnp.float32)
        * score_scale
    )


def contributions(
    query_heads, grad_heads, key_block, value_block, allowed, row_max, row_sum, delta, score_scale
):
    kv_heads = query_heads.shape[1]
    key_split = split_heads(key_block, kv_heads)
    value_split = split_heads(value_block, kv_heads)
    scores = scored(query_heads, key_block, score_scale)
    mask_full = allowed[None, None]
    probabilities = (
        jnp.where(mask_full, jnp.exp(scores - row_max[..., None]), 0.0) / row_sum[..., None]
    )
    d_prob = jnp.einsum(
        "qcgd,kcd->cgqk", grad_heads, value_split, preferred_element_type=jnp.float32
    )
    d_score = probabilities * (d_prob - delta[..., None])
    prob_bf = probabilities.astype(jnp.bfloat16)
    score_bf = d_score.astype(jnp.bfloat16)
    query_part = score_scale * jnp.einsum(
        "cgqk,kcd->qcgd", score_bf, key_split, preferred_element_type=jnp.float32
    )
    key_part = score_scale * jnp.einsum(
        "cgqk,qcgd->kcd", score_bf, query_heads, preferred_element_type=jnp.float32
    )
    value_part = jnp.einsum(
        "cgqk,qcgd->kcd", prob_bf, grad_heads, preferred_element_type=jnp.float32
    )
    width_rows = key_block.shape[0]
    partial_value = jnp.concatenate(
        [key_part.reshape(width_rows, -1), value_part.reshape(width_rows, -1)], axis=1
    )
    return (query_part, partial_value)


def on_device(inputs, w_key, values, queries, d_out, doc_lens, block_pos):
    local_rows = inputs.shape[0]
    kv_heads = values.shape[1] // HD
    group_size = queries.shape[1] // (kv_heads * HD)
    kv_columns = kv_heads * HD
    score_scale = 1.0 / math.sqrt(HD)
    key_rows = jnp.dot(inputs, w_key, preferred_element_type=jnp.float32).astype(jnp.bfloat16)
    all_keys, all_values, all_blocks = (
        lax.all_gather(key_rows, "dp", axis=0, tiled=True),
        lax.all_gather(values, "dp", axis=0, tiled=True),
        lax.all_gather(block_pos, "dp", axis=0, tiled=True),
    )
    key_pos = row_positions(all_blocks)
    key_doc = documents(key_pos, doc_lens)
    query_pos = row_positions(block_pos)
    query_doc = documents(query_pos, doc_lens)
    query_heads = queries.reshape(local_rows, kv_heads, group_size, HD)
    grad_heads = d_out.reshape(local_rows, kv_heads, group_size, HD)
    total_rows = all_keys.shape[0]
    key_width = math.gcd(512, total_rows)
    stat_shape = (kv_heads, group_size, local_rows)

    def mask_for(first_row, width_rows):
        pos_here = lax.dynamic_slice_in_dim(key_pos, first_row, width_rows, 0)
        doc_here = lax.dynamic_slice_in_dim(key_doc, first_row, width_rows, 0)
        return (query_doc[:, None] == doc_here[None, :]) & (pos_here[None, :] <= query_pos[:, None])

    def visit_stats(block_index, running):
        first_row = block_index * key_width
        key_block = lax.dynamic_slice_in_dim(all_keys, first_row, key_width, 0)
        value_block = lax.dynamic_slice_in_dim(all_values, first_row, key_width, 0)
        allowed = mask_for(first_row, key_width)

        def visit_compute_live(state_now):
            row_max, row_sum, weighted = state_now
            scores = scored(query_heads, key_block, score_scale)
            mask_full = allowed[None, None]
            new_max = jnp.maximum(
                row_max, jnp.max(jnp.where(mask_full, scores, masked_fill), axis=3)
            )
            exp_terms = jnp.where(mask_full, jnp.exp(scores - new_max[..., None]), 0.0)
            d_prob = jnp.einsum(
                "qcgd,kcd->cgqk",
                grad_heads,
                split_heads(value_block, kv_heads),
                preferred_element_type=jnp.float32,
            )
            shrink = jnp.exp(row_max - new_max)
            return (
                new_max,
                row_sum * shrink + jnp.sum(exp_terms, axis=3),
                weighted * shrink + jnp.sum(exp_terms * d_prob, axis=3),
            )

        return lax.cond(jnp.any(allowed), visit_compute_live, lambda state_now: state_now, running)

    start_state = (
        jnp.full(stat_shape, masked_fill, jnp.float32),
        jnp.zeros(stat_shape, jnp.float32),
        jnp.zeros(stat_shape, jnp.float32),
    )
    row_max, row_sum, weighted = lax.fori_loop(0, total_rows // key_width, visit_stats, start_state)
    delta = weighted / row_sum

    def block_work(key_block, value_block, allowed):
        width_rows = key_block.shape[0]

        def block_compute_live(operands):
            return contributions(
                query_heads,
                grad_heads,
                operands[0],
                operands[1],
                operands[2],
                row_max,
                row_sum,
                delta,
                score_scale,
            )

        def dead_block(operands):
            return (
                jnp.zeros((local_rows, kv_heads, group_size, HD), jnp.float32),
                jnp.zeros((width_rows, 2 * kv_columns), jnp.float32),
            )

        return lax.cond(
            jnp.any(allowed), block_compute_live, dead_block, (key_block, value_block, allowed)
        )

    query_start = jnp.zeros((local_rows, kv_heads, group_size, HD), jnp.float32)

    def visit_block(block_index, running):
        query_sum, buffer_rows = running
        first_row = block_index * key_width
        key_block = lax.dynamic_slice_in_dim(all_keys, first_row, key_width, 0)
        value_block = lax.dynamic_slice_in_dim(all_values, first_row, key_width, 0)
        query_part, partial_value = block_work(
            key_block, value_block, mask_for(first_row, key_width)
        )
        return (
            query_sum + query_part,
            lax.dynamic_update_slice_in_dim(buffer_rows, partial_value, first_row, 0),
        )

    empty_buffer = jnp.zeros((total_rows, 2 * kv_columns), jnp.float32)
    query_sum, buffer_rows = lax.fori_loop(
        0, total_rows // key_width, visit_block, (query_start, empty_buffer)
    )
    arrived = lax.all_to_all(
        buffer_rows.astype(jnp.bfloat16), "dp", split_axis=0, concat_axis=0, tiled=True
    ).astype(buffer_rows.dtype)
    own_sums = jnp.sum(arrived.reshape(-1, local_rows, 2 * kv_columns), axis=0)
    d_query = query_sum.astype(jnp.bfloat16).reshape(local_rows, kv_columns * group_size)
    key_grad = own_sums[:, :kv_columns].astype(jnp.bfloat16)
    d_value = own_sums[:, kv_columns:].astype(jnp.bfloat16)
    d_wkey = lax.psum_scatter(
        lax.dot_general(
            inputs, key_grad, (((0,), (0,)), ((), ())), preferred_element_type=jnp.float32
        ),
        "dp",
        scatter_dimension=0,
        tiled=True,
    )
    partial_input = lax.dot_general(
        key_grad, w_key, (((1,), (1,)), ((), ())), preferred_element_type=jnp.float32
    )
    d_input = lax.psum_scatter(
        partial_input.astype(jnp.bfloat16), "tensor", scatter_dimension=1, tiled=True
    )
    return (d_query, d_value, d_input, d_wkey)


CORE, Z_HI = 1, 8
GROUP = 4
ROWS = 128
TILE = 256
UNROLLED = 5
ATTEND_COST = 4_000_000_000
PART = 512
MARKED = ROWS + 16
Q_BLOCKS = GROUP * ROWS // BLK
SMEM = pltpu.SMEM
VMEM = pltpu.VMEM
HBM = pltpu.HBM
DMA = pltpu.SemaphoreType.DMA


def swap(array, mask):
    return lax.ppermute(array, "dp", [(i, i ^ mask) for i in range(16)])


def swap_tensor(array):
    return lax.ppermute(array, "tensor", [(0, 1), (1, 0)])


def own_head():
    return (lax.axis_index("dp") >> 1) & 3


def columns(index, width):
    return pl.ds(pl.multiple_of(index * width, width), width)


def whole_spec(space=VMEM):
    return pl.BlockSpec(memory_space=space)


def after(array, *earlier):
    return lax.optimization_barrier((array,) + earlier)[0]


def copy_all(pairs, semaphores):
    copies = [
        pltpu.make_async_copy(source, target, semaphores.at[i])
        for i, (source, target) in enumerate(pairs)
    ]
    for copy in copies:
        copy.start()
    return copies


def project_keys(pos_ref, inputs_ref, values_ref, w_ref, *refs):
    pair_refs = refs[:GROUP]
    inputs, weights, total, semaphores = refs[GROUP:]
    head = own_head()
    spans = [pl.ds(k * PART, PART) for k in range(weights.shape[0] // PART)]
    copies = copy_all(
        [(inputs_ref, inputs)] + [(w_ref.at[span], weights.at[span]) for span in spans],
        semaphores,
    )
    lanes = lax.broadcasted_iota(jnp.int32, (16, 2 * HD), 1)
    marks = jnp.where(lanes == 0, pos_ref[0], jnp.where(lanes == 1, pos_ref[1], 0))
    for m in range(GROUP):
        pair_refs[m][:ROWS, HD:] = values_ref[:, columns(head ^ m, HD)]
        pair_refs[m][ROWS:] = marks.astype(jnp.float32).astype(jnp.bfloat16)
    copies[0].wait()
    for k, span in enumerate(spans):
        copies[1 + k].wait()
        part = jnp.dot(inputs[:, span], weights[span], preferred_element_type=jnp.float32)
        total[...] = part if k == 0 else total[...] + part
    for m in range(GROUP):
        pair_refs[m][:ROWS, :HD] = total[:, columns(head ^ m, HD)].astype(jnp.bfloat16)


def pack_rows(queries_ref, grads_ref, *out_refs):
    head = own_head()
    for m, out_ref in enumerate(out_refs):
        span = columns(head ^ m, GROUP * HD)
        out_ref[:, : GROUP * HD] = queries_ref[:, span]
        out_ref[:, GROUP * HD :] = grads_ref[:, span]


def pack_weights(w_ref, leaving_ref, semaphore):
    first = (1 - lax.axis_index("tensor")) * 2 + (lax.axis_index("dp") & 1)
    copy = pltpu.make_async_copy(w_ref.at[columns(first, 2 * PART)], leaving_ref, semaphore)
    copy.start()
    copy.wait()


def pack_features(inputs_ref, near_ref, far_ref):
    chip = lax.axis_index("dp") >> 1
    side = lax.axis_index("tensor")
    for m in range(GROUP):
        near_ref[m] = inputs_ref[:, columns(2 * (chip ^ m) + side, 256)]
        far_ref[m] = inputs_ref[:, columns(2 * (chip ^ (m + GROUP)) + side, 256)]


def join_features(near_ref, far_ref, *joined_refs):
    for m, joined_ref in enumerate(joined_refs):
        joined_ref[0] = near_ref[m]
        joined_ref[1] = far_ref[m]


def turn_features(*refs):
    for j in range(2 * GROUP):
        turned = refs[j % GROUP][j // GROUP].astype(jnp.float32).T
        refs[-1][:, j * ROWS : (j + 1) * ROWS] = turned.astype(jnp.bfloat16)


def dot_nt(left, right):
    return lax.dot_general(
        left, right, (((1,), (1,)), ((), ())), preferred_element_type=jnp.float32
    )


def folded(array, reduce):
    return reduce(array.reshape(-1, 8, array.shape[-1]), axis=0)


def first_row_of(positions):
    def first_row(block):
        return pl.multiple_of(positions[block // 2, block % 2] * BLK, BLK)

    return first_row


def attend_rows(
    first_part, first_row, lens_ref, row_refs, dq_refs, keys, keys_t, values, dk, dv, scratch
):
    q_rows, g_rows, dq_all, scores, d_prob = scratch
    score_scale = 1.0 / math.sqrt(HD)
    base_two = score_scale * math.log2(math.e)
    parts = len(row_refs)
    for block in range(2 * parts):
        here = pl.ds(block % 2 * BLK, BLK)
        for h in range(GROUP):
            there = pl.ds(h * BLK, BLK)
            q_rows[block, there] = row_refs[block // 2][here, h * HD : (h + 1) * HD]
            g_rows[block, there] = row_refs[block // 2][
                here, (GROUP + h) * HD : (GROUP + h + 1) * HD
            ]
    starts = [lens_ref[0]]
    for k in (1, 2):
        starts.append(starts[-1] + lens_ref[k])

    def document_start(position):
        found = jnp.zeros_like(position)
        for start in starts:
            found = jnp.where(start <= position, start, found)
        return found

    zeros = jnp.zeros((8, GROUP * BLK), jnp.float32)
    last_tile = keys.shape[0] - TILE

    @pl.loop(0, parts)
    def _(part):
        blocks = [2 * part, 2 * part + 1]
        firsts = [first_row(2 * first_part + block) for block in blocks]
        lanes = lax.broadcasted_iota(jnp.int32, (1, GROUP * BLK), 1)
        positions = [first + (lanes & (BLK - 1)) for first in firsts]
        row_starts = [document_start(position) for position in positions]
        lows = [document_start(first) // HD * HD for first in firsts]
        counts = [
            (first + BLK - low + TILE - 1) // TILE for first, low in zip(firsts, lows)
        ]
        count = jnp.maximum(*counts)

        def rows_of(j, k):
            offset = jnp.minimum(lows[j] + k * TILE, last_tile)
            return pl.ds(pl.multiple_of(offset, HD), TILE)

        def run(over_tiles):
            query = [q_rows[block] for block in blocks]
            grad = [g_rows[block] for block in blocks]

            def visit_scores(k, row_max):
                seen = []
                for j in range(2):
                    here = rows_of(j, k)
                    raw = dot_nt(keys[here], query[j])
                    row = lows[j] + k * TILE + lax.broadcasted_iota(jnp.int32, raw.shape, 0)
                    allowed = (row <= positions[j]) & (row >= row_starts[j])
                    raw = jnp.where(allowed, raw, masked_fill)
                    scores[j, k] = raw
                    d_prob[j, k] = dot_nt(values[here], grad[j])
                    seen.append(jnp.maximum(row_max[j], folded(raw, jnp.max)))
                return seen

            row_max = over_tiles(visit_scores, [zeros + masked_fill] * 2)
            row_max = [jnp.max(part_max, axis=0, keepdims=True) for part_max in row_max]

            def visit_sums(k, running):
                sums = []
                for j in range(2):
                    terms = jnp.exp2((scores[j, k] - row_max[j]) * base_two)
                    scores[j, k] = terms
                    sums.append(running[2 * j] + folded(terms, jnp.sum))
                    sums.append(running[2 * j + 1] + folded(terms * d_prob[j, k], jnp.sum))
                return sums

            sums = over_tiles(visit_sums, [zeros] * 4)
            sums = [jnp.sum(part_sum, axis=0, keepdims=True) for part_sum in sums]
            inverse = [1.0 / sums[2 * j] for j in range(2)]
            delta = [sums[2 * j + 1] * inverse[j] for j in range(2)]

            def visit_grads(k, dq):
                added = []
                for j in range(2):
                    here = rows_of(j, k)
                    prob = scores[j, k] * inverse[j]
                    score_bf = (prob * (d_prob[j, k] - delta[j])).astype(jnp.bfloat16)
                    dk[here] += jnp.dot(score_bf, query[j], preferred_element_type=jnp.float32)
                    dv[here] += jnp.dot(
                        prob.astype(jnp.bfloat16), grad[j], preferred_element_type=jnp.float32
                    )
                    added.append(
                        dq[j]
                        + jnp.dot(
                            keys_t[:, here], score_bf, preferred_element_type=jnp.float32
                        )
                    )
                return added

            dq = over_tiles(visit_grads, [jnp.zeros((HD, GROUP * BLK), jnp.float32)] * 2)
            for j in range(2):
                turned = (dq[j] * score_scale).T.astype(jnp.bfloat16)
                for h in range(GROUP):
                    dq_all[blocks[j], :, h * HD : (h + 1) * HD] = turned[h * BLK : (h + 1) * BLK]

        for fixed in range(1, UNROLLED + 1):

            @pl.when(count == fixed)
            def _(fixed=fixed):
                def over_tiles(visit, running):
                    for k in range(fixed):
                        running = visit(k, running)
                    return running

                run(over_tiles)

        @pl.when(count > UNROLLED)
        def _():
            run(lambda visit, running: lax.fori_loop(0, count, visit, running))

    for block in range(2 * parts):
        dq_refs[block // 2][pl.ds(block % 2 * BLK, BLK)] = dq_all[block]


def attend_first(lens_ref, *refs):
    row_refs, refs = refs[: GROUP - 1], refs[GROUP - 1 :]
    own_a, own_b, far_a, far_b, core_pairs, refs = *refs[:5], refs[5:]
    dq_refs, refs = refs[: GROUP - 1], refs[GROUP - 1 :]
    keys, keys_t, values, dk, dv, marks, refs = *refs[:6], refs[6:]
    scratch, (positions, semaphore) = refs[:5], refs[5:]
    reach = 2 * MARKED
    pair_refs = [own_a, own_b]
    pair_refs += [core_pairs.at[pl.ds(k * reach, reach)] for k in range(2)]
    pair_refs += [far_a, far_b]
    pair_refs += [core_pairs.at[pl.ds(k * reach, reach)] for k in range(2, 4)]
    for part in range(4 * GROUP):
        here = pl.ds(part % 2 * MARKED + ROWS, 16)
        row = pair_refs[part // 2][here, :HD].astype(jnp.float32).astype(jnp.int32)
        marks[part : part + 1] = row[:1]
    to_scalars = pltpu.make_async_copy(marks, positions, semaphore)
    to_scalars.start()
    dk[...] = jnp.zeros_like(dk)
    dv[...] = jnp.zeros_like(dv)
    to_scalars.wait()
    first_row = first_row_of(positions)
    for block in range(4 * Q_BLOCKS):
        part = block // 2
        here = pl.ds(part % 2 * MARKED + block % 2 * BLK, BLK)
        there = pl.ds(first_row(block), BLK)
        keys[there] = pair_refs[part // 2][here, :HD]
        values[there] = pair_refs[part // 2][here, HD:]
    beyond = pl.ds(4 * GROUP * ROWS, HD)
    keys[beyond] = jnp.zeros((HD, HD), jnp.bfloat16)
    keys_t[:, beyond] = jnp.zeros((HD, HD), jnp.bfloat16)
    values[beyond] = jnp.zeros((HD, HD), jnp.bfloat16)
    for tile in range(keys.shape[0] // TILE):
        here = pl.ds(tile * TILE, TILE)
        keys_t[:, here] = keys[here].astype(jnp.float32).T.astype(jnp.bfloat16)
    attend_rows(
        0, first_row, lens_ref, row_refs, dq_refs, keys, keys_t, values, dk, dv, scratch
    )


def attend_last(lens_ref, row_ref, keys, keys_t, values, dk_first, dv_first, marks, *refs):
    dq_ref, kept, sent, dk, dv, refs = *refs[:5], refs[5:]
    scratch, (positions, semaphore) = refs[:5], refs[5:]
    score_scale = 1.0 / math.sqrt(HD)
    to_scalars = pltpu.make_async_copy(marks, positions, semaphore)
    to_scalars.start()
    dk[...] = dk_first[...]
    dv[...] = dv_first[...]
    to_scalars.wait()
    first_row = first_row_of(positions)
    attend_rows(
        GROUP - 1, first_row, lens_ref, [row_ref], [dq_ref], keys, keys_t, values, dk, dv, scratch
    )
    for block in range(4 * Q_BLOCKS):
        quarter = block // Q_BLOCKS
        here = pl.ds(quarter // 2 * Q_BLOCKS * BLK + block % Q_BLOCKS * BLK, BLK)
        there = pl.ds(first_row(block), BLK)
        out_ref = sent if quarter % 2 else kept
        out_ref[here, :HD] = dk[there] * score_scale
        out_ref[here, HD:] = dv[there]


def weight_grad(own_ref, other_ref, *refs):
    grad_refs, (keep_ref, send_ref, grads) = refs[:GROUP], refs[GROUP:]
    head = own_head()
    for k, grad_ref in enumerate(grad_refs):
        for far in range(2):
            for m in range(GROUP):
                here = pl.ds((far * GROUP + m) * ROWS, ROWS)
                there = pl.ds((far * GROUP + (m ^ k)) * ROWS, ROWS)
                grads[here, columns(head ^ k, HD)] = grad_ref[there]
    own = jnp.dot(own_ref[...], grads[...], preferred_element_type=jnp.float32)
    other = jnp.dot(other_ref[...], grads[...], preferred_element_type=jnp.float32)
    crossed = (lax.axis_index("dp") & 1) ^ lax.axis_index("tensor")

    @pl.when(crossed == 0)
    def _():
        keep_ref[...] = own
        send_ref[...] = other

    @pl.when(crossed == 1)
    def _():
        keep_ref[...] = other
        send_ref[...] = own


def input_grad(own_ref, other_ref, w_own, w_near, w_far, out_ref, own_all, other_all):
    head = own_head()
    core = lax.axis_index("dp") & 1
    side = lax.axis_index("tensor")
    for k in range(GROUP):
        own_all[:, columns(head ^ k, HD)] = own_ref[k]
        other_all[:, columns(head ^ k, HD)] = other_ref[k]
    for k in range(4):
        chunk = 2 * (core ^ (k // 2)) + k % 2
        w_other = (w_near, w_far)[k // 2][pl.ds(k % 2 * PART, PART)]
        part = dot_nt(own_all[...], w_own[columns(side * 4 + chunk, PART)])
        part = part + dot_nt(other_all[...], w_other)
        out_ref[:, columns(chunk, PART)] = part.astype(jnp.bfloat16)


def pack_grads(value_ref, *refs):
    for m, out_ref in enumerate(refs):
        out_ref[...] = value_ref[m * ROWS : (m + 1) * ROWS]


def finish(keep_ref, arrived_ref, *refs):
    row_refs, value_refs, refs = refs[:GROUP], refs[GROUP : 2 * GROUP], refs[2 * GROUP :]
    weight_out, query_out, value_out = refs
    head = own_head()
    weight_out[...] = keep_ref[...] + arrived_ref[...]
    for m in range(GROUP):
        query_out[:, columns(head ^ m, GROUP * HD)] = row_refs[m][...]
        value_out[:, columns(head ^ m, HD)] = value_refs[m][...]


def shaped(shape, dtype=jnp.bfloat16):
    return jax.ShapeDtypeStruct(shape, dtype)


def limits(mebibytes):
    return pltpu.CompilerParams(vmem_limit_bytes=mebibytes << 20)


def with_partners(arrays):
    return [arrays[0]] + [swap(arrays[m], 2 * m) for m in range(1, len(arrays))]


def on_device_by_heads(inputs, w_key, values, queries, d_out, doc_lens, block_pos):
    features = inputs.shape[1]
    kv_columns = values.shape[1]
    total_rows = 16 * ROWS
    half, quarter = total_rows // 2, total_rows // 4
    vmem, smem, hbm = whole_spec(), whole_spec(SMEM), whole_spec(HBM)

    pairs = pl.pallas_call(
        project_keys,
        out_shape=[shaped((MARKED, 2 * HD))] * GROUP,
        in_specs=[smem, hbm, vmem, hbm],
        out_specs=[vmem] * GROUP,
        scratch_shapes=[
            VMEM((ROWS, features), jnp.bfloat16),
            VMEM((features, kv_columns), jnp.bfloat16),
            VMEM((ROWS, kv_columns), jnp.float32),
            DMA((1 + features // PART,)),
        ],
        compiler_params=limits(60),
        cost_estimate=pl.CostEstimate(
            flops=2 * ROWS * features * kv_columns,
            bytes_accessed=features * kv_columns * 2,
            transcendentals=0,
        ),
        name="project_keys",
    )(block_pos, inputs, values, w_key)

    packed_rows = pl.pallas_call(
        pack_rows,
        out_shape=[shaped((ROWS, 2 * GROUP * HD))] * GROUP,
        in_specs=[vmem] * 2,
        out_specs=[vmem] * GROUP,
        compiler_params=limits(8),
        name="pack_rows",
    )(after(queries, pairs[0]), d_out)

    pairs = [after(pairs[0], packed_rows[0])] + list(pairs[1:])
    pairs = with_partners(pairs)
    own_a = jnp.concatenate(pairs[:2], axis=0)
    own_b = jnp.concatenate(pairs[2:], axis=0)
    far_a = swap(own_a, Z_HI)
    far_b = swap(own_b, Z_HI)
    rows = with_partners(packed_rows)

    near_features, far_features = pl.pallas_call(
        pack_features,
        out_shape=[shaped((GROUP, ROWS, 256))] * 2,
        in_specs=[vmem],
        out_specs=[vmem] * 2,
        compiler_params=limits(8),
        name="pack_features",
    )(after(inputs, own_a))
    leaving = pl.pallas_call(
        pack_weights,
        out_shape=shaped((2 * PART, kv_columns)),
        in_specs=[hbm],
        out_specs=vmem,
        scratch_shapes=[DMA],
        compiler_params=limits(56),
        name="pack_weights",
    )(after(w_key, own_b))
    w_near = swap_tensor(leaving)
    near_pairs = jnp.concatenate([own_a, own_b, far_a, far_b], axis=0)
    core_pairs = swap(after(near_pairs, near_features, leaving, rows[1], rows[2]), CORE)
    far_features = swap(far_features, Z_HI)

    row_grad = shaped((ROWS, GROUP * HD))
    padded_rows = total_rows + HD
    sorted_rows = shaped((padded_rows, HD))
    sums = shaped((padded_rows, HD), jnp.float32)
    half_sums = shaped((half, 2 * HD), jnp.float32)

    def attend_scratch(blocks):
        stacked = VMEM((blocks, GROUP * BLK, HD), jnp.bfloat16)
        tiles = VMEM((2, total_rows // TILE, TILE, GROUP * BLK), jnp.float32)
        return [
            stacked,
            stacked,
            VMEM((blocks, BLK, GROUP * HD), jnp.bfloat16),
            tiles,
            tiles,
            SMEM((4 * GROUP, HD), jnp.int32),
            DMA,
        ]

    *row_grads, keys, keys_t, all_values, dk_first, dv_first, marks = pl.pallas_call(
        attend_first,
        out_shape=[row_grad] * (GROUP - 1)
        + [sorted_rows, shaped((HD, padded_rows)), sorted_rows, sums, sums]
        + [shaped((4 * GROUP, HD), jnp.int32)],
        in_specs=[smem] + [vmem] * (GROUP + 4),
        out_specs=[vmem] * (GROUP + 5),
        scratch_shapes=attend_scratch(Q_BLOCKS - 2),
        compiler_params=limits(24),
        cost_estimate=pl.CostEstimate(flops=ATTEND_COST, bytes_accessed=0, transcendentals=0),
        name="attend_first",
    )(doc_lens, *rows[:-1], own_a, own_b, far_a, far_b, core_pairs)
    last_grad, kept, sent = pl.pallas_call(
        attend_last,
        out_shape=[row_grad, half_sums, half_sums],
        in_specs=[smem] + [vmem] * 7,
        out_specs=[vmem] * 3,
        scratch_shapes=[VMEM((padded_rows, HD), jnp.float32)] * 2 + attend_scratch(2),
        compiler_params=limits(24),
        cost_estimate=pl.CostEstimate(flops=ATTEND_COST, bytes_accessed=0, transcendentals=0),
        name="attend_last",
    )(doc_lens, after(rows[-1], w_near), keys, keys_t, all_values, dk_first, dv_first, marks)

    row_grads = with_partners(row_grads)
    sent = after(sent, far_features, *row_grads)
    grads = kept + swap(sent, CORE)
    dk_sum, dv_sum = grads[:, :HD], grads[:, HD:]
    dk_far = swap(dk_sum.astype(jnp.bfloat16), Z_HI)
    w_far = swap(after(w_near, dk_sum), CORE)

    feature_parts = pl.pallas_call(
        join_features,
        out_shape=[shaped((2, ROWS, 256))] * GROUP,
        in_specs=[vmem] * 2,
        out_specs=[vmem] * GROUP,
        compiler_params=limits(16),
        name="join_features",
    )(after(near_features, sent), far_features)
    own_features = pl.pallas_call(
        turn_features,
        out_shape=shaped((256, half)),
        in_specs=[vmem] * GROUP,
        out_specs=vmem,
        compiler_params=limits(16),
        cost_estimate=pl.CostEstimate(flops=8_000_000_000, bytes_accessed=0, transcendentals=0),
        name="turn_features",
    )(*with_partners(feature_parts))
    other_features = swap_tensor(own_features)

    dk_far = jnp.concatenate([dk_far[quarter:], dk_far[:quarter]], axis=0)
    key_grad = (dk_sum + dk_far.astype(jnp.float32)).astype(jnp.bfloat16)
    last_grad = swap(after(last_grad, dk_sum), 6)
    key_grad = after(key_grad, own_features, w_far, last_grad)
    key_grads = with_partners([key_grad] * GROUP)
    own_key_grad = jnp.stack([key_grads[m][m * ROWS : (m + 1) * ROWS] for m in range(GROUP)])
    other_key_grad = swap_tensor(own_key_grad)

    dv_far = swap(after(dv_sum[quarter:].astype(jnp.bfloat16), key_grad), Z_HI)
    value_grad = (dv_sum[:quarter] + dv_far.astype(jnp.float32)).astype(jnp.bfloat16)
    packed_grads = pl.pallas_call(
        pack_grads,
        out_shape=[shaped((ROWS, HD))] * GROUP,
        in_specs=[vmem],
        out_specs=[vmem] * GROUP,
        compiler_params=limits(16),
        name="pack_grads",
    )(value_grad)
    packed_grads = [after(packed_grads[0], own_key_grad)] + [
        after(grad, own_key_grad) for grad in packed_grads[1:]
    ]

    keep, send = pl.pallas_call(
        weight_grad,
        out_shape=[shaped((256, kv_columns), jnp.float32)] * 2,
        in_specs=[vmem] * (2 + GROUP),
        out_specs=[vmem] * 2,
        scratch_shapes=[VMEM((half, kv_columns), jnp.bfloat16)],
        compiler_params=limits(24),
        cost_estimate=pl.CostEstimate(
            flops=4 * 256 * half * kv_columns, bytes_accessed=4 << 20, transcendentals=0
        ),
        name="weight_grad",
    )(own_features, other_features, *key_grads)
    arrived = swap(send, CORE)

    d_input = pl.pallas_call(
        input_grad,
        out_shape=shaped((ROWS, features // 2)),
        in_specs=[vmem] * 5,
        out_specs=vmem,
        scratch_shapes=[VMEM((ROWS, kv_columns), jnp.bfloat16)] * 2,
        compiler_params=limits(16),
        cost_estimate=pl.CostEstimate(
            flops=8_000_000_000, bytes_accessed=5 << 20, transcendentals=0
        ),
        name="input_grad",
    )(after(own_key_grad, send), other_key_grad, w_key, w_near, w_far)

    d_wkey, d_query, d_value = pl.pallas_call(
        finish,
        out_shape=[
            shaped((256, kv_columns), jnp.float32),
            shaped(queries.shape),
            shaped(values.shape),
        ],
        in_specs=[vmem] * (2 + 2 * GROUP),
        out_specs=[vmem] * 3,
        compiler_params=limits(16),
        name="finish",
    )(keep, arrived, *row_grads, last_grad, *with_partners(packed_grads))
    return (d_query, d_value, d_input, d_wkey)


def solution(mesh):
    by_heads = mesh.shape["dp"] == 16 and mesh.shape["tensor"] == 2
    return jax.shard_map(
        on_device_by_heads if by_heads else on_device,
        mesh=mesh,
        in_specs=(
            P("dp", None),
            P(None, "tensor"),
            P("dp", "tensor"),
            P("dp", "tensor"),
            P("dp", "tensor"),
            P(),
            P("dp"),
        ),
        out_specs=(P("dp", "tensor"), P("dp", "tensor"), P("dp", "tensor"), P("dp", "tensor")),
        check_vma=False,
    )
```
